32 devices in a mesh: dp: 16 (over z, y, core), mp: 2 (over x).
Axes of the slice: x: 2, y: 2, z: 4, core: 2. Of those that a mesh axis runs over, the one named last changes fastest.
Arguments:
- tokens: bfloat16 [16384, 768], P('dp'), may hold values from -6 to 6
- cotangent: bfloat16 [16384, 768], P('dp'), may hold values from -6 to 6
- lengths: int32 [16], P('dp'), may hold values from 512 to 1024, as said below
- masked: int32 [16, 64], P('dp'), may hold values from 0 to 1023
- qk_weight: bfloat16 [768, 2, 768], P(None, None, 'mp'), may hold values from -0.625 to 0.625
- qk_bias: float32 [2, 768], P(None, 'mp'), may hold values from -3 to 3
- value_weight: bfloat16 [768, 768], P(None, 'mp'), may hold values from -0.21875 to 0.21875
- value_bias: float32 [768], P('mp'), may hold values from -3 to 3
- conv_taps: float32 [12, 33], P('mp'), may hold values from -0.3125 to 0.3125
- out_weight: bfloat16 [768, 768], P('mp'), may hold values from -0.4375 to 0.4375
- out_bias: float32 [768], replicated, may hold values from -3 to 3
- first_gain: float32 [768], replicated, may hold values from 0.5 to 1.5
- first_shift: float32 [768], replicated, may hold values from -1.75 to 1.75
- up_weight: bfloat16 [768, 3072], P(None, 'mp'), may hold values from -0.21875 to 0.21875
- up_bias: float32 [3072], P('mp'), may hold values from -3 to 3
- down_weight: bfloat16 [3072, 768], P('mp'), may hold values from -0.109375 to 0.109375
- down_bias: float32 [768], replicated, may hold values from -3 to 3
- second_gain: float32 [768], replicated, may hold values from 0.5 to 1.5
- second_shift: float32 [768], replicated, may hold values from -1.75 to 1.75
Outputs:
- output: bfloat16 [16384, 768], P('dp')
- tokens_grad: bfloat16 [16384, 768], P('dp')
- qk_weight_grad: float32 [768, 2, 768], P('dp', None, 'mp')
- qk_bias_grad: float32 [2, 768], P(None, 'mp')
- value_weight_grad: float32 [768, 768], P('dp', 'mp')
- value_bias_grad: float32 [768], P('mp')
- conv_taps_grad: float32 [12, 33], P('mp')
- out_weight_grad: float32 [768, 768], P('mp', 'dp')
- out_bias_grad: float32 [768], replicated
- first_gain_grad: float32 [768], replicated
- first_shift_grad: float32 [768], replicated
- up_weight_grad: float32 [768, 3072], P('dp', 'mp')
- up_bias_grad: float32 [3072], P('mp')
- down_weight_grad: float32 [3072, 768], P('mp', 'dp')
- down_bias_grad: float32 [768], replicated
- second_gain_grad: float32 [768], replicated
- second_shift_grad: float32 [768], replicated
The draws below stay inside these ranges and needn't reach their ends.
Inputs may be any that keep to these rules, and one draw needn't show every extreme that they name: `lengths`: positions of an item from its length on are padding. Listed positions are masked out of their item; a position may be listed twice or lie in the padding.
All inputs are finite; a program needn't handle non-finite values.
Results may differ from the reference program's by a relative error of at most 0.018.
Values may be sent and summed in bfloat16 or wider, within the bound.
A program may use at most 256 MiB of HBM per device.

```python
import math
import jax
import jax.numpy as jnp
from jax import lax

D = 768
HEADS = 12
HEAD_DIM = 64
FF = 3072
LANDMARKS = 64
NS_ITERS = 6
KERNEL = 33
SEQ = 1024
NMASK = 64
ITEMS = 16
TOKENS = 16384


def draw_lengths(key, part):
    key_first, key_second = jax.random.split(jax.random.fold_in(key, 11))
    drawn = jax.random.randint(key_first, (ITEMS,), SEQ // 2, SEQ + 1)
    chosen_place = jax.random.randint(key_second, (), 0, ITEMS)
    drawn = drawn.at[chosen_place].set(SEQ)
    drawn = drawn.at[(chosen_place + 1) % ITEMS].set(SEQ // 2)
    return drawn.astype(jnp.int32)


def touch_ends(values, key, smallest, largest):
    extent = values.shape
    spot = [jax.random.randint(jax.random.fold_in(key, axis), (), 0, extent[axis]) for axis in range(len(extent))]
    values = values.at[tuple(spot)].set(smallest)
    longest = extent.index(max(extent))
    spot[longest] = (spot[longest] + 1) % extent[longest]
    return values.at[tuple(spot)].set(largest)


def spiked(values, key, source, target, parts, factor):
    owner, partner = [(jnp.arange(values.shape[dim]) // (values.shape[dim] // parts)).reshape([-1 if axis == dim else 1 for axis in range(values.ndim)]) for dim in (source, target)]
    chosen = jax.random.permutation(key, parts)[partner]
    strong = (owner == chosen) | (owner == (partner + parts // 2) % parts)
    return jnp.where(strong, factor * values, values)


def shard_levels(stream_key, dims, pieces, low, top_value):
    level, own = 1.0, jax.random.fold_in(stream_key, 6)
    for axis_at, parts in pieces:
        heights = jnp.exp(jax.random.uniform(jax.random.fold_in(own, axis_at), (parts,), jnp.float32, low / len(pieces), top_value / len(pieces)))
        level = level * jnp.repeat(heights, dims[axis_at] // parts).reshape([-1 if axis == axis_at else 1 for axis in range(len(dims))])
    return level


def normal_values(rng, extent, scale, limit, cuts=(), kind=jnp.bfloat16):
    array = jax.random.normal(rng, extent, jnp.float32) * scale
    if len(cuts) > 0:
        array = shard_levels(rng, extent, cuts, -0.22, 0.18) * array
    return jnp.clip(array, min=-limit, max=limit).astype(kind)


def heavy_noise(key, shape, scale, reach, cuts, heavy, kind=jnp.bfloat16):
    values = scale * jax.random.normal(key, shape, jnp.float32)
    if cuts:
        values = values * shard_levels(key, shape, cuts, -0.22, 0.18)
    return jnp.clip(spiked(values, jax.random.fold_in(key, 3), *heavy), -reach, reach).astype(kind)


def setup_inputs(seed: int = 0) -> dict:
    splits = jax.random.split(jax.random.key(seed), 20)
    return {
        "tokens": heavy_noise(splits[0], (TOKENS, D), 1.0, 6.0, ((0, 16),), (0, 1, 16, 2.0)),
        "cotangent": heavy_noise(splits[1], (TOKENS, D), 1.0, 6.0, ((0, 16),), (0, 1, 16, 2.0)),
        "lengths": draw_lengths(jax.random.fold_in(splits[19], 71), 0),
        "masked": touch_ends(jax.random.randint(splits[3], (ITEMS, NMASK), 0, SEQ), jax.random.fold_in(splits[3], 1), 0, SEQ - 1).astype(jnp.int32),
        "qk_weight": normal_values(splits[4], (D, 2, D), (D // 8) ** -0.5, 0.625, ((2, 2),)),
        "qk_bias": normal_values(splits[5], (2, D), 0.5, 3.0, ((1, 2),), jnp.float32),
        "value_weight": normal_values(splits[6], (D, D), D ** -0.5, 0.21875, ((1, 2),)),
        "value_bias": normal_values(splits[7], (D,), 0.5, 3.0, ((0, 2),), jnp.float32),
        "conv_taps": normal_values(splits[8], (HEADS, KERNEL), 0.05, 0.3125, ((0, 2),), jnp.float32),
        "out_weight": normal_values(splits[9], (D, D), (D // 4) ** -0.5, 0.4375, ((0, 2),)),
        "out_bias": normal_values(splits[10], (D,), 0.5, 3.0, (), jnp.float32),
        "first_gain": jnp.clip(1.0 + 0.1 * jax.random.normal(splits[11], (D,), jnp.float32), 0.5, 1.5),
        "first_shift": normal_values(splits[12], (D,), 0.3, 1.75, (), jnp.float32),
        "up_weight": normal_values(splits[13], (D, FF), D ** -0.5, 0.21875, ((1, 2),)),
        "up_bias": normal_values(splits[14], (FF,), 0.5, 3.0, ((0, 2),), jnp.float32),
        "down_weight": normal_values(splits[15], (FF, D), FF ** -0.5, 0.109375, ((0, 2),)),
        "down_bias": normal_values(splits[16], (D,), 0.5, 3.0, (), jnp.float32),
        "second_gain": jnp.clip(1.0 + 0.1 * jax.random.normal(splits[17], (D,), jnp.float32), 0.5, 1.5),
        "second_shift": normal_values(splits[18], (D,), 0.3, 1.75, (), jnp.float32),
    }


highest_precision = lax.Precision.HIGHEST

@jax.custom_vjp
def low(v):
    return lax.optimization_barrier(v.astype(jnp.bfloat16)).astype(jnp.float32)

@jax.custom_vjp
def low_back(v):
    return v

def low_keep(v):
    return (low(v), None)

def low_pass(kept, grad):
    return (grad,)

def back_keep(v):
    return (v, None)

def back_low(kept, grad):
    return (low(grad),)
low.defvjp(low_keep, low_pass)
low_back.defvjp(back_keep, back_low)

def layer_norm(value, gain, shift):
    middle = lax.optimization_barrier(jnp.mean(value, axis=-1, keepdims=True))
    centered = value - middle
    spread = lax.optimization_barrier(jnp.mean(centered * centered, axis=-1, keepdims=True))
    return centered * lax.rsqrt(spread + 1e-05) * gain + shift

def item_mask(length_value, masked_row):
    places = jnp.arange(SEQ, dtype=jnp.int32)
    listed = jnp.any(places[:, None] == masked_row[None, :], axis=1)
    kept_place = (places < length_value) & jnp.logical_not(listed)
    return jnp.where(kept_place, 1.0, 0.0).astype(jnp.float32)

def softmax_along_last(scores, along):
    highest_score = lax.optimization_barrier(jnp.max(scores, axis=along, keepdims=True))
    weights = jnp.exp(scores - highest_score)
    return weights / lax.optimization_barrier(jnp.sum(weights, axis=along, keepdims=True))

def pseudo_inverse(matrix):
    identity = jnp.eye(matrix.shape[-1], dtype=matrix.dtype)
    square_sum = lax.optimization_barrier(jnp.sum(matrix * matrix, axis=(1, 2), keepdims=True))
    approx = jnp.swapaxes(matrix, 1, 2) / square_sum
    for iteration in range(NS_ITERS):
        product = jnp.einsum('hij,hjk->hik', matrix, approx, precision=highest_precision)
        inner_term = 7.0 * identity - product
        inner_term = 15.0 * identity - jnp.einsum('hij,hjk->hik', product, inner_term, precision=highest_precision)
        inner_term = 13.0 * identity - jnp.einsum('hij,hjk->hik', product, inner_term, precision=highest_precision)
        approx = 0.25 * jnp.einsum('hij,hjk->hik', approx, inner_term, precision=highest_precision)
    return approx

def nystrom(queries, key_rows, values, live_token_mask, conv_taps):
    length = queries.shape[0]
    head_count = conv_taps.shape[0]
    segment = length // LANDMARKS
    factor = HEAD_DIM ** (-0.25)
    live_rows = live_token_mask[:, None]
    query_head_rows = (queries * live_rows * factor).reshape(length, head_count, HEAD_DIM)
    key_head_rows = (key_rows * live_rows * factor).reshape(length, head_count, HEAD_DIM)
    value_head_rows = (values * live_rows).reshape(length, head_count, HEAD_DIM)
    counts = jnp.maximum(lax.optimization_barrier(jnp.sum(live_token_mask.reshape(LANDMARKS, segment), axis=1)), 1.0)
    query_landmark_rows = lax.optimization_barrier(jnp.sum(query_head_rows.reshape(LANDMARKS, segment, head_count, HEAD_DIM), axis=1)) / counts[:, None, None]
    key_landmark_rows = lax.optimization_barrier(jnp.sum(key_head_rows.reshape(LANDMARKS, segment, head_count, HEAD_DIM), axis=1)) / counts[:, None, None]
    first_attention_matrix = softmax_along_last(jnp.einsum('gsy,bsy->sgb', key_landmark_rows, query_head_rows, precision=highest_precision), 1)
    second_attention_matrix = softmax_along_last(jnp.einsum('fgb,ugb->gfu', query_landmark_rows, key_landmark_rows, precision=highest_precision), 2)
    third_attention_matrix = softmax_along_last(jnp.einsum('gsy,bsy->sgb', query_landmark_rows, key_head_rows, precision=highest_precision) - 10000.0 * (1.0 - live_token_mask), 2)
    kernel_inverse = pseudo_inverse(second_attention_matrix)
    carried_over = jnp.einsum('ekf,fet->ekt', third_attention_matrix, value_head_rows, precision=highest_precision)
    carried_over = jnp.einsum('toc,tcj->toj', kernel_inverse, carried_over, precision=highest_precision)
    mixed_values = jnp.einsum('fqr,fqt->rft', first_attention_matrix, carried_over, precision=highest_precision)
    margin = KERNEL // 2
    padded = jnp.pad(value_head_rows, ((margin, margin), (0, 0), (0, 0)))
    for offset in range(KERNEL):
        mixed_values = mixed_values + conv_taps[:, offset][None, :, None] * padded[offset:offset + length]
    return mixed_values.reshape(length, head_count * HEAD_DIM)

def block_forward(params, block_tokens, block_lengths, block_masked):
    qk_weight, qk_bias, value_weight, value_bias, conv_taps, out_weight, out_bias, first_gain, first_shift, up_weight, up_bias, down_weight, down_bias, second_gain, second_shift = params
    row_count = block_tokens.shape[0]
    model_width = block_tokens.shape[1]
    item_count = row_count // SEQ
    live_token_mask = jax.vmap(item_mask)(block_lengths, block_masked)
    joined = low_back(jnp.dot(block_tokens, qk_weight.reshape(model_width, 2 * model_width), precision=highest_precision)) + qk_bias.reshape(2 * model_width)
    values = low_back(jnp.dot(block_tokens, value_weight, precision=highest_precision)) + value_bias
    queries = joined[:, :model_width].reshape(item_count, SEQ, model_width)
    key_rows = joined[:, model_width:].reshape(item_count, SEQ, model_width)
    attended = jax.vmap(nystrom, in_axes=(0, 0, 0, 0, None))(queries, key_rows, values.reshape(item_count, SEQ, model_width), live_token_mask, conv_taps)
    attended = low(attended.reshape(row_count, model_width))
    summed = low_back(jnp.dot(attended, out_weight, precision=highest_precision)) + out_bias + block_tokens
    hidden = layer_norm(summed, first_gain, first_shift)
    hidden_low = low(hidden)
    raised = low_back(jnp.dot(hidden_low, up_weight, precision=highest_precision)) + up_bias
    active = low(jax.nn.gelu(raised, approximate=False))
    result = low_back(jnp.dot(active, down_weight, precision=highest_precision)) + down_bias + hidden
    return layer_norm(result, second_gain, second_shift)

def reference(tokens, cotangent, lengths, masked, qk_weight, qk_bias, value_weight, value_bias, conv_taps, out_weight, out_bias, first_gain, first_shift, up_weight, up_bias, down_weight, down_bias, second_gain, second_shift):
    params = (qk_weight.astype(jnp.float32), qk_bias.astype(jnp.float32), value_weight.astype(jnp.float32), value_bias.astype(jnp.float32), conv_taps.astype(jnp.float32), out_weight.astype(jnp.float32), out_bias.astype(jnp.float32), first_gain.astype(jnp.float32), first_shift.astype(jnp.float32), up_weight.astype(jnp.float32), up_bias.astype(jnp.float32), down_weight.astype(jnp.float32), down_bias.astype(jnp.float32), second_gain.astype(jnp.float32), second_shift.astype(jnp.float32))
    block_items = math.gcd(ITEMS, max(1, 4096 // SEQ))
    block_count = ITEMS // block_items
    block_rows = block_items * SEQ
    split_lengths = lengths.reshape(block_count, block_items)
    split_masked = masked.reshape(block_count, block_items, NMASK)

    def forward(whole, weights):

        def run(piece):
            return block_forward(weights, piece[0], piece[1], piece[2])
        outputs = lax.map(jax.checkpoint(run), (whole.reshape(block_count, block_rows, D), split_lengths, split_masked))
        return outputs.reshape(TOKENS, D)
    output, pull = jax.vjp(forward, tokens.astype(jnp.float32), params)
    tokens_grad, grads = pull(cotangent.astype(jnp.float32))
    qk_weight_grad, qk_bias_grad, value_weight_grad, value_bias_grad, conv_taps_grad, out_weight_grad, out_bias_grad, first_gain_grad, first_shift_grad, up_weight_grad, up_bias_grad, down_weight_grad, down_bias_grad, second_gain_grad, second_shift_grad = grads
    return (output.astype(jnp.bfloat16), tokens_grad.astype(jnp.bfloat16), qk_weight_grad, qk_bias_grad, value_weight_grad, value_bias_grad, conv_taps_grad, out_weight_grad, out_bias_grad, first_gain_grad, first_shift_grad, up_weight_grad, up_bias_grad, down_weight_grad, down_bias_grad, second_gain_grad, second_shift_grad)
```

```python
import functools

import jax
import jax.numpy as jnp
from jax import lax
from jax.experimental import pallas as pl
from jax.experimental.pallas import tpu as pltpu
from jax.sharding import Mesh
from jax.sharding import PartitionSpec as P

HEAD_DIM = 64
LANDMARKS = 64
NS_ITERS = 6
KERNEL = 33
EDGE = 112
BAND = 160
PAIR = 2 * HEAD_DIM
CHUNKS = 4

f32 = jnp.float32
bf16 = jnp.bfloat16
NN = (((1,), (0,)), ((), ()))
NT = (((1,), (1,)), ((), ()))
TN = (((0,), (0,)), ((), ()))
MESH = pl.DeviceIdType.MESH
VMEM = pl.BlockSpec(memory_space=pltpu.VMEM)
SMEM = pl.BlockSpec(memory_space=pltpu.SMEM)


def dot(a, b, dims=NN):
    return lax.dot_general(a, b, dims, preferred_element_type=f32)


def split(value):
    high = value.astype(bf16)
    return high, (value - high.astype(f32)).astype(bf16)


def dot3(a, b, dims=NN):
    return dot(a[0], b[0], dims) + (dot(a[0], b[1], dims) + dot(a[1], b[0], dims))


def iota(shape, axis):
    return lax.broadcasted_iota(jnp.int32, shape, axis)


def same_head():
    return iota((PAIR, PAIR), 0) // HEAD_DIM == iota((PAIR, PAIR), 1) // HEAD_DIM


def identity():
    return jnp.where(iota((PAIR, PAIR), 0) == iota((PAIR, PAIR), 1), 1.0, 0.0).astype(f32)


def segments(length):
    spread = length // LANDMARKS
    hit = iota((length, PAIR), 0) // spread == iota((length, PAIR), 1) % LANDMARKS
    return jnp.where(hit, 1.0, 0.0).astype(bf16)


def segments_turned(length):
    spread = length // LANDMARKS
    hit = iota((PAIR, length), 1) // spread == iota((PAIR, length), 0) % LANDMARKS
    return jnp.where(hit, 1.0, 0.0).astype(bf16)


def segment_counts(live, seg):
    rows = jnp.broadcast_to(live, (8, live.shape[1])).astype(bf16)
    return jnp.maximum(dot(rows, seg)[0:1], 1.0)


def head_sum(value):
    heads = value.shape[0] // HEAD_DIM
    cut = value.reshape(heads, HEAD_DIM, value.shape[1])
    total = jnp.sum(cut, axis=1, keepdims=True)
    return jnp.broadcast_to(total, cut.shape).reshape(value.shape)


def head_max(value):
    heads = value.shape[0] // HEAD_DIM
    cut = value.reshape(heads, HEAD_DIM, value.shape[1])
    top = jnp.max(cut, axis=1, keepdims=True)
    return jnp.broadcast_to(top, cut.shape).reshape(value.shape)


def softmax_lanes(scores):
    weights = jnp.exp(scores - jnp.max(scores, axis=1, keepdims=True))
    return weights / jnp.sum(weights, axis=1, keepdims=True)


def band_matrix(taps_ref, head, turned):
    gap = iota((BAND, 128), 0) - iota((BAND, 128), 1)
    total = jnp.zeros((BAND, 128), f32)
    for tap in range(KERNEL):
        source = KERNEL - 1 - tap if turned else tap
        total = jnp.where(gap == tap, taps_ref[head, source], total)
    zeros = jnp.zeros((EDGE, 128), f32)
    return jnp.concatenate([zeros, total, zeros], axis=0)


def windows(rows):
    zeros = jnp.zeros((rows.shape[0], 128), rows.dtype)
    padded = jnp.concatenate([zeros, rows, zeros], axis=1)
    blocks = rows.shape[1] // 128
    return jnp.concatenate([padded[:, b * 128 : b * 128 + 384] for b in range(blocks)], axis=0)


def blocks_down(rows):
    blocks = rows.shape[1] // 128
    return jnp.concatenate([rows[:, b * 128 : (b + 1) * 128] for b in range(blocks)], axis=0)


def blocks_back(stacked, height):
    blocks = stacked.shape[0] // height
    return jnp.concatenate([stacked[b * height : (b + 1) * height] for b in range(blocks)], axis=1)


def attend_kernel(
    x_ref,
    wt_ref,
    bias_ref,
    taps_ref,
    live_ref,
    qkv_ref,
    first_ref,
    third_ref,
    attended_ref,
    marks_ref,
    chain_ref,
    q_ref,
    k_ref,
    v_ref,
):
    width = q_ref.shape[0]
    length = x_ref.shape[0]
    pairs = width // PAIR
    live = live_ref[...]
    factor = live * HEAD_DIM ** (-0.25)
    for at, (kept, scale) in enumerate(((q_ref, factor), (k_ref, factor), (v_ref, live))):
        rows = slice(at * width, (at + 1) * width)
        value = (dot(wt_ref[rows, :], x_ref[...], NT) + bias_ref[rows, :]) * scale
        kept[...] = value
        qkv_ref[rows, :] = value.astype(bf16)
    seg = segments(length)
    counts = segment_counts(live, seg)
    diagonal = same_head()
    eye = identity()
    state = []
    for pair in range(pairs):
        rows = slice(pair * PAIR, (pair + 1) * PAIR)
        q = split(q_ref[rows, :])
        k = split(k_ref[rows, :])
        qm_turned = jnp.where(diagonal, (dot(q[0], seg) + dot(q[1], seg)) / counts, 0.0)
        km_turned = jnp.where(diagonal, (dot(k[0], seg) + dot(k[1], seg)) / counts, 0.0)
        qm = qm_turned.T
        km = km_turned.T
        qm_parts = split(qm)
        scores = dot3(split(km), q)
        weights = jnp.exp(scores - head_max(scores))
        first_ref[rows, :] = (weights / head_sum(weights)).astype(bf16)
        third = softmax_lanes(dot3(qm_parts, k) - 10000.0 * (1.0 - live))
        third_ref[rows, :] = third.astype(bf16)
        scores = dot3(qm_parts, split(km_turned))
        second = softmax_lanes(jnp.where(diagonal, scores, -1e30))
        carried = jnp.where(diagonal, dot3(split(third), split(v_ref[rows, :]), NT), 0.0)
        marks_ref[0, pair] = qm
        marks_ref[1, pair] = km
        marks_ref[2, pair] = second
        marks_ref[3, pair] = carried
        square_sum = head_sum(jnp.sum(second * second, axis=1, keepdims=True))
        state.append((split(second), second.T / square_sum))
    for step in range(NS_ITERS):
        following = []
        for pair in range(pairs):
            matrix, approx = state[pair]
            chain_ref[step, 0, pair] = approx
            approx_parts = split(approx)
            product = dot3(matrix, approx_parts)
            chain_ref[step, 1, pair] = product
            parts = split(product)
            inner = 15.0 * eye - dot3(parts, split(7.0 * eye - product))
            chain_ref[step, 2, pair] = inner
            inner = 13.0 * eye - dot3(parts, split(inner))
            chain_ref[step, 3, pair] = inner
            following.append((matrix, 0.25 * dot3(approx_parts, split(inner))))
        state = following
    for pair in range(pairs):
        rows = slice(pair * PAIR, (pair + 1) * PAIR)
        inverse = state[pair][1]
        mixed = dot3(split(inverse), split(marks_ref[3, pair]))
        marks_ref[4, pair] = inverse
        marks_ref[5, pair] = mixed
        out = dot(mixed.T.astype(bf16), first_ref[rows, :])
        v = split(v_ref[rows, :])
        smoothed = []
        for half in range(2):
            head_rows = slice(half * HEAD_DIM, (half + 1) * HEAD_DIM)
            band = split(band_matrix(taps_ref, 2 * pair + half, False))
            high = windows(v[0][head_rows])
            smooth = dot(high, band[0]) + (dot(high, band[1]) + dot(windows(v[1][head_rows]), band[0]))
            smoothed.append(blocks_back(smooth, HEAD_DIM))
        out = out + jnp.concatenate(smoothed, axis=0)
        attended_ref[:, rows] = out.astype(bf16).T


def attend_back_kernel(
    d_ref,
    x_ref,
    wt_ref,
    taps_ref,
    live_ref,
    qkv_ref,
    first_ref,
    third_ref,
    marks_ref,
    chain_ref,
    grad_ref,
    part_ref,
    bias_ref,
    taps_grad_ref,
    joined_ref,
):
    width = d_ref.shape[0]
    length = d_ref.shape[1]
    pairs = width // PAIR
    live = live_ref[...]
    factor = live * HEAD_DIM ** (-0.25)
    diagonal = same_head()
    flip = jnp.where(iota((128, 128), 0) + iota((128, 128), 1) == 127, 1.0, 0.0).astype(bf16)
    seg_turned = segments_turned(length)
    counts = segment_counts(live, segments(length))
    state = []
    for pair in range(pairs):
        rows = slice(pair * PAIR, (pair + 1) * PAIR)
        d_out = d_ref[rows, :]
        d_mixed = split(jnp.where(diagonal, dot(first_ref[rows, :], d_out, NT), 0.0))
        d_inverse = dot3(d_mixed, split(marks_ref[3, pair]), NT)
        d_carried = dot3(split(marks_ref[4, pair]), d_mixed, TN)
        state.append((d_inverse, jnp.zeros((PAIR, PAIR), f32), d_carried))
    for step in reversed(range(NS_ITERS)):
        following = []
        for pair in range(pairs):
            d_approx, d_matrix, d_carried = state[pair]
            approx = split(chain_ref[step, 0, pair])
            product = chain_ref[step, 1, pair]
            inner = split(7.0 * identity() - product)
            product = split(product)
            middle = split(chain_ref[step, 2, pair])
            outer = split(chain_ref[step, 3, pair])
            d_parts = split(0.25 * d_approx)
            d_outer = split(dot3(approx, d_parts, TN))
            d_next = dot3(d_parts, outer, NT)
            d_product = -dot3(d_outer, middle, NT)
            d_middle = split(-dot3(product, d_outer, TN))
            d_product = d_product - dot3(d_middle, inner, NT) + dot3(product, d_middle, TN)
            d_product = split(d_product)
            d_matrix = d_matrix + dot3(d_product, approx, NT)
            d_next = d_next + dot3(split(marks_ref[2, pair]), d_product, TN)
            following.append((d_next, d_matrix, d_carried))
        state = following
    for pair in range(pairs):
        rows = slice(pair * PAIR, (pair + 1) * PAIR)
        k_rows = slice(width + pair * PAIR, width + (pair + 1) * PAIR)
        v_rows = slice(2 * width + pair * PAIR, 2 * width + (pair + 1) * PAIR)
        d_approx, d_matrix, d_carried = state[pair]
        qm = marks_ref[0, pair]
        km = marks_ref[1, pair]
        second = marks_ref[2, pair]
        square_sum = head_sum(jnp.sum(second * second, axis=1, keepdims=True))
        turned = d_approx.T
        along = head_sum(jnp.sum(turned * second, axis=1, keepdims=True))
        d_matrix = d_matrix + turned / square_sum - second * (2.0 * along / (square_sum * square_sum))
        d_scores = second * (d_matrix - jnp.sum(d_matrix * second, axis=1, keepdims=True))
        d_scores = split(d_scores)
        d_out = d_ref[rows, :]
        first = first_ref[rows, :].astype(f32)
        d_first = dot(marks_ref[5, pair].astype(bf16), d_out)
        d_first = (first * (d_first - head_sum(d_first * first))).astype(bf16)
        third = third_ref[rows, :]
        d_third = dot(d_carried.astype(bf16), qkv_ref[v_rows, :])
        third_wide = third.astype(f32)
        d_third = third_wide * (d_third - jnp.sum(d_third * third_wide, axis=1, keepdims=True))
        d_third = d_third.astype(bf16)
        d_qm = dot3(d_scores, split(km)) + jnp.where(diagonal, dot(d_third, qkv_ref[k_rows, :], NT), 0.0)
        d_km = dot3(d_scores, split(qm), TN) + jnp.where(diagonal, dot(d_first, qkv_ref[rows, :], NT), 0.0)
        d_qm = split(d_qm.T / counts)
        d_km = split(d_km.T / counts)
        d_q = dot(km.T.astype(bf16), d_first) + (dot(d_qm[0], seg_turned) + dot(d_qm[1], seg_turned))
        d_k = dot(qm.T.astype(bf16), d_third) + (dot(d_km[0], seg_turned) + dot(d_km[1], seg_turned))
        d_v = dot(d_carried.T.astype(bf16), third)
        smoothed = []
        for half in range(2):
            head = 2 * pair + half
            head_rows = slice(half * HEAD_DIM, (half + 1) * HEAD_DIM)
            band = split(band_matrix(taps_ref, head, True))
            around = windows(d_out[head_rows])
            smoothed.append(blocks_back(dot(around, band[0]) + dot(around, band[1]), HEAD_DIM))
            start = 2 * width + head * HEAD_DIM
            flipped = dot(blocks_down(d_out[head_rows]), flip).astype(bf16)
            products = dot(flipped, windows(qkv_ref[start : start + HEAD_DIM, :]), TN)
            lined = pltpu.roll(products, 0, 1, stride=1, stride_axis=0)
            total = jnp.sum(lined, axis=0, keepdims=True)
            taps_grad_ref[head : head + 1, :] = total[:, 128:]
        d_v = d_v + jnp.concatenate(smoothed, axis=0)
        for place, value, scale in ((rows, d_q, factor), (k_rows, d_k, factor), (v_rows, d_v, live)):
            value = value * scale
            joined_ref[place, :] = value.astype(bf16)
            bias_ref[place, :] = jnp.sum(value, axis=1, keepdims=True)
    part_ref[...] = dot(joined_ref[...], wt_ref[...], TN).astype(bf16)
    grad_ref[...] = dot(x_ref[...].T, joined_ref[...], NT).astype(bf16)


def normalize(value):
    middle = jnp.mean(value, axis=1, keepdims=True)
    centered = value - middle
    spread = jnp.mean(centered * centered, axis=1, keepdims=True)
    scale = lax.rsqrt(spread + 1e-05)
    return centered * scale, scale


def normalize_back(grad, normal, scale):
    middle = jnp.mean(grad, axis=1, keepdims=True)
    along = jnp.mean(grad * normal, axis=1, keepdims=True)
    return scale * (grad - middle - normal * along)


def feed_kernel(
    attended_ref,
    x_ref,
    cotangent_ref,
    wo_ref,
    vector_ref,
    wu_ref,
    bu_ref,
    wd_ref,
    output_ref,
    d_attended_ref,
    d_summed_ref,
    sums_ref,
    up_sums_ref,
    out_grad_ref,
    up_grad_ref,
    down_grad_ref,
    mine,
    theirs,
    normal_ref,
    scale_ref,
    low_ref,
    active_ref,
    slope_ref,
    d_result_ref,
    d_low_ref,
    send_sem,
    recv_sem,
):
    length, width = x_ref.shape
    hidden_units = wu_ref.shape[1]
    block = 256
    rows_at = length // CHUNKS
    sister = {"core": 1 - lax.axis_index("core")}
    barrier = pltpu.get_barrier_semaphore()
    pl.semaphore_signal(barrier, inc=1, device_id=sister, device_id_type=MESH)
    pl.semaphore_wait(barrier, 1)
    out_bias, first_gain, first_shift, down_bias, second_gain, second_shift = (
        vector_ref[i : i + 1, :] for i in range(6)
    )
    sums_ref[...] = jnp.zeros_like(sums_ref)
    up_sums_ref[...] = jnp.zeros_like(up_sums_ref)

    def copy(stage, chunk):
        rows = pl.ds(chunk * rows_at, rows_at)
        return pltpu.make_async_remote_copy(
            src_ref=mine.at[stage, rows],
            dst_ref=theirs.at[stage, rows],
            send_sem=send_sem.at[stage, chunk],
            recv_sem=recv_sem.at[stage, chunk],
            device_id=sister,
            device_id_type=MESH,
        )

    def summed_with_sister(stage, chunk):
        copy(stage, chunk).wait()
        rows = pl.ds(chunk * rows_at, rows_at)
        return mine[stage, rows, :].astype(f32) + theirs[stage, rows, :].astype(f32)

    def send(stage, chunk, value):
        mine[stage, pl.ds(chunk * rows_at, rows_at), :] = value.astype(bf16)
        copy(stage, chunk).start()

    def add_row(at, value):
        sums_ref[at : at + 1, :] += jnp.sum(value, axis=0, keepdims=True)

    @pl.loop(0, CHUNKS)
    def project(chunk):
        rows = pl.ds(chunk * rows_at, rows_at)
        send(0, chunk, dot(attended_ref[rows, :], wo_ref[...]))

    @pl.loop(0, CHUNKS)
    def forward(chunk):
        rows = pl.ds(chunk * rows_at, rows_at)
        summed = summed_with_sister(0, chunk) + out_bias + x_ref[rows, :].astype(f32)
        normal, scale = normalize(summed)
        normal_ref[rows, :] = normal
        scale_ref[rows, :] = scale
        low = (normal * first_gain + first_shift).astype(bf16)
        low_ref[rows, :] = low
        for at in range(0, hidden_units, block):
            columns = slice(at, at + block)
            raised = dot(low, wu_ref[:, columns]) + bu_ref[:, columns]
            bell = 0.5 + 0.5 * lax.erf(raised * 0.7071067811865476)
            active_ref[rows, columns] = (raised * bell).astype(bf16)
            density = jnp.exp(-0.5 * raised * raised) * 0.3989422804014327
            slope_ref[rows, columns] = (bell + raised * density).astype(bf16)
        send(1, chunk, dot(active_ref[rows, :], wd_ref[...]))

    @pl.loop(0, CHUNKS)
    def turn(chunk):
        rows = pl.ds(chunk * rows_at, rows_at)
        hidden = normal_ref[rows, :] * first_gain + first_shift
        result = summed_with_sister(1, chunk) + down_bias + hidden
        normal, scale = normalize(result)
        output_ref[rows, :] = (normal * second_gain + second_shift).astype(bf16)
        cotangent = cotangent_ref[rows, :].astype(f32)
        d_result = normalize_back(cotangent * second_gain, normal, scale)
        add_row(4, cotangent * normal)
        add_row(5, cotangent)
        add_row(3, d_result)
        d_result_ref[rows, :] = d_result
        d_low = d_result.astype(bf16)
        d_low_ref[rows, :] = d_low
        for at in range(0, hidden_units, block):
            columns = slice(at, at + block)
            d_raised = dot(d_low, wd_ref[columns, :], NT) * slope_ref[rows, columns].astype(f32)
            up_sums_ref[:, columns] += jnp.sum(d_raised, axis=0, keepdims=True)
            slope_ref[rows, columns] = d_raised.astype(bf16)
        send(2, chunk, dot(slope_ref[rows, :], wu_ref[...], NT))

    @pl.loop(0, CHUNKS)
    def back(chunk):
        rows = pl.ds(chunk * rows_at, rows_at)
        d_hidden = d_result_ref[rows, :] + summed_with_sister(2, chunk)
        normal = normal_ref[rows, :]
        add_row(1, d_hidden * normal)
        add_row(2, d_hidden)
        d_summed = normalize_back(d_hidden * first_gain, normal, scale_ref[rows, :])
        add_row(0, d_summed)
        d_summed_ref[rows, :] = d_summed
        mine[2, rows, :] = d_summed.astype(bf16)

    d_low = mine[2]
    d_attended_ref[...] = dot(wo_ref[...], d_low, NT).astype(bf16)
    turned = d_low.T
    out_grad_ref[...] = dot(turned, attended_ref[...]).astype(bf16)
    turned = low_ref[...].T
    for at in range(0, hidden_units, 2 * block):
        columns = slice(at, at + 2 * block)
        up_grad_ref[:, columns] = dot(turned, slope_ref[:, columns]).astype(bf16)
    turned = d_low_ref[...].T
    for at in range(0, hidden_units, 2 * block):
        columns = slice(at, at + 2 * block)
        down_grad_ref[:, columns] = dot(turned, active_ref[:, columns]).astype(bf16)


AXES = ("y", "z_low", "z_high")


def scatter_kernel(orders, shape, *refs):
    chip_bits, rows = shape
    parts = len(orders)
    ins = refs[:parts]
    small = refs[parts]
    outs = refs[parts + 1 : 2 * parts + 1]
    small_out = refs[2 * parts + 1]
    scratch = refs[2 * parts + 2 :]
    chip = lax.axis_index("chip")
    core = lax.axis_index("core")
    half = lax.axis_index("mp")
    bits = chip_bits + 1
    place = [half] + [lax.rem(lax.div(chip, 2**i), 2) for i in range(chip_bits)]

    def partner(bit):
        if bit == 0:
            return (chip, core, 1 - half)
        step = 2 ** (bit - 1)
        return (chip + step * (1 - 2 * place[bit]), core, half)

    barrier = pltpu.get_barrier_semaphore()
    for bit in range(bits):
        pl.semaphore_signal(barrier, inc=1, device_id=partner(bit), device_id_type=MESH)
    pl.semaphore_wait(barrier, bits)
    landing = scratch[: parts * bits]
    kept = scratch[parts * bits : 2 * parts * bits]
    small_land, small_sum, send_sem, recv_sem = scratch[2 * parts * bits :]

    def view(ref, fixed):
        index = tuple(fixed.get(bit, slice(None)) for bit in reversed(range(bits)))
        return ref.at[index]

    def start(part, level):
        source = ins[part] if level == 0 else kept[part * bits + level - 1]
        bit = orders[part][level]
        left = [b for b in reversed(range(bits)) if b not in orders[part][:level]]
        index = tuple(1 - place[b] if b == bit else slice(None) for b in left)
        copy = pltpu.make_async_remote_copy(
            src_ref=source.at[index],
            dst_ref=landing[part * bits + level],
            send_sem=send_sem.at[part, level],
            recv_sem=recv_sem.at[part, level],
            device_id=partner(bit),
            device_id_type=MESH,
        )
        copy.start()
        return copy

    def finish(copy, part, level):
        copy.wait()
        source = ins[part] if level == 0 else kept[part * bits + level - 1]
        bit = orders[part][level]
        left = [b for b in reversed(range(bits)) if b not in orders[part][:level]]
        index = tuple(place[b] if b == bit else slice(None) for b in left)
        own = source[index + (slice(None), slice(None))]
        total = own.astype(f32) + landing[part * bits + level][...].astype(f32)
        if level == bits - 1:
            outs[part][...] = total
        else:
            kept[part * bits + level][...] = total.astype(bf16)

    def small_start(level):
        copy = pltpu.make_async_remote_copy(
            src_ref=small if level == 0 else small_sum.at[level - 1],
            dst_ref=small_land.at[level],
            send_sem=send_sem.at[parts, level],
            recv_sem=recv_sem.at[parts, level],
            device_id=partner(level),
            device_id_type=MESH,
        )
        copy.start()
        return copy

    flying = [small_start(0)] + [start(part, 0) for part in range(parts)]
    for level in range(bits):
        flying[0].wait()
        own = small[...] if level == 0 else small_sum[level - 1]
        total = own + small_land[level]
        if level == bits - 1:
            small_out[...] = total
        else:
            small_sum[level] = total
            flying[0] = small_start(level + 1)
        for part in range(parts):
            finish(flying[part + 1], part, level)
            if level < bits - 1:
                flying[part + 1] = start(part, level + 1)


def scatter(grads, small, chips):
    rows = grads[0].shape[0]
    bits = chips.bit_length() - 1
    share = rows // (2 * chips)
    if 2**bits == chips and share % 16 == 0:
        orders = [[0] + list(range(1, bits + 1)), [1, 0] + list(range(2, bits + 1))]
        orders.append(list(range(2, bits + 1)) + [0, 1])
        orders = [orders[i % 3] for i in range(len(grads))]
        ins = [g.reshape((2,) * (bits + 1) + (share, g.shape[1])) for g in grads]
        landing, kept = [], []
        for g in ins:
            for level in range(bits + 1):
                left = (2,) * (bits - level) + g.shape[-2:]
                landing.append(pltpu.VMEM(left, bf16))
                kept.append(pltpu.VMEM(left if level < bits else (16, 128), bf16))
        levels = bits + 1
        got = pl.pallas_call(
            functools.partial(scatter_kernel, orders, (bits, share)),
            out_shape=[jax.ShapeDtypeStruct((share, g.shape[1]), f32) for g in grads]
            + [jax.ShapeDtypeStruct(small.shape, f32)],
            in_specs=[VMEM] * (len(ins) + 1),
            out_specs=[VMEM] * (len(ins) + 1),
            scratch_shapes=landing
            + kept
            + [
                pltpu.VMEM((levels,) + small.shape, f32),
                pltpu.VMEM((levels,) + small.shape, f32),
                pltpu.SemaphoreType.DMA((len(ins) + 1, levels)),
                pltpu.SemaphoreType.DMA((len(ins) + 1, levels)),
            ],
            compiler_params=pltpu.CompilerParams(
                collective_id=1, has_side_effects=True, vmem_limit_bytes=58 << 20
            ),
        )(*ins, small)
        return got[:-1], got[-1]
    shares = [
        lax.psum_scatter(g, ("chip", "mp"), scatter_dimension=0, tiled=True).astype(f32)
        for g in grads
    ]
    return shares, lax.psum(small, ("chip", "mp"))


def crossed(value):
    return lax.ppermute(value, ("core", "mp"), [(0, 0), (1, 2), (2, 1), (3, 3)])


def body(
    tokens,
    cotangent,
    lengths,
    masked,
    qk_weight,
    qk_bias,
    value_weight,
    value_bias,
    conv_taps,
    out_weight,
    out_bias,
    first_gain,
    first_shift,
    up_weight,
    up_bias,
    down_weight,
    down_bias,
    second_gain,
    second_shift,
):
    chips = lax.axis_size("chip")
    length, model = tokens.shape
    width = value_weight.shape[1]
    units = up_weight.shape[1]
    heads = conv_taps.shape[0]
    pairs = width // PAIR
    places = jnp.arange(length, dtype=jnp.int32)
    listed = jnp.any(places[None, :] == masked.reshape(-1, 1), axis=0)
    live = jnp.where((places < lengths[0]) & jnp.logical_not(listed), 1.0, 0.0).astype(f32)
    joint = jnp.concatenate([qk_weight.reshape(model, 2 * width), value_weight], axis=1).T
    slim = jnp.concatenate(
        [
            live,
            qk_bias.reshape(-1),
            value_bias,
            conv_taps.reshape(-1),
            up_bias,
        ]
    )
    slim = crossed(slim)
    live = slim[:length].reshape(1, length)
    at = length
    bias = slim[at : at + 3 * width].reshape(3 * width, 1)
    at += 3 * width
    taps = slim[at : at + heads * KERNEL].reshape(heads, KERNEL)
    at += heads * KERNEL
    bu = slim[at:].reshape(1, units)
    x = crossed(tokens)
    joint = crossed(joint)
    wo = crossed(out_weight)
    wu = crossed(up_weight)
    wd = crossed(down_weight)
    cot = crossed(cotangent)
    shape = jax.ShapeDtypeStruct
    big = pltpu.CompilerParams(vmem_limit_bytes=58 << 20)

    qkv, first, third, attended, marks, chain = pl.pallas_call(
        attend_kernel,
        out_shape=[
            shape((3 * width, length), bf16),
            shape((width, length), bf16),
            shape((width, length), bf16),
            shape((length, width), bf16),
            shape((6, pairs, PAIR, PAIR), f32),
            shape((NS_ITERS, 4, pairs, PAIR, PAIR), f32),
        ],
        in_specs=[VMEM, VMEM, VMEM, SMEM, VMEM],
        out_specs=[VMEM] * 6,
        scratch_shapes=[pltpu.VMEM((width, length), f32)] * 3,
        compiler_params=big,
        name="attend",
    )(x, joint, bias, taps, live)

    vectors = jnp.stack([out_bias, first_gain, first_shift, down_bias, second_gain, second_shift])
    output, d_attended, d_summed, sums, up_sums, out_grad, up_grad, down_grad = pl.pallas_call(
        feed_kernel,
        out_shape=[
            shape((length, model), bf16),
            shape((width, length), bf16),
            shape((length, model), f32),
            shape((6, model), f32),
            shape((1, units), f32),
            shape((model, width), bf16),
            shape((model, units), bf16),
            shape((model, units), bf16),
        ],
        in_specs=[VMEM] * 8,
        out_specs=[VMEM] * 8,
        scratch_shapes=[
            pltpu.VMEM((3, length, model), bf16),
            pltpu.VMEM((3, length, model), bf16),
            pltpu.VMEM((length, model), f32),
            pltpu.VMEM((length, 1), f32),
            pltpu.VMEM((length, model), bf16),
            pltpu.VMEM((length, units), bf16),
            pltpu.VMEM((length, units), bf16),
            pltpu.VMEM((length, model), f32),
            pltpu.VMEM((length, model), bf16),
            pltpu.SemaphoreType.DMA((3, CHUNKS)),
            pltpu.SemaphoreType.DMA((3, CHUNKS)),
        ],
        compiler_params=pltpu.CompilerParams(
            collective_id=0, has_side_effects=True, vmem_limit_bytes=60 << 20
        ),
        name="feed",
    )(attended, x, cot, wo, vectors, wu, bu, wd)

    joint_grad, part, bias_sums, taps_grad = pl.pallas_call(
        attend_back_kernel,
        out_shape=[
            shape((model, 3 * width), bf16),
            shape((length, model), bf16),
            shape((3 * width, 1), f32),
            shape((heads, 256), f32),
        ],
        in_specs=[VMEM, VMEM, VMEM, SMEM] + [VMEM] * 6,
        out_specs=[VMEM] * 4,
        scratch_shapes=[pltpu.VMEM((3 * width, length), bf16)],
        compiler_params=big,
        name="attend_back",
    )(d_attended, x, joint, taps, live, qkv, first, third, marks, chain)

    sister = lax.ppermute(part, "core", [(0, 1), (1, 0)])
    tokens_grad = (d_summed + part.astype(f32) + sister.astype(f32)).astype(bf16)
    tokens_grad = crossed(tokens_grad)
    output = crossed(output)

    small = jnp.concatenate(
        [
            sums.reshape(-1),
            up_sums.reshape(-1),
            bias_sums.reshape(-1),
            taps_grad[:, EDGE - 1 : EDGE - 1 + KERNEL].reshape(-1),
        ]
    )
    count = small.shape[0]
    padded = -(-count // 1024) * 1024
    small = jnp.pad(small, (0, padded - count)).reshape(padded // 128, 128)
    shares, small = scatter(
        [up_grad, down_grad, jnp.concatenate([joint_grad, out_grad], axis=1)], small, chips
    )
    small = small.reshape(-1)
    common = small[: 6 * model].reshape(6, model)
    own = jnp.concatenate([s.reshape(-1) for s in shares] + [small[6 * model : count]])
    own = crossed(own)
    share = shares[0].shape[0]
    up_total = own[: share * units].reshape(share, units)
    at = share * units
    down_total = own[at : at + share * units].reshape(share, units).T
    at += share * units
    rest = own[at : at + share * 4 * width].reshape(share, 4 * width)
    at += share * 4 * width
    up_bias_total = own[at : at + units]
    at += units
    bias_total = own[at : at + 3 * width]
    at += 3 * width
    conv_total = own[at:].reshape(heads, KERNEL)
    return (
        output,
        tokens_grad,
        rest[:, : 2 * width].reshape(share, 2, width),
        bias_total[: 2 * width].reshape(2, width),
        rest[:, 2 * width : 3 * width],
        bias_total[2 * width :],
        conv_total,
        rest[:, 3 * width :].T,
        common[0],
        common[1],
        common[2],
        up_total,
        up_bias_total,
        down_total,
        common[3],
        common[4],
        common[5],
    )


def solution(mesh):
    dp = ("chip", "core")
    placed = (
        P(dp, None),
        P(dp, None),
        P(dp),
        P(dp, None),
        P(None, None, "mp"),
        P(None, "mp"),
        P(None, "mp"),
        P("mp"),
        P("mp", None),
        P("mp", None),
        P(),
        P(),
        P(),
        P(None, "mp"),
        P("mp"),
        P("mp", None),
        P(),
        P(),
        P(),
    )
    chips = mesh.shape["dp"] // 2
    fine = Mesh(mesh.devices.reshape(chips, 2, mesh.shape["mp"]), ("chip", "core", "mp"))
    return jax.shard_map(
        body,
        mesh=fine,
        in_specs=placed,
        out_specs=(
            P(dp, None),
            P(dp, None),
            P(dp, None, "mp"),
            P(None, "mp"),
            P(dp, "mp"),
            P("mp"),
            P("mp", None),
            P("mp", dp),
            P(),
            P(),
            P(),
            P(dp, "mp"),
            P("mp"),
            P("mp", dp),
            P(),
            P(),
            P(),
        ),
        check_vma=False,
    )
```

```python
import functools
import types

import jax
import jax.numpy as jnp
from jax import lax
from jax.experimental import pallas as pl
from jax.experimental.pallas import tpu as pltpu
from jax.sharding import Mesh
from jax.sharding import PartitionSpec as P

HEAD_DIM = 64
LANDMARKS = 64
NS_ITERS = 6
KERNEL = 33
EDGE = 112
BAND = 160
PAIR = 2 * HEAD_DIM
CHUNKS = 4
VMEM_LIMIT = 64 << 20

f32 = jnp.float32
bf16 = jnp.bfloat16
NN = (((1,), (0,)), ((), ()))
NT = (((1,), (1,)), ((), ()))
TN = (((0,), (0,)), ((), ()))
MESH = pl.DeviceIdType.MESH
VMEM = pl.BlockSpec(memory_space=pltpu.VMEM)
SMEM = pl.BlockSpec(memory_space=pltpu.SMEM)


def dot(a, b, dims=NN):
    return lax.dot_general(a, b, dims, preferred_element_type=f32)


def split(value):
    high = value.astype(bf16)
    return high, (value - high.astype(f32)).astype(bf16)


def dot3(a, b, dims=NN):
    return dot(a[0], b[0], dims) + (dot(a[0], b[1], dims) + dot(a[1], b[0], dims))


def iota(shape, axis):
    return lax.broadcasted_iota(jnp.int32, shape, axis)


def same_head():
    return iota((PAIR, PAIR), 0) // HEAD_DIM == iota((PAIR, PAIR), 1) // HEAD_DIM


def identity():
    return jnp.where(iota((PAIR, PAIR), 0) == iota((PAIR, PAIR), 1), 1.0, 0.0).astype(f32)


def segments(length):
    spread = length // LANDMARKS
    hit = iota((length, PAIR), 0) // spread == iota((length, PAIR), 1) % LANDMARKS
    return jnp.where(hit, 1.0, 0.0).astype(bf16)


def segments_turned(length):
    spread = length // LANDMARKS
    hit = iota((PAIR, length), 1) // spread == iota((PAIR, length), 0) % LANDMARKS
    return jnp.where(hit, 1.0, 0.0).astype(bf16)


def segment_counts(live, seg):
    rows = jnp.broadcast_to(live, (8, live.shape[1])).astype(bf16)
    return jnp.maximum(dot(rows, seg)[0:1], 1.0)


def head_sum(value):
    heads = value.shape[0] // HEAD_DIM
    cut = value.reshape(heads, HEAD_DIM, value.shape[1])
    total = jnp.sum(cut, axis=1, keepdims=True)
    return jnp.broadcast_to(total, cut.shape).reshape(value.shape)


def head_max(value):
    heads = value.shape[0] // HEAD_DIM
    cut = value.reshape(heads, HEAD_DIM, value.shape[1])
    top = jnp.max(cut, axis=1, keepdims=True)
    return jnp.broadcast_to(top, cut.shape).reshape(value.shape)


def softmax_lanes(scores):
    weights = jnp.exp(scores - jnp.max(scores, axis=1, keepdims=True))
    return weights / jnp.sum(weights, axis=1, keepdims=True)


def band_matrix(taps_ref, head, turned):
    gap = iota((BAND, 128), 0) - iota((BAND, 128), 1)
    total = jnp.zeros((BAND, 128), f32)
    for tap in range(KERNEL):
        source = KERNEL - 1 - tap if turned else tap
        weight = taps_ref[head : head + 1, source : source + 1]
        total = jnp.where(gap == tap, weight, total)
    zeros = jnp.zeros((EDGE, 128), f32)
    return jnp.concatenate([zeros, total, zeros], axis=0)


def windows(rows):
    zeros = jnp.zeros((rows.shape[0], 128), rows.dtype)
    padded = jnp.concatenate([zeros, rows, zeros], axis=1)
    blocks = rows.shape[1] // 128
    return jnp.concatenate([padded[:, b * 128 : b * 128 + 384] for b in range(blocks)], axis=0)


def blocks_down(rows):
    blocks = rows.shape[1] // 128
    return jnp.concatenate([rows[:, b * 128 : (b + 1) * 128] for b in range(blocks)], axis=0)


def blocks_back(stacked, height):
    blocks = stacked.shape[0] // height
    return jnp.concatenate([stacked[b * height : (b + 1) * height] for b in range(blocks)], axis=1)


def normalize(value):
    middle = jnp.mean(value, axis=1, keepdims=True)
    centered = value - middle
    spread = jnp.mean(centered * centered, axis=1, keepdims=True)
    scale = lax.rsqrt(spread + 1e-05)
    return centered * scale, scale


def normalize_back(grad, normal, scale):
    middle = jnp.mean(grad, axis=1, keepdims=True)
    along = jnp.mean(grad * normal, axis=1, keepdims=True)
    return scale * (grad - middle - normal * along)


def column(row):
    return jnp.broadcast_to(row, (8, row.shape[1])).T[:, 0:1]


def row_sums(value):
    parts = split(value)
    ones = jnp.ones((8, value.shape[1]), bf16)
    return (dot(ones, parts[0], NT) + dot(ones, parts[1], NT))[0:1]


class Layer:
    def __init__(self, refs, bits, parts, sizes):
        self.r = types.SimpleNamespace(**refs)
        self.bits = bits
        self.parts = parts
        self.length, self.model, self.width, self.units, self.heads = sizes
        self.chip = lax.axis_index("chip")
        self.core = lax.axis_index("core")
        self.half = lax.axis_index("mp")
        self.own = self.core == self.half
        self.other = self.core != self.half
        self.side = lax.rem(self.chip, 2)
        self.sister = (self.chip, 1 - self.core, self.half)
        self.beyond = (self.chip, self.core, 1 - self.half)
        self.cross = (self.chip, 1 - self.core, 1 - self.half)
        self.beside = (self.chip + 1 - 2 * self.side, self.core, self.half)
        self.place = [self.half] + [lax.rem(lax.div(self.chip, 2**i), 2) for i in range(bits)]
        self.levels = [0] * len(parts)
        self.small_level = 0

    def partner(self, bit):
        if bit == 0:
            return self.beyond
        step = 2 ** (bit - 1)
        return (self.chip + step * (1 - 2 * self.place[bit]), self.core, self.half)

    def greet(self):
        known = [self.sister, self.beyond, self.cross]
        known += [self.partner(bit) for bit in range(1, self.bits + 1)] if self.parts else [self.beside]
        barrier = pltpu.get_barrier_semaphore()
        for device in known:
            pl.semaphore_signal(barrier, inc=1, device_id=device, device_id_type=MESH)
        pl.semaphore_wait(barrier, len(known))

    def remote(self, source, target, sems, at, device):
        return pltpu.make_async_remote_copy(
            src_ref=source,
            dst_ref=target,
            send_sem=sems[0].at[at],
            recv_sem=sems[1].at[at],
            device_id=device,
            device_id_type=MESH,
        )


    def pieces(self):
        r = self.r
        whole = [(r.wqk.at[0], r.sqk.at[0]), (r.wqk.at[1], r.sqk.at[1]), (r.wv, r.sv), (r.wo, r.so)]
        found = [(a, b, 0, 1) for a, b in whole]
        for a, b in ((r.wu, r.su), (r.wd, r.sd)):
            found += [(a, b, 0, 2), (a, b, 1, 2)]
        return found

    def piece_rows(self, ref, sub, subs, side):
        rows = ref.shape[0] // 2
        step = rows // subs
        return pl.ds(pl.multiple_of(side * rows + sub * step, 16), step)

    def weight_copy(self, at):
        source, target, sub, subs = self.pieces()[at]
        rows = self.piece_rows(source, sub, subs, self.side)
        sems = (self.r.weight_sem.at[0], self.r.weight_sem.at[1])
        return self.remote(source.at[rows], target.at[rows], sems, at, self.beyond)

    def weight_onward(self, at, side):
        source, target, sub, subs = self.pieces()[at]
        rows = self.piece_rows(source, sub, subs, side)
        sems = (self.r.weight_sem.at[2], self.r.weight_sem.at[3])
        return self.remote(target.at[rows], target.at[rows], sems, at, self.beside)

    def locals(self):
        r = self.r
        pairs = ((r.tokens, r.x), (r.wqk, r.sqk), (r.wv, r.sv), (r.wo, r.so), (r.wu, r.su), (r.wd, r.sd), (r.cotangent, r.cot))
        return [pltpu.make_async_copy(a, b, r.local_sem.at[i]) for i, (a, b) in enumerate(pairs)]

    def item_copies(self):
        r = self.r
        sems = (r.item_sem.at[0], r.item_sem.at[1])
        pairs = ((r.live, r.live), (r.tokens, r.x), (r.cotangent, r.cot))
        return [self.remote(a, b, sems, i, self.sister) for i, (a, b) in enumerate(pairs)]

    def bias_copies(self):
        r = self.r
        sems = (r.bias_sem.at[0], r.bias_sem.at[1])
        pairs = ((r.qk_bias, r.pqk), (r.v_bias, r.pv), (r.taps, r.ptaps), (r.u_bias, r.pu))
        return [self.remote(a, b, sems, i, self.beyond) for i, (a, b) in enumerate(pairs)]

    def begin(self):
        r = self.r
        length = self.length

        @pl.when(self.own)
        def send():
            for copy in self.locals():
                copy.start()
            listed = r.masked[...].astype(f32)
            count = listed.shape[1]
            wide = jnp.broadcast_to(listed, (count, count))
            wide = jnp.where(iota((count, count), 0) == iota((count, count), 1), wide, 0.0)
            listed = jnp.sum(wide, axis=1, keepdims=True)
            places = iota((count, length), 1)
            hit = jnp.where(places.astype(f32) == listed, 1.0, 0.0)
            hit = jnp.max(hit, axis=0, keepdims=True)
            live = jnp.where(iota((1, length), 1) < r.lengths[0], 1.0 - hit, 0.0)
            r.live[...] = jnp.broadcast_to(live, (8, length))
            item = self.item_copies()
            item[0].start()
            item[1].start()
            for copy in self.bias_copies():
                copy.start()
            for at in range(3):
                self.weight_copy(at).start()
            for at in range(3, 8):
                self.weight_copy(at).start()
            item[2].start()
            r.pqk[...] = r.qk_bias[...]
            r.pv[...] = r.v_bias[...]
            r.ptaps[...] = r.taps[...]
            r.pu[...] = r.u_bias[...]
            for at in range(3):
                self.locals()[at].wait()

        @pl.when(self.other)
        def receive():
            for at in range(3):
                self.weight_copy(at).wait_recv()
                self.weight_onward(at, self.side).start()
            item = self.item_copies()
            item[0].wait_recv()
            item[1].wait_recv()
            for copy in self.bias_copies():
                copy.wait_recv()
            for at in range(3):
                self.weight_onward(at, 1 - self.side).wait_recv()

    def onward(self, *ats):
        @pl.when(self.other)
        def forward():
            for at in ats:
                self.weight_copy(at).wait_recv()
                self.weight_onward(at, self.side).start()

    def arrive(self, local, ats, cotangent=False):
        @pl.when(self.own)
        def here():
            for at in local:
                self.locals()[at].wait()

        @pl.when(self.other)
        def there():
            for at in ats:
                self.weight_onward(at, 1 - self.side).wait_recv()
            if cotangent:
                self.item_copies()[2].wait_recv()

    def drain(self):
        @pl.when(self.own)
        def here():
            for copy in self.item_copies() + self.bias_copies():
                copy.wait_send()
            for at in range(8):
                self.weight_copy(at).wait_send()

        @pl.when(self.other)
        def there():
            for at in range(8):
                self.weight_onward(at, self.side).wait_send()


    def attend(self, q_ref, k_ref, v_ref):
        r = self.r
        width, length = self.width, self.length
        pairs = width // PAIR
        live = r.live[0:1, :]
        factor = live * HEAD_DIM ** (-0.25)
        plan = (
            (q_ref, r.sqk[0], r.pqk[0:1, :], factor),
            (k_ref, r.sqk[1], r.pqk[1:2, :], factor),
            (v_ref, r.sv[...], r.pv[...], live),
        )
        for at, (kept, weight, bias, scale) in enumerate(plan):
            rows = slice(at * width, (at + 1) * width)
            value = (dot(weight.T, r.x[...], NT) + column(bias)) * scale
            kept[...] = value
            r.qkv[rows, :] = value.astype(bf16)
        self.onward(3)
        seg = segments(length)
        counts = segment_counts(live, seg)
        diagonal = same_head()
        eye = identity()
        state = []
        for pair in range(pairs):
            rows = slice(pair * PAIR, (pair + 1) * PAIR)
            q = split(q_ref[rows, :])
            k = split(k_ref[rows, :])
            qm_turned = jnp.where(diagonal, (dot(q[0], seg) + dot(q[1], seg)) / counts, 0.0)
            km_turned = jnp.where(diagonal, (dot(k[0], seg) + dot(k[1], seg)) / counts, 0.0)
            qm = qm_turned.T
            km = km_turned.T
            qm_parts = split(qm)
            scores = dot3(split(km), q)
            weights = jnp.exp(scores - head_max(scores))
            r.first[rows, :] = (weights / head_sum(weights)).astype(bf16)
            third = softmax_lanes(dot3(qm_parts, k) - 10000.0 * (1.0 - live))
            r.third[rows, :] = third.astype(bf16)
            scores = dot3(qm_parts, split(km_turned))
            second = softmax_lanes(jnp.where(diagonal, scores, -1e30))
            carried = jnp.where(diagonal, dot3(split(third), split(v_ref[rows, :]), NT), 0.0)
            r.marks[0, pair] = qm
            r.marks[1, pair] = km
            r.marks[2, pair] = second
            r.marks[3, pair] = carried
            square_sum = head_sum(jnp.sum(second * second, axis=1, keepdims=True))
            state.append((split(second), second.T / square_sum))
        self.onward(4)
        for step in range(NS_ITERS):
            following = []
            for pair in range(pairs):
                matrix, approx = state[pair]
                r.chain[step, 0, pair] = approx
                approx_parts = split(approx)
                product = dot3(matrix, approx_parts)
                r.chain[step, 1, pair] = product
                parts = split(product)
                inner = 15.0 * eye - dot3(parts, split(7.0 * eye - product))
                r.chain[step, 2, pair] = inner
                inner = 13.0 * eye - dot3(parts, split(inner))
                r.chain[step, 3, pair] = inner
                following.append((matrix, 0.25 * dot3(approx_parts, split(inner))))
            state = following
        self.onward(5)
        for pair in range(pairs):
            rows = slice(pair * PAIR, (pair + 1) * PAIR)
            inverse = state[pair][1]
            mixed = dot3(split(inverse), split(r.marks[3, pair]))
            r.marks[4, pair] = inverse
            r.marks[5, pair] = mixed
            out = dot(mixed.T.astype(bf16), r.first[rows, :])
            v = split(v_ref[rows, :])
            smoothed = []
            for half in range(2):
                head_rows = slice(half * HEAD_DIM, (half + 1) * HEAD_DIM)
                band = split(band_matrix(r.ptaps, 2 * pair + half, False))
                high = windows(v[0][head_rows])
                smooth = dot(high, band[0]) + (
                    dot(high, band[1]) + dot(windows(v[1][head_rows]), band[0])
                )
                smoothed.append(blocks_back(smooth, HEAD_DIM))
            out = out + jnp.concatenate(smoothed, axis=0)
            r.attended[:, rows] = out.astype(bf16).T

    def attend_back(self, joined):
        r = self.r
        width, length = self.width, self.length
        pairs = width // PAIR
        live = r.live[0:1, :]
        factor = live * HEAD_DIM ** (-0.25)
        diagonal = same_head()
        flip = jnp.where(iota((128, 128), 0) + iota((128, 128), 1) == 127, 1.0, 0.0).astype(bf16)
        state = []
        for pair in range(pairs):
            rows = slice(pair * PAIR, (pair + 1) * PAIR)
            d_out = r.d_attended[rows, :]
            d_mixed = split(jnp.where(diagonal, dot(r.first[rows, :], d_out, NT), 0.0))
            d_inverse = dot3(d_mixed, split(r.marks[3, pair]), NT)
            d_carried = dot3(split(r.marks[4, pair]), d_mixed, TN)
            state.append((d_inverse, jnp.zeros((PAIR, PAIR), f32), d_carried))
        for step in reversed(range(NS_ITERS)):
            following = []
            for pair in range(pairs):
                d_approx, d_matrix, d_carried = state[pair]
                approx = split(r.chain[step, 0, pair])
                product = r.chain[step, 1, pair]
                inner = split(7.0 * identity() - product)
                product = split(product)
                middle = split(r.chain[step, 2, pair])
                outer = split(r.chain[step, 3, pair])
                d_parts = split(0.25 * d_approx)
                d_outer = split(dot3(approx, d_parts, TN))
                d_next = dot3(d_parts, outer, NT)
                d_product = -dot3(d_outer, middle, NT)
                d_middle = split(-dot3(product, d_outer, TN))
                d_product = d_product - dot3(d_middle, inner, NT) + dot3(product, d_middle, TN)
                d_product = split(d_product)
                d_matrix = d_matrix + dot3(d_product, approx, NT)
                d_next = d_next + dot3(split(r.marks[2, pair]), d_product, TN)
                following.append((d_next, d_matrix, d_carried))
            state = following
            self.tick()
        seg_turned = segments_turned(length)
        counts = segment_counts(live, segments(length))
        for pair in range(pairs):
            rows = slice(pair * PAIR, (pair + 1) * PAIR)
            k_rows = slice(width + pair * PAIR, width + (pair + 1) * PAIR)
            v_rows = slice(2 * width + pair * PAIR, 2 * width + (pair + 1) * PAIR)
            d_approx, d_matrix, d_carried = state[pair]
            qm = r.marks[0, pair]
            km = r.marks[1, pair]
            second = r.marks[2, pair]
            square_sum = head_sum(jnp.sum(second * second, axis=1, keepdims=True))
            turned = d_approx.T
            along = head_sum(jnp.sum(turned * second, axis=1, keepdims=True))
            d_matrix = d_matrix + turned / square_sum
            d_matrix = d_matrix - second * (2.0 * along / (square_sum * square_sum))
            d_scores = second * (d_matrix - jnp.sum(d_matrix * second, axis=1, keepdims=True))
            d_scores = split(d_scores)
            d_out = r.d_attended[rows, :]
            first = r.first[rows, :].astype(f32)
            d_first = dot(r.marks[5, pair].astype(bf16), d_out)
            d_first = (first * (d_first - head_sum(d_first * first))).astype(bf16)
            third = r.third[rows, :]
            d_third = dot(d_carried.astype(bf16), r.qkv[v_rows, :])
            wide = third.astype(f32)
            d_third = wide * (d_third - jnp.sum(d_third * wide, axis=1, keepdims=True))
            d_third = d_third.astype(bf16)
            d_qm = dot3(d_scores, split(km))
            d_qm = d_qm + jnp.where(diagonal, dot(d_third, r.qkv[k_rows, :], NT), 0.0)
            d_km = dot3(d_scores, split(qm), TN)
            d_km = d_km + jnp.where(diagonal, dot(d_first, r.qkv[rows, :], NT), 0.0)
            d_qm = split(d_qm.T / counts)
            d_km = split(d_km.T / counts)
            d_q = dot(km.T.astype(bf16), d_first) + (dot(d_qm[0], seg_turned) + dot(d_qm[1], seg_turned))
            d_k = dot(qm.T.astype(bf16), d_third) + (dot(d_km[0], seg_turned) + dot(d_km[1], seg_turned))
            d_v = dot(d_carried.T.astype(bf16), third)
            smoothed = []
            for half in range(2):
                head = 2 * pair + half
                head_rows = slice(half * HEAD_DIM, (half + 1) * HEAD_DIM)
                band = split(band_matrix(r.ptaps, head, True))
                around = windows(d_out[head_rows])
                smoothed.append(blocks_back(dot(around, band[0]) + dot(around, band[1]), HEAD_DIM))
                start = 2 * width + head * HEAD_DIM
                flipped = dot(blocks_down(d_out[head_rows]), flip).astype(bf16)
                products = dot(flipped, windows(r.qkv[start : start + HEAD_DIM, :]), TN)
                lined = pltpu.roll(products, 17, 1, stride=1, stride_axis=0)
                total = jnp.sum(lined, axis=0, keepdims=True)
                r.small[5:6, head * 128 : (head + 1) * 128] = total[:, 256:]
            d_v = d_v + jnp.concatenate(smoothed, axis=0)
            for at, (value, scale) in enumerate(((d_q, factor), (d_k, factor), (d_v, live))):
                place = slice(at * width + pair * PAIR, at * width + (pair + 1) * PAIR)
                value = value * scale
                joined[place, :] = value.astype(bf16)
                r.small[4:5, place] = row_sums(value)
            self.tick()


    def exchange(self, stage, chunk):
        r = self.r
        at = stage % 2
        rows_at = self.length // CHUNKS
        rows = pl.ds(chunk * rows_at, rows_at)
        sems = (r.send_sem.at[stage], r.recv_sem.at[stage])
        return self.remote(r.mine.at[at, rows], r.theirs.at[at, rows], sems, chunk, self.sister)

    def chunk_rows(self, chunk):
        rows_at = self.length // CHUNKS
        start = chunk * rows_at
        if not isinstance(chunk, int):
            start = pl.multiple_of(start, rows_at)
        return pl.ds(start, rows_at)

    def together(self, stage, chunk):
        self.exchange(stage, chunk).wait()
        rows = self.chunk_rows(chunk)
        at = stage % 2
        return self.r.mine[at, rows, :].astype(f32) + self.r.theirs[at, rows, :].astype(f32)

    def offer(self, stage, chunk, value):
        self.r.mine[stage % 2, self.chunk_rows(chunk), :] = value.astype(bf16)
        self.exchange(stage, chunk).start()

    def feed(self, low_ref, active_ref, slope_ref, d_low_ref, scale_ref):
        r = self.r
        block = 256
        units, width = self.units, self.width
        out_bias, first_gain, first_shift = r.out_bias[...], r.first_gain[...], r.first_shift[...]
        down_bias, second_gain, second_shift = r.down_bias[...], r.second_gain[...], r.second_shift[...]
        r.small[...] = jnp.zeros_like(r.small)

        def add_row(at, value):
            columns = slice((at % 2) * self.model, (at % 2 + 1) * self.model)
            r.small[at // 2 : at // 2 + 1, columns] += jnp.sum(value, axis=0, keepdims=True)

        self.arrive([3], [3])

        @pl.loop(0, CHUNKS)
        def project(chunk):
            self.offer(0, chunk, dot(r.attended[self.chunk_rows(chunk), :], r.so[...]))

        self.onward(6)
        self.arrive([4], [4, 5])
        self.onward(7)
        self.arrive([5], [6, 7])

        @pl.loop(0, CHUNKS)
        def forward(chunk):
            rows = self.chunk_rows(chunk)
            summed = self.together(0, chunk) + out_bias + r.x[rows, :].astype(f32)
            normal, scale = normalize(summed)
            r.normal[rows, :] = normal
            scale_ref[rows, :] = scale
            low = (normal * first_gain + first_shift).astype(bf16)
            low_ref[rows, :] = low
            for at in range(0, units, block):
                columns = slice(at, at + block)
                raised = dot(low, r.su[:, columns]) + r.pu[:, columns]
                bell = 0.5 + 0.5 * lax.erf(raised * 0.7071067811865476)
                active_ref[rows, columns] = (raised * bell).astype(bf16)
                density = jnp.exp(-0.5 * raised * raised) * 0.3989422804014327
                slope_ref[rows, columns] = (bell + raised * density).astype(bf16)
            self.offer(1, chunk, dot(active_ref[rows, :], r.sd[...]))

        self.arrive([6], [], True)

        @pl.loop(0, CHUNKS)
        def turn(chunk):
            rows = self.chunk_rows(chunk)
            hidden = r.normal[rows, :] * first_gain + first_shift
            result = self.together(1, chunk) + down_bias + hidden
            normal, scale = normalize(result)
            r.out[rows, :] = (normal * second_gain + second_shift).astype(bf16)
            cotangent = r.cot[rows, :].astype(f32)
            d_result = normalize_back(cotangent * second_gain, normal, scale)
            add_row(4, cotangent * normal)
            add_row(5, cotangent)
            add_row(3, d_result)
            d_low = d_result.astype(bf16)
            d_low_ref[rows, :] = d_low
            for at in range(0, units, block):
                columns = slice(at, at + block)
                d_raised = dot(d_low, r.sd[columns, :], NT) * slope_ref[rows, columns].astype(f32)
                r.small[3:4, columns] += jnp.sum(d_raised, axis=0, keepdims=True)
                slope_ref[rows, columns] = d_raised.astype(bf16)
            self.offer(2, chunk, dot(slope_ref[rows, :], r.su[...], NT))

        for chunk in range(CHUNKS):
            self.deliver(r.out, r.output, 0, chunk)
        turned = d_low_ref[...].T
        for at in range(0, units, block):
            columns = slice(at, at + block)
            self.store(r.g_down, columns, dot(turned, active_ref[:, columns]))
        self.launch(r.g_down)

        @pl.loop(0, CHUNKS)
        def back(chunk):
            rows = self.chunk_rows(chunk)
            d_hidden = d_low_ref[rows, :].astype(f32) + self.together(2, chunk)
            normal = r.normal[rows, :]
            add_row(1, d_hidden * normal)
            add_row(2, d_hidden)
            d_summed = normalize_back(d_hidden * first_gain, normal, scale_ref[rows, :])
            add_row(0, d_summed)
            r.normal[rows, :] = d_summed
            d_low_ref[rows, :] = d_summed.astype(bf16)

        turned = low_ref[...].T
        for at in range(0, units, block):
            columns = slice(at, at + block)
            self.store(r.g_up, columns, dot(turned, slope_ref[:, columns]))
        self.launch(r.g_up)
        r.d_attended[...] = dot(r.so[...], d_low_ref[...], NT).astype(bf16)
        turned = d_low_ref[...].T
        self.store(r.g_rest, slice(3 * width, 4 * width), dot(turned, r.attended[...]))

    def store(self, ref, columns, value):
        value = value.astype(bf16)
        if self.parts:
            value = value.reshape(ref.shape[:-1] + (value.shape[1],))
            ref[:, :, :, :, :, columns] = value
        else:
            ref[:, columns] = value

    def deliver(self, source, target, at, chunk):
        r = self.r
        rows = self.chunk_rows(chunk)
        local, away = self.deliveries(source, target, at, chunk)

        @pl.when(self.own)
        def here():
            local.start()
            if chunk < CHUNKS // 2:
                away.start()

        if chunk >= CHUNKS // 2:

            @pl.when(self.other)
            def there():
                away.start()

    def deliveries(self, source, target, at, chunk):
        r = self.r
        rows = self.chunk_rows(chunk)
        local = pltpu.make_async_copy(source.at[rows], target.at[rows], r.home_sem.at[at, chunk])
        device = self.beyond if chunk < CHUNKS // 2 else self.cross
        sems = (r.away_sem.at[2 * at], r.away_sem.at[2 * at + 1])
        return local, self.remote(source.at[rows], target.at[rows], sems, chunk, device)

    def delivered(self, source, target, at):
        for chunk in range(CHUNKS):
            local, away = self.deliveries(source, target, at, chunk)

            @pl.when(self.own)
            def here():
                local.wait()
                if chunk < CHUNKS // 2:
                    away.wait_send()

            @pl.when(self.other)
            def there():
                away.wait_recv()
                if chunk >= CHUNKS // 2:
                    away.wait_send()


    def part_copy(self, part, level):
        name, start, count, order = self.parts[part]
        ref = getattr(self.r, name)
        bit = order[level]
        index = []
        for b in reversed(range(self.bits + 1)):
            if b in order[:level]:
                index.append(self.place[b])
            else:
                index.append(1 - self.place[b] if b == bit else slice(None))
        source = ref.at[tuple(index) + (slice(None), slice(start, start + count))]
        landing = self.r.landings[part * (self.bits + 1) + level]
        sems = (self.r.part_sem.at[0, part], self.r.part_sem.at[1, part])
        return self.remote(source, landing, sems, level, self.partner(bit))

    def part_finish(self, part, level):
        name, start, count, order = self.parts[part]
        ref = getattr(self.r, name)
        self.part_copy(part, level).wait()
        index = []
        for b in reversed(range(self.bits + 1)):
            index.append(self.place[b] if b in order[: level + 1] else slice(None))
        index = tuple(index) + (slice(None), slice(start, start + count))
        landing = self.r.landings[part * (self.bits + 1) + level]
        total = ref[index].astype(f32) + landing[...].astype(f32)
        if level < self.bits:
            ref[index] = total.astype(bf16)
        else:
            self.part_last(part, total)

    def part_swap(self, part):
        name, start, count, order = self.parts[part]
        ref = self.r.swap_out.at[part]
        sems = (self.r.swap_sem.at[0], self.r.swap_sem.at[1])
        return self.remote(ref, self.r.swap_in.at[part], sems, part, self.cross)

    def part_target(self, part):
        name, start, count, order = self.parts[part]
        return getattr(self.r, "t" + name[1:]), slice(start, start + count)

    def part_last(self, part, total):
        target, columns = self.part_target(part)

        @pl.when(self.own)
        def here():
            target[:, columns] = total

        @pl.when(self.other)
        def there():
            self.r.swap_out[part] = total.astype(bf16)
            self.part_swap(part).start()

    def launch(self, ref):
        for part, (name, start, count, order) in enumerate(self.parts):
            if getattr(self.r, name) is ref:
                self.part_copy(part, 0).start()

    def advance(self, part):
        level = self.levels[part]
        if level > self.bits:
            return
        self.part_finish(part, level)
        if level < self.bits:
            self.part_copy(part, level + 1).start()
        self.levels[part] = level + 1

    def tick(self):
        if self.parts and self.agenda:
            for part in self.agenda.pop(0):
                self.advance(part)

    def small_copy(self, level):
        r = self.r
        source = r.small if level == 0 else r.small_sum.at[level - 1]
        sems = (r.small_sem.at[0], r.small_sem.at[1])
        return self.remote(source, r.small_land.at[level], sems, level, self.partner(level))

    def small_advance(self, level):
        r = self.r
        self.small_copy(level).wait()
        own = r.small[...] if level == 0 else r.small_sum[level - 1]
        r.small_sum[level] = own + r.small_land[level]
        if level < self.bits:
            self.small_copy(level + 1).start()

    def small_swap(self):
        r = self.r
        sems = (r.small_sem.at[0], r.small_sem.at[1])
        return self.remote(r.small_sum.at[self.bits], r.small_sister, sems, self.bits + 1, self.sister)

    def small_done(self):
        r = self.r
        total = r.small_sum[self.bits]
        r.tsmall[0:3, :] = total[0:3]

        @pl.when(self.own)
        def here():
            self.small_swap().start()
            r.tsmall[3:8, :] = total[3:8]
            self.small_swap().wait_send()

        @pl.when(self.other)
        def there():
            self.small_swap().wait_recv()
            r.tsmall[3:8, :] = r.small_sister[3:8, :]

    def finish(self, joined):
        r = self.r
        width, model, length = self.width, self.model, self.length
        bits = self.bits
        if self.parts:
            self.small_copy(0).start()
        turned = r.x[...].T
        for at in range(3):
            rows = slice(at * width, (at + 1) * width)
            self.store(r.g_rest, rows, dot(turned, joined[rows, :], NT))
        self.launch(r.g_rest)
        rows_at = length // CHUNKS
        for chunk in range(CHUNKS):
            columns = slice(chunk * rows_at, (chunk + 1) * rows_at)
            back = dot(r.sqk[0], joined[0:width, columns])
            back = back + dot(r.sqk[1], joined[width : 2 * width, columns])
            back = back + dot(r.sv[...], joined[2 * width :, columns])
            self.offer(3, chunk, back.astype(bf16).T)
        for chunk in range(CHUNKS):
            rows = self.chunk_rows(chunk)
            r.grad[rows, :] = (r.normal[rows, :] + self.together(3, chunk)).astype(bf16)
            self.deliver(r.grad, r.tokens_grad, 1, chunk)
        if self.parts:
            for level in range(bits + 1):
                self.small_advance(level)
                for part in range(len(self.parts)):
                    if self.levels[part] <= level:
                        self.advance(part)
            self.small_done()
        else:
            r.tsmall[...] = r.small[...]
        self.delivered(r.out, r.output, 0)
        self.delivered(r.grad, r.tokens_grad, 1)
        for part in range(len(self.parts)):
            target, columns = self.part_target(part)

            @pl.when(self.other)
            def there():
                self.part_swap(part).wait()
                target[:, columns] = r.swap_in[part].astype(f32)

        self.drain()


def layer_kernel(names, bits, parts, agenda, sizes, *refs):
    found = dict(zip(names, refs))
    found["landings"] = refs[len(names) :]
    layer = Layer(found, bits, parts, sizes)
    layer.agenda = list(agenda)
    length, model, width, units, heads = sizes
    layer.greet()
    layer.begin()
    pl.run_scoped(layer.attend, *[pltpu.VMEM((width, length), f32)] * 3)
    pl.run_scoped(
        layer.feed,
        pltpu.VMEM((length, model), bf16),
        pltpu.VMEM((length, units), bf16),
        pltpu.VMEM((length, units), bf16),
        pltpu.VMEM((length, model), bf16),
        pltpu.VMEM((length, 1), f32),
    )

    def back(joined):
        layer.attend_back(joined)
        layer.finish(joined)

    pl.run_scoped(back, pltpu.VMEM((3 * width, length), bf16))


ORDERS = {
    3: ([0, 1, 2, 3], [1, 2, 3, 0], [0, 1, 2, 3], [2, 1, 3, 0], [1, 2, 3, 0], [2, 1, 3, 0]),
}
AGENDA = ([], [], [], [], [0, 1], [], [2, 3], [], [0, 1])


def body(
    tokens,
    cotangent,
    lengths,
    masked,
    qk_weight,
    qk_bias,
    value_weight,
    value_bias,
    conv_taps,
    out_weight,
    out_bias,
    first_gain,
    first_shift,
    up_weight,
    up_bias,
    down_weight,
    down_bias,
    second_gain,
    second_shift,
):
    chips = lax.axis_size("chip")
    length, model = tokens.shape
    width = value_weight.shape[1]
    units = up_weight.shape[1]
    heads = conv_taps.shape[0]
    pairs = width // PAIR
    bits = chips.bit_length() - 1
    share = model // (2 * chips)
    fused = bits in ORDERS and share % 16 == 0
    parts = []
    if fused:
        count = units // 2
        names = ("g_down", "g_down", "g_up", "g_up", "g_rest", "g_rest")
        for at, (name, order) in enumerate(zip(names, ORDERS[bits])):
            parts.append((name, (at % 2) * count, count, order))
    shape = jax.ShapeDtypeStruct
    hbm = pl.BlockSpec(memory_space=pl.ANY)
    row = lambda v: v.reshape(1, -1)
    inputs = [
        ("tokens", tokens, hbm),
        ("cotangent", cotangent, hbm),
        ("wqk", jnp.transpose(qk_weight, (1, 0, 2)), hbm),
        ("wv", value_weight, hbm),
        ("wo", out_weight, hbm),
        ("wu", up_weight, hbm),
        ("wd", down_weight, hbm),
        ("lengths", lengths, SMEM),
        ("masked", masked, VMEM),
        ("qk_bias", qk_bias, VMEM),
        ("v_bias", row(value_bias), VMEM),
        ("taps", conv_taps, VMEM),
        ("u_bias", row(up_bias), VMEM),
        ("out_bias", row(out_bias), VMEM),
        ("first_gain", row(first_gain), VMEM),
        ("first_shift", row(first_shift), VMEM),
        ("down_bias", row(down_bias), VMEM),
        ("second_gain", row(second_gain), VMEM),
        ("second_shift", row(second_shift), VMEM),
    ]
    outputs = [("output", shape((length, model), bf16), hbm), ("tokens_grad", shape((length, model), bf16), hbm)]
    outputs.append(("tsmall", shape((8, units), f32), VMEM))
    scratch = []
    for name in ("down", "up", "rest"):
        if fused:
            outputs.append(("t_" + name, shape((share, units), f32), VMEM))
            scratch.append(("g_" + name, pltpu.VMEM((2,) * (bits + 1) + (share, units), bf16)))
        else:
            outputs.append(("g_" + name, shape((model, units), bf16), VMEM))
    dma = pltpu.SemaphoreType.DMA
    scratch += [
        ("sqk", pltpu.VMEM((2, model, width), bf16)),
        ("sv", pltpu.VMEM((model, width), bf16)),
        ("so", pltpu.VMEM((width, model), bf16)),
        ("su", pltpu.VMEM((model, units), bf16)),
        ("sd", pltpu.VMEM((units, model), bf16)),
        ("x", pltpu.VMEM((length, model), bf16)),
        ("cot", pltpu.VMEM((length, model), bf16)),
        ("live", pltpu.VMEM((8, length), f32)),
        ("pqk", pltpu.VMEM((2, width), f32)),
        ("pv", pltpu.VMEM((1, width), f32)),
        ("ptaps", pltpu.VMEM((heads, KERNEL), f32)),
        ("pu", pltpu.VMEM((1, units), f32)),
        ("qkv", pltpu.VMEM((3 * width, length), bf16)),
        ("first", pltpu.VMEM((width, length), bf16)),
        ("third", pltpu.VMEM((width, length), bf16)),
        ("attended", pltpu.VMEM((length, width), bf16)),
        ("marks", pltpu.VMEM((6, pairs, PAIR, PAIR), f32)),
        ("chain", pltpu.VMEM((NS_ITERS, 4, pairs, PAIR, PAIR), f32)),
        ("mine", pltpu.VMEM((2, length, model), bf16)),
        ("theirs", pltpu.VMEM((2, length, model), bf16)),
        ("normal", pltpu.VMEM((length, model), f32)),
        ("d_attended", pltpu.VMEM((width, length), bf16)),
        ("out", pltpu.VMEM((length, model), bf16)),
        ("grad", pltpu.VMEM((length, model), bf16)),
        ("small", pltpu.VMEM((8, units), f32)),
        ("weight_sem", dma((4, 8))),
        ("local_sem", dma((7,))),
        ("item_sem", dma((2, 3))),
        ("bias_sem", dma((2, 4))),
        ("send_sem", dma((4, CHUNKS))),
        ("recv_sem", dma((4, CHUNKS))),
        ("home_sem", dma((2, CHUNKS))),
        ("away_sem", dma((4, CHUNKS))),
    ]
    landings = []
    if fused:
        levels = bits + 1
        scratch += [
            ("small_land", pltpu.VMEM((levels, 8, units), f32)),
            ("small_sum", pltpu.VMEM((levels, 8, units), f32)),
            ("small_sister", pltpu.VMEM((8, units), f32)),
            ("small_sem", dma((2, levels + 1))),
            ("part_sem", dma((2, len(parts), levels))),
            ("swap_sem", dma((2, len(parts)))),
            ("swap_out", pltpu.VMEM((len(parts), share, parts[0][2]), bf16)),
            ("swap_in", pltpu.VMEM((len(parts), share, parts[0][2]), bf16)),
        ]
        for name, start, count, order in parts:
            landings += [pltpu.VMEM((2,) * (bits - level) + (share, count), bf16) for level in range(levels)]
    names = [n for n, *_ in inputs + outputs + scratch]
    got = pl.pallas_call(
        functools.partial(
            layer_kernel, names, bits, parts, AGENDA, (length, model, width, units, heads)
        ),
        out_shape=[kind for _, kind, _ in outputs],
        in_specs=[spec for *_, spec in inputs],
        out_specs=[spec for *_, spec in outputs],
        scratch_shapes=[kind for _, kind in scratch] + landings,
        compiler_params=pltpu.CompilerParams(
            collective_id=0, has_side_effects=True, vmem_limit_bytes=VMEM_LIMIT
        ),
        name="layer",
    )(*[value for _, value, _ in inputs])
    output, tokens_grad, small, down, up, rest = got
    if not fused:
        swap = lambda v: lax.ppermute(v, ("core", "mp"), [(0, 0), (1, 2), (2, 1), (3, 3)])
        gather = lambda g: swap(
            lax.psum_scatter(g, ("chip", "mp"), scatter_dimension=0, tiled=True).astype(f32)
        )
        down, up, rest = gather(down), gather(up), gather(rest)
        small = lax.psum(small, ("chip", "mp"))
        small = jnp.concatenate([small[:3], swap(small[3:])], axis=0)
    taps = small[5, : heads * 128].reshape(heads, 128)[:, :KERNEL]
    return (
        output,
        tokens_grad,
        rest[:, : 2 * width].reshape(share, 2, width),
        small[4, : 2 * width].reshape(2, width),
        rest[:, 2 * width : 3 * width],
        small[4, 2 * width : 3 * width],
        taps,
        rest[:, 3 * width :].T,
        small[0, :model],
        small[0, model:],
        small[1, :model],
        up,
        small[3],
        down.T,
        small[1, model:],
        small[2, :model],
        small[2, model:],
    )


def solution(mesh):
    dp = ("chip", "core")
    placed = (
        P(dp, None),
        P(dp, None),
        P(dp),
        P(dp, None),
        P(None, None, "mp"),
        P(None, "mp"),
        P(None, "mp"),
        P("mp"),
        P("mp", None),
        P("mp", None),
        P(),
        P(),
        P(),
        P(None, "mp"),
        P("mp"),
        P("mp", None),
        P(),
        P(),
        P(),
    )
    chips = mesh.shape["dp"] // 2
    fine = Mesh(mesh.devices.reshape(chips, 2, mesh.shape["mp"]), ("chip", "core", "mp"))
    return jax.shard_map(
        body,
        mesh=fine,
        in_specs=placed,
        out_specs=(
            P(dp, None),
            P(dp, None),
            P(dp, None, "mp"),
            P(None, "mp"),
            P(dp, "mp"),
            P("mp"),
            P("mp", None),
            P("mp", dp),
            P(),
            P(),
            P(),
            P(dp, "mp"),
            P("mp"),
            P("mp", dp),
            P(),
            P(),
            P(),
        ),
        check_vma=False,
    )
```

```python
import functools
import types

import jax
import jax.numpy as jnp
from jax import lax
from jax.experimental import pallas as pl
from jax.experimental.pallas import tpu as pltpu
from jax.sharding import Mesh
from jax.sharding import PartitionSpec as P

HEAD_DIM = 64
LANDMARKS = 64
NS_ITERS = 6
KERNEL = 33
EDGE = 112
BAND = 160
PAIR = 2 * HEAD_DIM
CHUNKS = 4
PIECES = 8
AHEAD = 2
VMEM_LIMIT = 64 << 20

f32 = jnp.float32
bf16 = jnp.bfloat16
NN = (((1,), (0,)), ((), ()))
NT = (((1,), (1,)), ((), ()))
TN = (((0,), (0,)), ((), ()))
MESH = pl.DeviceIdType.MESH
VMEM = pl.BlockSpec(memory_space=pltpu.VMEM)
SMEM = pl.BlockSpec(memory_space=pltpu.SMEM)


def dot(a, b, dims=NN):
    return lax.dot_general(a, b, dims, preferred_element_type=f32)


def split(value):
    high = value.astype(bf16)
    return high, (value - high.astype(f32)).astype(bf16)


def dot3(a, b, dims=NN):
    return dot(a[0], b[0], dims) + (dot(a[0], b[1], dims) + dot(a[1], b[0], dims))


def iota(shape, axis):
    return lax.broadcasted_iota(jnp.int32, shape, axis)


def same_head():
    return iota((PAIR, PAIR), 0) // HEAD_DIM == iota((PAIR, PAIR), 1) // HEAD_DIM


def identity():
    return jnp.where(iota((PAIR, PAIR), 0) == iota((PAIR, PAIR), 1), 1.0, 0.0).astype(f32)


def segments(length):
    spread = length // LANDMARKS
    hit = iota((length, PAIR), 0) // spread == iota((length, PAIR), 1) % LANDMARKS
    return jnp.where(hit, 1.0, 0.0).astype(bf16)


def segments_turned(length):
    spread = length // LANDMARKS
    hit = iota((PAIR, length), 1) // spread == iota((PAIR, length), 0) % LANDMARKS
    return jnp.where(hit, 1.0, 0.0).astype(bf16)


def segment_counts(live, seg):
    rows = jnp.broadcast_to(live, (8, live.shape[1])).astype(bf16)
    return jnp.maximum(dot(rows, seg)[0:1], 1.0)


def head_sum(value):
    heads = value.shape[0] // HEAD_DIM
    cut = value.reshape(heads, HEAD_DIM, value.shape[1])
    total = jnp.sum(cut, axis=1, keepdims=True)
    return jnp.broadcast_to(total, cut.shape).reshape(value.shape)


def head_max(value):
    heads = value.shape[0] // HEAD_DIM
    cut = value.reshape(heads, HEAD_DIM, value.shape[1])
    top = jnp.max(cut, axis=1, keepdims=True)
    return jnp.broadcast_to(top, cut.shape).reshape(value.shape)


def softmax_lanes(scores):
    weights = jnp.exp(scores - jnp.max(scores, axis=1, keepdims=True))
    return weights / jnp.sum(weights, axis=1, keepdims=True)


def band_matrix(taps_ref, head, turned):
    gap = iota((BAND, 128), 0) - iota((BAND, 128), 1)
    total = jnp.zeros((BAND, 128), f32)
    for tap in range(KERNEL):
        source = KERNEL - 1 - tap if turned else tap
        weight = taps_ref[head : head + 1, source : source + 1]
        total = jnp.where(gap == tap, weight, total)
    zeros = jnp.zeros((EDGE, 128), f32)
    return jnp.concatenate([zeros, total, zeros], axis=0)


def windows(rows):
    zeros = jnp.zeros((rows.shape[0], 128), rows.dtype)
    padded = jnp.concatenate([zeros, rows, zeros], axis=1)
    blocks = rows.shape[1] // 128
    return jnp.concatenate([padded[:, b * 128 : b * 128 + 384] for b in range(blocks)], axis=0)


def blocks_down(rows):
    blocks = rows.shape[1] // 128
    return jnp.concatenate([rows[:, b * 128 : (b + 1) * 128] for b in range(blocks)], axis=0)


def blocks_back(stacked, height):
    blocks = stacked.shape[0] // height
    return jnp.concatenate([stacked[b * height : (b + 1) * height] for b in range(blocks)], axis=1)


def normalize(value):
    middle = jnp.mean(value, axis=1, keepdims=True)
    centered = value - middle
    spread = jnp.mean(centered * centered, axis=1, keepdims=True)
    scale = lax.rsqrt(spread + 1e-05)
    return centered * scale, scale


def normalize_back(grad, normal, scale):
    middle = jnp.mean(grad, axis=1, keepdims=True)
    along = jnp.mean(grad * normal, axis=1, keepdims=True)
    return scale * (grad - middle - normal * along)


def column(row):
    return jnp.broadcast_to(row, (8, row.shape[1])).T[:, 0:1]


def row_sums(value):
    parts = split(value)
    ones = jnp.ones((8, value.shape[1]), bf16)
    return (dot(ones, parts[0], NT) + dot(ones, parts[1], NT))[0:1]


class Layer:
    def __init__(self, refs, bits, parts, sizes):
        self.r = types.SimpleNamespace(**refs)
        self.bits = bits
        self.parts = parts
        self.length, self.model, self.width, self.units, self.heads = sizes
        self.chip = lax.axis_index("chip")
        self.core = lax.axis_index("core")
        self.half = lax.axis_index("mp")
        self.own = self.core == self.half
        self.other = self.core != self.half
        self.sister = (self.chip, 1 - self.core, self.half)
        self.beyond = (self.chip, self.core, 1 - self.half)
        self.cross = (self.chip, 1 - self.core, 1 - self.half)
        self.place = [self.half] + [lax.rem(lax.div(self.chip, 2**i), 2) for i in range(bits)]
        self.levels = [None] * len(parts)
        self.small_level = 0

    def partner(self, bit):
        if bit == 0:
            return self.beyond
        step = 2 ** (bit - 1)
        return (self.chip + step * (1 - 2 * self.place[bit]), self.core, self.half)

    def greet(self):
        known = [self.sister, self.beyond, self.cross]
        known += [self.partner(bit) for bit in range(1, (self.bits if self.parts else 2) + 1)]
        barrier = pltpu.get_barrier_semaphore()
        for device in known:
            pl.semaphore_signal(barrier, inc=1, device_id=device, device_id_type=MESH)
        pl.semaphore_wait(barrier, len(known))

    def remote(self, source, target, sems, at, device):
        return pltpu.make_async_remote_copy(
            src_ref=source,
            dst_ref=target,
            send_sem=sems[0].at[at],
            recv_sem=sems[1].at[at],
            device_id=device,
            device_id_type=MESH,
        )


    def pieces(self):
        r = self.r
        found = []
        for a, b in ((r.wqk.at[0], r.sqk.at[0]), (r.wqk.at[1], r.sqk.at[1]), (r.wv, r.sv), (r.wo, r.so)):
            found.append((a, b, 0, 1))
        for a, b in ((r.wu, r.su), (r.wd, r.sd)):
            found += [(a, b, sub, 2) for sub in range(2)]
        return found

    def quarter(self, flips):
        low, high = self.place[1], self.place[2]
        if 0 in flips:
            low = 1 - low
        if 1 in flips:
            high = 1 - high
        return low + 2 * high

    def weight_copy(self, kind, at, arriving=False):
        source, target, sub, subs = self.pieces()[at]
        first, second = (0, 1) if at % 2 else (1, 0)
        if kind == "over":
            flips, device, lane = (), self.cross, 0
        elif kind == "first":
            flips, device, lane = (), self.partner(first + 1), 1
            if arriving:
                flips = (first,)
        elif kind == "second":
            flips, device, lane = (), self.partner(second + 1), 2
            if arriving:
                flips = (second,)
        else:
            flips, device, lane = (first,), self.partner(second + 1), 3
            if arriving:
                flips = (first, second)
        rows = source.shape[0] // 4
        step = rows // subs
        start = self.quarter(flips) * rows + sub * step
        place = pl.ds(pl.multiple_of(start, 16), step)
        sems = (self.r.weight_sem.at[2 * lane], self.r.weight_sem.at[2 * lane + 1])
        begin = source if kind == "over" else target
        return self.remote(begin.at[place], target.at[place], sems, at, device)

    def relay(self, at):
        self.weight_copy("over", at, True).wait_recv()
        self.weight_copy("first", at).start()
        self.weight_copy("second", at).start()
        self.weight_copy("over", at).wait_send()
        if at + AHEAD < PIECES:
            self.weight_copy("over", at + AHEAD).start()

    def relay_on(self, at):
        self.weight_copy("first", at, True).wait_recv()
        self.weight_copy("third", at).start()

    def landed(self, at):
        self.weight_copy("second", at, True).wait_recv()
        self.weight_copy("third", at, True).wait_recv()

    def onward(self, *steps):
        @pl.when(self.other)
        def forward():
            for step in steps:
                if step < PIECES:
                    self.relay(step)
                else:
                    self.relay_on(step - PIECES)

    def locals(self):
        r = self.r
        pairs = ((r.tokens, r.x), (r.wqk, r.sqk), (r.wv, r.sv), (r.wo, r.so), (r.wu, r.su), (r.wd, r.sd), (r.cotangent, r.cot))
        return [pltpu.make_async_copy(a, b, r.local_sem.at[i]) for i, (a, b) in enumerate(pairs)]

    def item_copies(self):
        r = self.r
        sems = (r.item_sem.at[0], r.item_sem.at[1])
        pairs = ((r.live, r.live), (r.tokens, r.x), (r.cotangent, r.cot))
        return [self.remote(a, b, sems, i, self.sister) for i, (a, b) in enumerate(pairs)]

    def bias_copies(self):
        r = self.r
        sems = (r.bias_sem.at[0], r.bias_sem.at[1])
        pairs = ((r.qk_bias, r.pqk), (r.halves, r.phalves), (r.taps, r.ptaps))
        return [self.remote(a, b, sems, i, self.cross) for i, (a, b) in enumerate(pairs)]

    def begin(self):
        r = self.r
        length = self.length
        r.halves[:, : self.width] = r.v_bias[...].reshape(1, self.width)
        r.halves[:, self.width :] = r.u_bias[...].reshape(1, self.units)

        @pl.when(self.own)
        def send():
            for copy in self.locals():
                copy.start()
            listed = r.masked[...].astype(f32)
            count = listed.shape[1]
            wide = jnp.broadcast_to(listed, (count, count))
            wide = jnp.where(iota((count, count), 0) == iota((count, count), 1), wide, 0.0)
            listed = jnp.sum(wide, axis=1, keepdims=True)
            places = iota((count, length), 1)
            hit = jnp.where(places.astype(f32) == listed, 1.0, 0.0)
            hit = jnp.max(hit, axis=0, keepdims=True)
            live = jnp.where(iota((1, length), 1) < r.lengths[0], 1.0 - hit, 0.0)
            r.live[...] = jnp.broadcast_to(live, (8, length))
            item = self.item_copies()
            item[0].start()
            item[1].start()
            item[2].start()
            r.pqk[...] = r.qk_bias[...]
            r.phalves[...] = r.halves[...]
            r.ptaps[...] = r.taps[...]
            for at in range(3):
                self.locals()[at].wait()

        @pl.when(self.other)
        def receive():
            for copy in self.bias_copies():
                copy.start()
            for at in range(AHEAD):
                self.weight_copy("over", at).start()
            self.relay(0)
            self.relay(1)
            self.relay_on(0)
            self.relay(2)
            self.relay_on(1)
            self.relay(3)
            self.relay_on(2)
            item = self.item_copies()
            item[0].wait_recv()
            item[1].wait_recv()
            for copy in self.bias_copies():
                copy.wait()
            self.landed(0)
            self.landed(1)
            self.relay(4)
            self.relay_on(3)
            self.landed(2)

    def arrive(self, local, ats, cotangent=False):
        @pl.when(self.own)
        def here():
            for at in local:
                self.locals()[at].wait()

        @pl.when(self.other)
        def there():
            for at in ats:
                self.landed(at)
            if cotangent:
                self.item_copies()[2].wait_recv()

    def drain(self):
        @pl.when(self.own)
        def here():
            for copy in self.item_copies():
                copy.wait_send()

        @pl.when(self.other)
        def there():
            for at in range(PIECES):
                for kind in ("first", "second", "third"):
                    self.weight_copy(kind, at).wait_send()


    def attend(self, q_ref, k_ref, v_ref):
        r = self.r
        width, length = self.width, self.length
        pairs = width // PAIR
        live = r.live[0:1, :]
        factor = live * HEAD_DIM ** (-0.25)
        plan = (
            (q_ref, r.sqk[0], r.pqk[0:1, :], factor),
            (k_ref, r.sqk[1], r.pqk[1:2, :], factor),
            (v_ref, r.sv[...], r.phalves[:, : self.width], live),
        )
        for at, (kept, weight, bias, scale) in enumerate(plan):
            rows = slice(at * width, (at + 1) * width)
            value = (dot(weight.T, r.x[...], NT) + column(bias)) * scale
            kept[...] = value
            r.qkv[rows, :] = value.astype(bf16)
        self.onward(5, PIECES + 4)
        seg = segments(length)
        counts = segment_counts(live, seg)
        diagonal = same_head()
        eye = identity()
        state = []
        for pair in range(pairs):
            rows = slice(pair * PAIR, (pair + 1) * PAIR)
            q = split(q_ref[rows, :])
            k = split(k_ref[rows, :])
            qm_turned = jnp.where(diagonal, (dot(q[0], seg) + dot(q[1], seg)) / counts, 0.0)
            km_turned = jnp.where(diagonal, (dot(k[0], seg) + dot(k[1], seg)) / counts, 0.0)
            qm = qm_turned.T
            km = km_turned.T
            qm_parts = split(qm)
            scores = dot3(split(km), q)
            weights = jnp.exp(scores - head_max(scores))
            r.first[rows, :] = (weights / head_sum(weights)).astype(bf16)
            third = softmax_lanes(dot3(qm_parts, k) - 10000.0 * (1.0 - live))
            r.third[rows, :] = third.astype(bf16)
            scores = dot3(qm_parts, split(km_turned))
            second = softmax_lanes(jnp.where(diagonal, scores, -1e30))
            carried = jnp.where(diagonal, dot3(split(third), split(v_ref[rows, :]), NT), 0.0)
            r.marks[0, pair] = qm
            r.marks[1, pair] = km
            r.marks[2, pair] = second
            r.marks[3, pair] = carried
            square_sum = head_sum(jnp.sum(second * second, axis=1, keepdims=True))
            state.append((split(second), second.T / square_sum))
            if pair == 1:
                self.onward(PIECES + 5)
            if pair == 2:
                self.onward(6)
        for step in range(NS_ITERS):
            following = []
            for pair in range(pairs):
                matrix, approx = state[pair]
                r.chain[step, 0, pair] = approx
                approx_parts = split(approx)
                product = dot3(matrix, approx_parts)
                r.chain[step, 1, pair] = product
                parts = split(product)
                inner = 15.0 * eye - dot3(parts, split(7.0 * eye - product))
                r.chain[step, 2, pair] = inner
                inner = 13.0 * eye - dot3(parts, split(inner))
                r.chain[step, 3, pair] = inner
                following.append((matrix, 0.25 * dot3(approx_parts, split(inner))))
            state = following
        self.onward(PIECES + 6, 7)
        for pair in range(pairs):
            rows = slice(pair * PAIR, (pair + 1) * PAIR)
            inverse = state[pair][1]
            mixed = dot3(split(inverse), split(r.marks[3, pair]))
            r.marks[4, pair] = inverse
            r.marks[5, pair] = mixed
            out = dot(mixed.T.astype(bf16), r.first[rows, :])
            v = split(v_ref[rows, :])
            smoothed = []
            for half in range(2):
                head_rows = slice(half * HEAD_DIM, (half + 1) * HEAD_DIM)
                band = split(band_matrix(r.ptaps, 2 * pair + half, False))
                high = windows(v[0][head_rows])
                smooth = dot(high, band[0]) + (
                    dot(high, band[1]) + dot(windows(v[1][head_rows]), band[0])
                )
                smoothed.append(blocks_back(smooth, HEAD_DIM))
            out = out + jnp.concatenate(smoothed, axis=0)
            r.attended[:, rows] = out.astype(bf16).T
            if pair == 1:
                self.onward(PIECES + 7)

    def attend_back(self, joined):
        r = self.r
        width, length = self.width, self.length
        pairs = width // PAIR
        live = r.live[0:1, :]
        factor = live * HEAD_DIM ** (-0.25)
        diagonal = same_head()
        flip = jnp.where(iota((128, 128), 0) + iota((128, 128), 1) == 127, 1.0, 0.0).astype(bf16)
        state = []
        for pair in range(pairs):
            rows = slice(pair * PAIR, (pair + 1) * PAIR)
            d_out = r.d_attended[rows, :]
            d_mixed = split(jnp.where(diagonal, dot(r.first[rows, :], d_out, NT), 0.0))
            d_inverse = dot3(d_mixed, split(r.marks[3, pair]), NT)
            d_carried = dot3(split(r.marks[4, pair]), d_mixed, TN)
            state.append((d_inverse, jnp.zeros((PAIR, PAIR), f32), d_carried))
            d_v = dot(d_carried.T.astype(bf16), r.third[rows, :])
            smoothed = []
            for half in range(2):
                head = 2 * pair + half
                head_rows = slice(half * HEAD_DIM, (half + 1) * HEAD_DIM)
                band = split(band_matrix(r.ptaps, head, True))
                around = windows(d_out[head_rows])
                smoothed.append(blocks_back(dot(around, band[0]) + dot(around, band[1]), HEAD_DIM))
                start = 2 * width + head * HEAD_DIM
                flipped = dot(blocks_down(d_out[head_rows]), flip).astype(bf16)
                products = dot(flipped, windows(r.qkv[start : start + HEAD_DIM, :]), TN)
                lined = pltpu.roll(products, 17, 1, stride=1, stride_axis=0)
                total = jnp.sum(lined, axis=0, keepdims=True)
                r.small[5:6, head * 128 : (head + 1) * 128] = total[:, 256:]
            d_v = (d_v + jnp.concatenate(smoothed, axis=0)) * live
            place = slice(2 * width + pair * PAIR, 2 * width + (pair + 1) * PAIR)
            joined[place, :] = d_v.astype(bf16)
            r.small[4:5, place] = row_sums(d_v)
        self.store(r.g_rest, slice(2 * width, 3 * width), dot(r.x[...].T, joined[2 * width :, :], NT))
        self.launch("g_rest", 2 * width, 3 * width)
        self.tick()
        for step in reversed(range(NS_ITERS)):
            following = []
            for pair in range(pairs):
                d_approx, d_matrix, d_carried = state[pair]
                approx = split(r.chain[step, 0, pair])
                product = r.chain[step, 1, pair]
                inner = split(7.0 * identity() - product)
                product = split(product)
                middle = split(r.chain[step, 2, pair])
                outer = split(r.chain[step, 3, pair])
                d_parts = split(0.25 * d_approx)
                d_outer = split(dot3(approx, d_parts, TN))
                d_next = dot3(d_parts, outer, NT)
                d_product = -dot3(d_outer, middle, NT)
                d_middle = split(-dot3(product, d_outer, TN))
                d_product = d_product - dot3(d_middle, inner, NT) + dot3(product, d_middle, TN)
                d_product = split(d_product)
                d_matrix = d_matrix + dot3(d_product, approx, NT)
                d_next = d_next + dot3(split(r.marks[2, pair]), d_product, TN)
                following.append((d_next, d_matrix, d_carried))
            state = following
            self.tick()
        seg_turned = segments_turned(length)
        counts = segment_counts(live, segments(length))
        for pair in range(pairs):
            rows = slice(pair * PAIR, (pair + 1) * PAIR)
            k_rows = slice(width + pair * PAIR, width + (pair + 1) * PAIR)
            v_rows = slice(2 * width + pair * PAIR, 2 * width + (pair + 1) * PAIR)
            d_approx, d_matrix, d_carried = state[pair]
            qm = r.marks[0, pair]
            km = r.marks[1, pair]
            second = r.marks[2, pair]
            square_sum = head_sum(jnp.sum(second * second, axis=1, keepdims=True))
            turned = d_approx.T
            along = head_sum(jnp.sum(turned * second, axis=1, keepdims=True))
            d_matrix = d_matrix + turned / square_sum
            d_matrix = d_matrix - second * (2.0 * along / (square_sum * square_sum))
            d_scores = second * (d_matrix - jnp.sum(d_matrix * second, axis=1, keepdims=True))
            d_scores = split(d_scores)
            d_out = r.d_attended[rows, :]
            first = r.first[rows, :].astype(f32)
            d_first = dot(r.marks[5, pair].astype(bf16), d_out)
            d_first = (first * (d_first - head_sum(d_first * first))).astype(bf16)
            third = r.third[rows, :]
            d_third = dot(d_carried.astype(bf16), r.qkv[v_rows, :])
            wide = third.astype(f32)
            d_third = wide * (d_third - jnp.sum(d_third * wide, axis=1, keepdims=True))
            d_third = d_third.astype(bf16)
            d_qm = dot3(d_scores, split(km))
            d_qm = d_qm + jnp.where(diagonal, dot(d_third, r.qkv[k_rows, :], NT), 0.0)
            d_km = dot3(d_scores, split(qm), TN)
            d_km = d_km + jnp.where(diagonal, dot(d_first, r.qkv[rows, :], NT), 0.0)
            d_qm = split(d_qm.T / counts)
            d_km = split(d_km.T / counts)
            d_q = dot(km.T.astype(bf16), d_first) + (dot(d_qm[0], seg_turned) + dot(d_qm[1], seg_turned))
            d_k = dot(qm.T.astype(bf16), d_third) + (dot(d_km[0], seg_turned) + dot(d_km[1], seg_turned))
            for at, (value, scale) in enumerate(((d_q, factor), (d_k, factor))):
                place = slice(at * width + pair * PAIR, at * width + (pair + 1) * PAIR)
                value = value * scale
                joined[place, :] = value.astype(bf16)
                r.small[4:5, place] = row_sums(value)
            self.tick()


    def exchange(self, stage, chunk):
        r = self.r
        at = stage % 2
        rows_at = self.length // CHUNKS
        rows = pl.ds(chunk * rows_at, rows_at)
        sems = (r.send_sem.at[stage], r.recv_sem.at[stage])
        return self.remote(r.mine.at[at, rows], r.theirs.at[at, rows], sems, chunk, self.sister)

    def chunk_rows(self, chunk):
        rows_at = self.length // CHUNKS
        start = chunk * rows_at
        if not isinstance(chunk, int):
            start = pl.multiple_of(start, rows_at)
        return pl.ds(start, rows_at)

    def together(self, stage, chunk):
        self.exchange(stage, chunk).wait()
        rows = self.chunk_rows(chunk)
        at = stage % 2
        return self.r.mine[at, rows, :].astype(f32) + self.r.theirs[at, rows, :].astype(f32)

    def offer(self, stage, chunk, value):
        self.r.mine[stage % 2, self.chunk_rows(chunk), :] = value.astype(bf16)
        self.exchange(stage, chunk).start()

    def feed(self, low_ref, active_ref, slope_ref, d_low_ref, scale_ref):
        r = self.r
        block = 256
        units, width = self.units, self.width
        wide = units // 2
        out_bias, first_gain, first_shift, down_bias, second_gain, second_shift = (
            ref[...].reshape(1, self.model)
            for ref in (
                r.out_bias,
                r.first_gain,
                r.first_shift,
                r.down_bias,
                r.second_gain,
                r.second_shift,
            )
        )
        r.small[...] = jnp.zeros_like(r.small)

        def add_row(at, value):
            columns = slice((at % 2) * self.model, (at % 2 + 1) * self.model)
            r.small[at // 2 : at // 2 + 1, columns] += jnp.sum(value, axis=0, keepdims=True)

        self.arrive([3], [3])

        @pl.loop(0, CHUNKS)
        def project(chunk):
            self.offer(0, chunk, dot(r.attended[self.chunk_rows(chunk), :], r.so[...]))

        self.arrive([4], [4, 5])

        def raise_rows(chunk):
            rows = self.chunk_rows(chunk)
            summed = self.together(0, chunk) + out_bias + r.x[rows, :].astype(f32)
            normal, scale = normalize(summed)
            r.normal[rows, :] = normal
            scale_ref[rows, :] = scale
            low = (normal * first_gain + first_shift).astype(bf16)
            low_ref[rows, :] = low
            for at in range(0, units, block):
                columns = slice(at, at + block)
                raised = dot(low, r.su[:, columns]) + r.phalves[:, width + at : width + at + block]
                bell = 0.5 + 0.5 * lax.erf(raised * 0.7071067811865476)
                active_ref[rows, columns] = (raised * bell).astype(bf16)
                density = jnp.exp(-0.5 * raised * raised) * 0.3989422804014327
                slope_ref[rows, columns] = (bell + raised * density).astype(bf16)

        pl.loop(0, CHUNKS)(raise_rows)
        self.arrive([5], [6, 7])

        @pl.loop(0, CHUNKS)
        def lower(chunk):
            self.offer(1, chunk, dot(active_ref[self.chunk_rows(chunk), :], r.sd[...]))

        self.arrive([6], [], True)

        @pl.loop(0, CHUNKS)
        def turn(chunk):
            rows = self.chunk_rows(chunk)
            hidden = r.normal[rows, :] * first_gain + first_shift
            result = self.together(1, chunk) + down_bias + hidden
            normal, scale = normalize(result)
            r.out[rows, :] = (normal * second_gain + second_shift).astype(bf16)
            cotangent = r.cot[rows, :].astype(f32)
            d_result = normalize_back(cotangent * second_gain, normal, scale)
            add_row(4, cotangent * normal)
            add_row(5, cotangent)
            add_row(3, d_result)
            d_low_ref[rows, :] = d_result.astype(bf16)

        for chunk in range(CHUNKS):
            self.deliver(r.out, r.output, 0, chunk)
        turned = d_low_ref[...].T
        for at in range(0, units, wide):
            columns = slice(at, at + wide)
            self.store(r.g_down, columns, dot(turned, active_ref[:, columns]))
            self.launch("g_down", at, at + wide)

        def descend(chunk):
            rows = self.chunk_rows(chunk)
            d_low = d_low_ref[rows, :]
            for at in range(0, units, block):
                columns = slice(at, at + block)
                d_raised = dot(d_low, r.sd[columns, :], NT) * slope_ref[rows, columns].astype(f32)
                r.small[3:4, columns] += jnp.sum(d_raised, axis=0, keepdims=True)
                slope_ref[rows, columns] = d_raised.astype(bf16)
            self.offer(2, chunk, dot(slope_ref[rows, :], r.su[...], NT))

        pl.loop(0, CHUNKS // 2)(descend)
        self.tick()
        pl.loop(CHUNKS // 2, CHUNKS)(descend)
        self.tick()
        turned = low_ref[...].T
        for at in range(0, units, wide):
            columns = slice(at, at + wide)
            self.store(r.g_up, columns, dot(turned, slope_ref[:, columns]))
            self.launch("g_up", at, at + wide)
        self.tick()

        @pl.loop(0, CHUNKS)
        def back(chunk):
            rows = self.chunk_rows(chunk)
            d_hidden = d_low_ref[rows, :].astype(f32) + self.together(2, chunk)
            normal = r.normal[rows, :]
            add_row(1, d_hidden * normal)
            add_row(2, d_hidden)
            d_summed = normalize_back(d_hidden * first_gain, normal, scale_ref[rows, :])
            add_row(0, d_summed)
            r.normal[rows, :] = d_summed
            d_low_ref[rows, :] = d_summed.astype(bf16)

        r.d_attended[...] = dot(r.so[...], d_low_ref[...], NT).astype(bf16)
        turned = d_low_ref[...].T
        self.store(r.g_rest, slice(3 * width, 4 * width), dot(turned, r.attended[...]))
        self.launch("g_rest", 3 * width, 4 * width)
        self.tick()

    def store(self, ref, columns, value):
        value = value.astype(bf16)
        if self.parts:
            value = value.reshape(ref.shape[:-1] + (value.shape[1],))
            ref[:, :, :, :, :, columns] = value
        else:
            ref[:, columns] = value

    def deliver(self, source, target, at, chunk):
        r = self.r
        rows = self.chunk_rows(chunk)
        local, away = self.deliveries(source, target, at, chunk)

        @pl.when(self.own)
        def here():
            local.start()
            if chunk < CHUNKS // 2:
                away.start()

        if chunk >= CHUNKS // 2:

            @pl.when(self.other)
            def there():
                away.start()

    def deliveries(self, source, target, at, chunk):
        r = self.r
        rows = self.chunk_rows(chunk)
        local = pltpu.make_async_copy(source.at[rows], target.at[rows], r.home_sem.at[at, chunk])
        device = self.beyond if chunk < CHUNKS // 2 else self.cross
        sems = (r.away_sem.at[2 * at], r.away_sem.at[2 * at + 1])
        return local, self.remote(source.at[rows], target.at[rows], sems, chunk, device)

    def delivered(self, source, target, at):
        for chunk in range(CHUNKS):
            local, away = self.deliveries(source, target, at, chunk)

            @pl.when(self.own)
            def here():
                local.wait()
                if chunk < CHUNKS // 2:
                    away.wait_send()

            @pl.when(self.other)
            def there():
                away.wait_recv()
                if chunk >= CHUNKS // 2:
                    away.wait_send()


    def part_copy(self, part, level):
        name, start, count, order = self.parts[part]
        ref = getattr(self.r, name)
        bit = order[level]
        index = []
        for b in reversed(range(self.bits + 1)):
            if b in order[:level]:
                index.append(self.place[b])
            else:
                index.append(1 - self.place[b] if b == bit else slice(None))
        source = ref.at[tuple(index) + (slice(None), slice(start, start + count))]
        landing = self.r.landings[part * (self.bits + 1) + level]
        sems = (self.r.part_sem.at[0, part], self.r.part_sem.at[1, part])
        return self.remote(source, landing, sems, level, self.partner(bit))

    def part_finish(self, part, level):
        name, start, count, order = self.parts[part]
        ref = getattr(self.r, name)
        self.part_copy(part, level).wait()
        index = []
        for b in reversed(range(self.bits + 1)):
            index.append(self.place[b] if b in order[: level + 1] else slice(None))
        index = tuple(index) + (slice(None), slice(start, start + count))
        landing = self.r.landings[part * (self.bits + 1) + level]
        total = ref[index].astype(f32) + landing[...].astype(f32)
        if level < self.bits:
            ref[index] = total.astype(bf16)
        else:
            self.part_last(part, total)

    def part_swap(self, part):
        name, start, count, order = self.parts[part]
        ref = self.r.swap_out.at[part]
        sems = (self.r.swap_sem.at[0], self.r.swap_sem.at[1])
        return self.remote(ref, self.r.swap_in.at[part], sems, part, self.cross)

    def part_target(self, part):
        name, start, count, order = self.parts[part]
        return getattr(self.r, "t" + name[1:]), slice(start, start + count)

    def part_last(self, part, total):
        target, columns = self.part_target(part)

        @pl.when(self.own)
        def here():
            target[:, columns] = total

        @pl.when(self.other)
        def there():
            self.r.swap_out[part] = total.astype(bf16)
            self.part_swap(part).start()

    def launch(self, wanted, first, last):
        for part, (name, start, count, order) in enumerate(self.parts):
            if name == wanted and first <= start < last:
                self.part_copy(part, 0).start()
                self.levels[part] = 0

    def advance(self, part):
        level = self.levels[part]
        if level is None or level > self.bits:
            return
        self.part_finish(part, level)
        if level < self.bits:
            self.part_copy(part, level + 1).start()
        self.levels[part] = level + 1

    def tick(self):
        if self.parts and self.agenda:
            for part in self.agenda.pop(0):
                self.advance(part)

    def small_copy(self, level):
        r = self.r
        source = r.small if level == 0 else r.small_sum.at[level - 1]
        sems = (r.small_sem.at[0], r.small_sem.at[1])
        return self.remote(source, r.small_land.at[level], sems, level, self.partner(level))

    def small_advance(self):
        r = self.r
        level = self.small_level
        self.small_level += 1
        self.small_copy(level).wait()
        own = r.small[...] if level == 0 else r.small_sum[level - 1]
        r.small_sum[level] = own + r.small_land[level]
        if level < self.bits:
            self.small_copy(level + 1).start()

    def small_swap(self):
        r = self.r
        sems = (r.small_sem.at[0], r.small_sem.at[1])
        return self.remote(r.small_sum.at[self.bits], r.small_sister, sems, self.bits + 1, self.sister)

    def small_done(self):
        r = self.r
        total = r.small_sum[self.bits]
        r.tsmall[0:3, :] = total[0:3]

        @pl.when(self.own)
        def here():
            self.small_swap().start()
            r.tsmall[3:8, :] = total[3:8]
            self.small_swap().wait_send()

        @pl.when(self.other)
        def there():
            self.small_swap().wait_recv()
            r.tsmall[3:8, :] = r.small_sister[3:8, :]

    def finish(self, joined):
        r = self.r
        width, model, length = self.width, self.model, self.length
        bits = self.bits
        if self.parts:
            self.small_copy(0).start()
        turned = r.x[...].T
        for at in range(2):
            rows = slice(at * width, (at + 1) * width)
            self.store(r.g_rest, rows, dot(turned, joined[rows, :], NT))
            self.launch("g_rest", at * width, (at + 1) * width)
        rows_at = length // CHUNKS
        for chunk in range(CHUNKS):
            columns = slice(chunk * rows_at, (chunk + 1) * rows_at)
            back = dot(r.sqk[0], joined[0:width, columns])
            back = back + dot(r.sqk[1], joined[width : 2 * width, columns])
            back = back + dot(r.sv[...], joined[2 * width :, columns])
            self.offer(3, chunk, back.astype(bf16).T)
        for chunk in range(CHUNKS):
            rows = self.chunk_rows(chunk)
            r.grad[rows, :] = (r.normal[rows, :] + self.together(3, chunk)).astype(bf16)
            self.deliver(r.grad, r.tokens_grad, 1, chunk)
        if self.parts:
            for at, part in enumerate(FINAL):
                self.advance(part)
                if at % 6 == 5 and self.small_level <= bits:
                    self.small_advance()
            while self.small_level <= bits:
                self.small_advance()
            for level in range(bits + 1):
                for part in range(len(self.parts)):
                    if self.levels[part] <= level:
                        self.advance(part)
            self.small_done()
        else:
            r.tsmall[...] = r.small[...]
        self.delivered(r.out, r.output, 0)
        self.delivered(r.grad, r.tokens_grad, 1)
        for part in range(len(self.parts)):
            target, columns = self.part_target(part)

            @pl.when(self.other)
            def there():
                self.part_swap(part).wait()
                target[:, columns] = r.swap_in[part].astype(f32)

        self.drain()


def layer_kernel(names, bits, parts, agenda, sizes, *refs):
    found = dict(zip(names, refs))
    found["landings"] = refs[len(names) :]
    layer = Layer(found, bits, parts, sizes)
    layer.agenda = list(agenda)
    length, model, width, units, heads = sizes
    layer.greet()
    layer.begin()
    pl.run_scoped(layer.attend, *[pltpu.VMEM((width, length), f32)] * 3)
    pl.run_scoped(
        layer.feed,
        pltpu.VMEM((length, model), bf16),
        pltpu.VMEM((length, units), bf16),
        pltpu.VMEM((length, units), bf16),
        pltpu.VMEM((length, model), bf16),
        pltpu.VMEM((length, 1), f32),
    )

    def back(joined):
        layer.attend_back(joined)
        layer.finish(joined)

    pl.run_scoped(back, pltpu.VMEM((3 * width, length), bf16))


ORDERS = {
    3: (
        (0, 2, 1, 3),
        (1, 2, 3, 0),
        (2, 1, 0, 3),
        (2, 1, 0, 3),
        (0, 2, 1, 3),
        (2, 3, 1, 0),
        (1, 2, 3, 0),
        (1, 2, 0, 3),
        (0, 1, 2, 3),
        (1, 2, 3, 0),
        (2, 1, 3, 0),
        (0, 1, 2, 3),
    ),
}
AGENDA = (
    [],
    [],
    [],
    [1],
    [2, 3],
    [0],
    [],
    [],
    [1],
    [6, 7],
    [5],
    [2, 3, 4],
    [11],
    [0, 1],
)
FINAL = (2, 3, 11, 1, 0, 6, 10, 7, 5, 4, 9, 11, 8, 2, 3, 7, 0, 5, 4, 6, 10, 11, 7, 5, 8, 9, 4, 6, 10, 8, 9, 10, 8, 9)


def body(
    tokens,
    cotangent,
    lengths,
    masked,
    qk_weight,
    qk_bias,
    value_weight,
    value_bias,
    conv_taps,
    out_weight,
    out_bias,
    first_gain,
    first_shift,
    up_weight,
    up_bias,
    down_weight,
    down_bias,
    second_gain,
    second_shift,
):
    chips = lax.axis_size("chip")
    length, model = tokens.shape
    width = value_weight.shape[1]
    units = up_weight.shape[1]
    heads = conv_taps.shape[0]
    pairs = width // PAIR
    bits = chips.bit_length() - 1
    share = model // (2 * chips)
    fused = bits in ORDERS and share % 16 == 0
    parts = []
    if fused:
        count = units // 4
        for at, order in enumerate(ORDERS[bits]):
            parts.append((("g_down", "g_up", "g_rest")[at // 4], at % 4 * count, count, order))
    shape = jax.ShapeDtypeStruct
    hbm = pl.BlockSpec(memory_space=pl.ANY)
    inputs = [
        ("tokens", tokens, hbm),
        ("cotangent", cotangent, hbm),
        ("wqk", jnp.transpose(qk_weight, (1, 0, 2)), hbm),
        ("wv", value_weight, hbm),
        ("wo", out_weight, hbm),
        ("wu", up_weight, hbm),
        ("wd", down_weight, hbm),
        ("lengths", lengths, SMEM),
        ("masked", masked, VMEM),
        ("qk_bias", qk_bias, VMEM),
        ("taps", conv_taps, VMEM),
        ("v_bias", value_bias, VMEM),
        ("u_bias", up_bias, VMEM),
        ("out_bias", out_bias, VMEM),
        ("first_gain", first_gain, VMEM),
        ("first_shift", first_shift, VMEM),
        ("down_bias", down_bias, VMEM),
        ("second_gain", second_gain, VMEM),
        ("second_shift", second_shift, VMEM),
    ]
    outputs = [("output", shape((length, model), bf16), hbm), ("tokens_grad", shape((length, model), bf16), hbm)]
    outputs.append(("tsmall", shape((8, units), f32), VMEM))
    scratch = []
    for name in ("down", "up", "rest"):
        if fused:
            outputs.append(("t_" + name, shape((share, units), f32), VMEM))
            scratch.append(("g_" + name, pltpu.VMEM((2,) * (bits + 1) + (share, units), bf16)))
        else:
            outputs.append(("g_" + name, shape((model, units), bf16), VMEM))
    dma = pltpu.SemaphoreType.DMA
    scratch += [
        ("sqk", pltpu.VMEM((2, model, width), bf16)),
        ("sv", pltpu.VMEM((model, width), bf16)),
        ("so", pltpu.VMEM((width, model), bf16)),
        ("su", pltpu.VMEM((model, units), bf16)),
        ("sd", pltpu.VMEM((units, model), bf16)),
        ("x", pltpu.VMEM((length, model), bf16)),
        ("cot", pltpu.VMEM((length, model), bf16)),
        ("live", pltpu.VMEM((8, length), f32)),
        ("pqk", pltpu.VMEM((2, width), f32)),
        ("halves", pltpu.VMEM((1, width + units), f32)),
        ("phalves", pltpu.VMEM((1, width + units), f32)),
        ("ptaps", pltpu.VMEM((heads, KERNEL), f32)),
        ("qkv", pltpu.VMEM((3 * width, length), bf16)),
        ("first", pltpu.VMEM((width, length), bf16)),
        ("third", pltpu.VMEM((width, length), bf16)),
        ("attended", pltpu.VMEM((length, width), bf16)),
        ("marks", pltpu.VMEM((6, pairs, PAIR, PAIR), f32)),
        ("chain", pltpu.VMEM((NS_ITERS, 4, pairs, PAIR, PAIR), f32)),
        ("mine", pltpu.VMEM((2, length, model), bf16)),
        ("theirs", pltpu.VMEM((2, length, model), bf16)),
        ("normal", pltpu.VMEM((length, model), f32)),
        ("d_attended", pltpu.VMEM((width, length), bf16)),
        ("out", pltpu.VMEM((length, model), bf16)),
        ("grad", pltpu.VMEM((length, model), bf16)),
        ("small", pltpu.VMEM((8, units), f32)),
        ("weight_sem", dma((8, PIECES))),
        ("local_sem", dma((7,))),
        ("item_sem", dma((2, 3))),
        ("bias_sem", dma((2, 3))),
        ("send_sem", dma((4, CHUNKS))),
        ("recv_sem", dma((4, CHUNKS))),
        ("home_sem", dma((2, CHUNKS))),
        ("away_sem", dma((4, CHUNKS))),
    ]
    landings = []
    if fused:
        levels = bits + 1
        scratch += [
            ("small_land", pltpu.VMEM((levels, 8, units), f32)),
            ("small_sum", pltpu.VMEM((levels, 8, units), f32)),
            ("small_sister", pltpu.VMEM((8, units), f32)),
            ("small_sem", dma((2, levels + 1))),
            ("part_sem", dma((2, len(parts), levels))),
            ("swap_sem", dma((2, len(parts)))),
            ("swap_out", pltpu.VMEM((len(parts), share, parts[0][2]), bf16)),
            ("swap_in", pltpu.VMEM((len(parts), share, parts[0][2]), bf16)),
        ]
        for name, start, count, order in parts:
            landings += [pltpu.VMEM((2,) * (bits - level) + (share, count), bf16) for level in range(levels)]
    names = [n for n, *_ in inputs + outputs + scratch]
    got = pl.pallas_call(
        functools.partial(
            layer_kernel, names, bits, parts, AGENDA, (length, model, width, units, heads)
        ),
        out_shape=[kind for _, kind, _ in outputs],
        in_specs=[spec for *_, spec in inputs],
        out_specs=[spec for *_, spec in outputs],
        scratch_shapes=[kind for _, kind in scratch] + landings,
        compiler_params=pltpu.CompilerParams(
            collective_id=0, has_side_effects=True, vmem_limit_bytes=VMEM_LIMIT
        ),
        name="layer",
    )(*[value for _, value, _ in inputs])
    output, tokens_grad, small, down, up, rest = got
    if not fused:
        swap = lambda v: lax.ppermute(v, ("core", "mp"), [(0, 0), (1, 2), (2, 1), (3, 3)])
        gather = lambda g: swap(
            lax.psum_scatter(g, ("chip", "mp"), scatter_dimension=0, tiled=True).astype(f32)
        )
        down, up, rest = gather(down), gather(up), gather(rest)
        small = lax.psum(small, ("chip", "mp"))
        small = jnp.concatenate([small[:3], swap(small[3:])], axis=0)
    return arrange(output, tokens_grad, small, up, down, rest, heads)


def arrange_kernel(
    output,
    tokens_grad,
    small,
    up,
    down,
    rest,
    output_to,
    tokens_grad_to,
    qk_to,
    qk_bias_to,
    v_to,
    v_bias_to,
    taps_to,
    out_to,
    out_bias_to,
    first_gain_to,
    first_shift_to,
    up_to,
    up_bias_to,
    down_to,
    down_bias_to,
    second_gain_to,
    second_shift_to,
    output_at,
    tokens_grad_at,
    up_at,
    down_at,
    rest_at,
    small_at,
    sems,
):
    pairs = (
        (small, small_at),
        (rest, rest_at),
        (output, output_at),
        (tokens_grad, tokens_grad_at),
        (up, up_at),
        (down, down_at),
    )
    coming = [pltpu.make_async_copy(a, b, sems.at[0, i]) for i, (a, b) in enumerate(pairs)]
    pairs = (
        (output_at, output_to),
        (tokens_grad_at, tokens_grad_to),
        (up_at, up_to),
        (down_at, down_to),
    )
    going = [pltpu.make_async_copy(a, b, sems.at[1, i]) for i, (a, b) in enumerate(pairs)]
    for copy in coming:
        copy.start()
    for copy in coming[:2]:
        copy.wait()
    small, rest = small_at, rest_at
    width = v_to.shape[1]
    model = out_bias_to.shape[0]
    units = up_bias_to.shape[0]
    for at in range(2):
        columns = slice(at * width, (at + 1) * width)
        qk_to[:, at, :] = rest[:, columns]
        qk_bias_to[at : at + 1, :] = small[4:5, columns]
    v_to[...] = rest[:, 2 * width : 3 * width]
    out_to[...] = rest[:, 3 * width :]
    v_bias_to[...] = small[4:5, 2 * width : 3 * width].reshape(width)
    up_bias_to[...] = small[3:4, :].reshape(units)
    for head in range(taps_to.shape[0]):
        taps_to[head : head + 1, :] = small[5:6, head * 128 : head * 128 + KERNEL]
    common = (out_bias_to, first_gain_to, first_shift_to, down_bias_to, second_gain_to, second_shift_to)
    for at, ref in enumerate(common):
        columns = slice(at % 2 * model, (at % 2 + 1) * model)
        ref[...] = small[at // 2 : at // 2 + 1, columns].reshape(model)
    for here, there in zip(coming[2:], going):
        here.wait()
        there.start()
    for copy in going:
        copy.wait()


def arrange(output, tokens_grad, small, up, down, rest, heads):
    share, units = up.shape
    width = rest.shape[1] // 4
    model = output.shape[1]
    hbm = pl.BlockSpec(memory_space=pl.ANY)
    kinds = [
        (output.shape, bf16),
        (output.shape, bf16),
        ((share, 2, width), f32),
        ((2, width), f32),
        ((share, width), f32),
        ((width,), f32),
        ((heads, KERNEL), f32),
        ((share, width), f32),
        ((model,), f32),
        ((model,), f32),
        ((model,), f32),
        ((share, units), f32),
        ((units,), f32),
        ((share, units), f32),
        ((model,), f32),
        ((model,), f32),
        ((model,), f32),
    ]
    got = pl.pallas_call(
        arrange_kernel,
        out_shape=[jax.ShapeDtypeStruct(a, b) for a, b in kinds],
        in_specs=[hbm] * 6,
        out_specs=[hbm if at in (0, 1, 11, 13) else VMEM for at in range(len(kinds))],
        scratch_shapes=[
            pltpu.VMEM(output.shape, bf16),
            pltpu.VMEM(output.shape, bf16),
            pltpu.VMEM(up.shape, f32),
            pltpu.VMEM(up.shape, f32),
            pltpu.VMEM(up.shape, f32),
            pltpu.VMEM(small.shape, f32),
            pltpu.SemaphoreType.DMA((2, 6)),
        ],
        compiler_params=pltpu.CompilerParams(vmem_limit_bytes=VMEM_LIMIT),
        name="arrange",
    )(output, tokens_grad, small, up, down, rest)
    got = list(got)
    got[7] = got[7].T
    got[13] = got[13].T
    return tuple(got)


def solution(mesh):
    dp = ("chip", "core")
    placed = (
        P(dp, None),
        P(dp, None),
        P(dp),
        P(dp, None),
        P(None, None, "mp"),
        P(None, "mp"),
        P(None, "mp"),
        P("mp"),
        P("mp", None),
        P("mp", None),
        P(),
        P(),
        P(),
        P(None, "mp"),
        P("mp"),
        P("mp", None),
        P(),
        P(),
        P(),
    )
    chips = mesh.shape["dp"] // 2
    fine = Mesh(mesh.devices.reshape(chips, 2, mesh.shape["mp"]), ("chip", "core", "mp"))
    return jax.shard_map(
        body,
        mesh=fine,
        in_specs=placed,
        out_specs=(
            P(dp, None),
            P(dp, None),
            P(dp, None, "mp"),
            P(None, "mp"),
            P(dp, "mp"),
            P("mp"),
            P("mp", None),
            P("mp", dp),
            P(),
            P(),
            P(),
            P(dp, "mp"),
            P("mp"),
            P("mp", dp),
            P(),
            P(),
            P(),
        ),
        check_vma=False,
    )
```

```python
import functools
import types

import jax
import jax.numpy as jnp
from jax import lax
from jax.experimental import pallas as pl
from jax.experimental.pallas import tpu as pltpu
from jax.sharding import Mesh
from jax.sharding import PartitionSpec as P

HEAD_DIM = 64
LANDMARKS = 64
NS_ITERS = 6
KERNEL = 33
EDGE = 112
BAND = 160
PAIR = 2 * HEAD_DIM
CHUNKS = 4
PIECES = 8
AHEAD = 2
VMEM_LIMIT = 64 << 20

f32 = jnp.float32
bf16 = jnp.bfloat16
NN = (((1,), (0,)), ((), ()))
NT = (((1,), (1,)), ((), ()))
TN = (((0,), (0,)), ((), ()))
MESH = pl.DeviceIdType.MESH
VMEM = pl.BlockSpec(memory_space=pltpu.VMEM)
SMEM = pl.BlockSpec(memory_space=pltpu.SMEM)


def dot(a, b, dims=NN):
    return lax.dot_general(a, b, dims, preferred_element_type=f32)


def split(value):
    high = value.astype(bf16)
    return high, (value - high.astype(f32)).astype(bf16)


def dot3(a, b, dims=NN):
    return dot(a[0], b[0], dims) + (dot(a[0], b[1], dims) + dot(a[1], b[0], dims))


def iota(shape, axis):
    return lax.broadcasted_iota(jnp.int32, shape, axis)


def same_head():
    return iota((PAIR, PAIR), 0) // HEAD_DIM == iota((PAIR, PAIR), 1) // HEAD_DIM


def identity():
    return jnp.where(iota((PAIR, PAIR), 0) == iota((PAIR, PAIR), 1), 1.0, 0.0).astype(f32)


def segments(length):
    spread = length // LANDMARKS
    hit = iota((length, PAIR), 0) // spread == iota((length, PAIR), 1) % LANDMARKS
    return jnp.where(hit, 1.0, 0.0).astype(bf16)


def segments_turned(length):
    spread = length // LANDMARKS
    hit = iota((PAIR, length), 1) // spread == iota((PAIR, length), 0) % LANDMARKS
    return jnp.where(hit, 1.0, 0.0).astype(bf16)


def segment_counts(live, seg):
    rows = jnp.broadcast_to(live, (8, live.shape[1])).astype(bf16)
    return jnp.maximum(dot(rows, seg)[0:1], 1.0)


def head_sum(value):
    heads = value.shape[0] // HEAD_DIM
    cut = value.reshape(heads, HEAD_DIM, value.shape[1])
    total = jnp.sum(cut, axis=1, keepdims=True)
    return jnp.broadcast_to(total, cut.shape).reshape(value.shape)


def head_max(value):
    heads = value.shape[0] // HEAD_DIM
    cut = value.reshape(heads, HEAD_DIM, value.shape[1])
    top = jnp.max(cut, axis=1, keepdims=True)
    return jnp.broadcast_to(top, cut.shape).reshape(value.shape)


def softmax_lanes(scores):
    weights = jnp.exp(scores - jnp.max(scores, axis=1, keepdims=True))
    return weights / jnp.sum(weights, axis=1, keepdims=True)


def band_matrix(taps_ref, head, turned):
    gap = iota((BAND, 128), 0) - iota((BAND, 128), 1)
    total = jnp.zeros((BAND, 128), f32)
    for tap in range(KERNEL):
        source = KERNEL - 1 - tap if turned else tap
        weight = taps_ref[head : head + 1, source : source + 1]
        total = jnp.where(gap == tap, weight, total)
    zeros = jnp.zeros((EDGE, 128), f32)
    return jnp.concatenate([zeros, total, zeros], axis=0)


def windows(rows):
    zeros = jnp.zeros((rows.shape[0], 128), rows.dtype)
    padded = jnp.concatenate([zeros, rows, zeros], axis=1)
    blocks = rows.shape[1] // 128
    return jnp.concatenate([padded[:, b * 128 : b * 128 + 384] for b in range(blocks)], axis=0)


def blocks_down(rows):
    blocks = rows.shape[1] // 128
    return jnp.concatenate([rows[:, b * 128 : (b + 1) * 128] for b in range(blocks)], axis=0)


def blocks_back(stacked, height):
    blocks = stacked.shape[0] // height
    return jnp.concatenate([stacked[b * height : (b + 1) * height] for b in range(blocks)], axis=1)


def normalize(value):
    middle = jnp.mean(value, axis=1, keepdims=True)
    centered = value - middle
    spread = jnp.mean(centered * centered, axis=1, keepdims=True)
    scale = lax.rsqrt(spread + 1e-05)
    return centered * scale, scale


def normalize_back(grad, normal, scale):
    middle = jnp.mean(grad, axis=1, keepdims=True)
    along = jnp.mean(grad * normal, axis=1, keepdims=True)
    return scale * (grad - middle - normal * along)


def column(row):
    return jnp.broadcast_to(row, (8, row.shape[1])).T[:, 0:1]


def row_sums(value):
    parts = split(value)
    ones = jnp.ones((8, value.shape[1]), bf16)
    return (dot(ones, parts[0], NT) + dot(ones, parts[1], NT))[0:1]


class Layer:
    def __init__(self, refs, bits, parts, sizes):
        self.r = types.SimpleNamespace(**refs)
        self.bits = bits
        self.parts = parts
        self.length, self.model, self.width, self.units, self.heads = sizes
        self.chip = lax.axis_index("chip")
        self.core = lax.axis_index("core")
        self.half = lax.axis_index("mp")
        self.own = self.core == self.half
        self.other = self.core != self.half
        self.sister = (self.chip, 1 - self.core, self.half)
        self.beyond = (self.chip, self.core, 1 - self.half)
        self.cross = (self.chip, 1 - self.core, 1 - self.half)
        self.place = [self.half] + [lax.rem(lax.div(self.chip, 2**i), 2) for i in range(bits)]
        self.levels = [None] * len(parts)
        self.small_level = 0

    def partner(self, bit):
        if bit == 0:
            return self.beyond
        step = 2 ** (bit - 1)
        return (self.chip + step * (1 - 2 * self.place[bit]), self.core, self.half)

    def greet(self):
        known = [self.sister, self.beyond, self.cross]
        known += [self.partner(bit) for bit in range(1, (self.bits if self.parts else 2) + 1)]
        barrier = pltpu.get_barrier_semaphore()
        for device in known:
            pl.semaphore_signal(barrier, inc=1, device_id=device, device_id_type=MESH)
        pl.semaphore_wait(barrier, len(known))

    def remote(self, source, target, sems, at, device):
        return pltpu.make_async_remote_copy(
            src_ref=source,
            dst_ref=target,
            send_sem=sems[0].at[at],
            recv_sem=sems[1].at[at],
            device_id=device,
            device_id_type=MESH,
        )


    def pieces(self):
        r = self.r
        found = []
        for a, b in ((r.wqk.at[0], r.sqk.at[0]), (r.wqk.at[1], r.sqk.at[1]), (r.wv, r.sv), (r.wo, r.so)):
            found.append((a, b, 0, 1))
        for a, b in ((r.wu, r.su), (r.wd, r.sd)):
            found += [(a, b, sub, 2) for sub in range(2)]
        return found

    def quarter(self, flips):
        low, high = self.place[1], self.place[2]
        if 0 in flips:
            low = 1 - low
        if 1 in flips:
            high = 1 - high
        return low + 2 * high

    def weight_copy(self, kind, at, arriving=False):
        source, target, sub, subs = self.pieces()[at]
        first, second = (0, 1) if at % 2 else (1, 0)
        if kind == "over":
            flips, device, lane = (), self.cross, 0
        elif kind == "first":
            flips, device, lane = (), self.partner(first + 1), 1
            if arriving:
                flips = (first,)
        elif kind == "second":
            flips, device, lane = (), self.partner(second + 1), 2
            if arriving:
                flips = (second,)
        else:
            flips, device, lane = (first,), self.partner(second + 1), 3
            if arriving:
                flips = (first, second)
        rows = source.shape[0] // 4
        step = rows // subs
        start = self.quarter(flips) * rows + sub * step
        place = pl.ds(pl.multiple_of(start, 16), step)
        sems = (self.r.weight_sem.at[2 * lane], self.r.weight_sem.at[2 * lane + 1])
        begin = source if kind == "over" else target
        return self.remote(begin.at[place], target.at[place], sems, at, device)

    def relay(self, at):
        self.weight_copy("over", at, True).wait_recv()
        self.weight_copy("first", at).start()
        self.weight_copy("second", at).start()
        self.weight_copy("over", at).wait_send()
        if at + AHEAD < PIECES:
            self.weight_copy("over", at + AHEAD).start()

    def relay_on(self, at):
        self.weight_copy("first", at, True).wait_recv()
        self.weight_copy("third", at).start()

    def landed(self, at):
        self.weight_copy("second", at, True).wait_recv()
        self.weight_copy("third", at, True).wait_recv()

    def onward(self, *steps):
        @pl.when(self.other)
        def forward():
            for step in steps:
                if step < PIECES:
                    self.relay(step)
                else:
                    self.relay_on(step - PIECES)

    def locals(self):
        r = self.r
        pairs = ((r.tokens, r.x), (r.wqk, r.sqk), (r.wv, r.sv), (r.wo, r.so), (r.wu, r.su), (r.wd, r.sd), (r.cotangent, r.cot))
        return [pltpu.make_async_copy(a, b, r.local_sem.at[i]) for i, (a, b) in enumerate(pairs)]

    def item_copies(self):
        r = self.r
        sems = (r.item_sem.at[0], r.item_sem.at[1])
        pairs = ((r.live, r.live), (r.tokens, r.x), (r.cotangent, r.cot))
        return [self.remote(a, b, sems, i, self.sister) for i, (a, b) in enumerate(pairs)]

    def bias_copies(self):
        r = self.r
        sems = (r.bias_sem.at[0], r.bias_sem.at[1])
        pairs = ((r.qk_bias, r.pqk), (r.halves, r.phalves), (r.taps, r.ptaps))
        return [self.remote(a, b, sems, i, self.cross) for i, (a, b) in enumerate(pairs)]

    def begin(self):
        r = self.r
        length = self.length
        r.halves[:, : self.width] = r.v_bias[...].reshape(1, self.width)
        r.halves[:, self.width :] = r.u_bias[...].reshape(1, self.units)

        @pl.when(self.own)
        def send():
            for copy in self.locals():
                copy.start()
            listed = r.masked[...].astype(f32)
            count = listed.shape[1]
            wide = jnp.broadcast_to(listed, (count, count))
            wide = jnp.where(iota((count, count), 0) == iota((count, count), 1), wide, 0.0)
            listed = jnp.sum(wide, axis=1, keepdims=True)
            places = iota((count, length), 1)
            hit = jnp.where(places.astype(f32) == listed, 1.0, 0.0)
            hit = jnp.max(hit, axis=0, keepdims=True)
            live = jnp.where(iota((1, length), 1) < r.lengths[0], 1.0 - hit, 0.0)
            r.live[...] = jnp.broadcast_to(live, (8, length))
            item = self.item_copies()
            item[0].start()
            item[1].start()
            item[2].start()
            r.pqk[...] = r.qk_bias[...]
            r.phalves[...] = r.halves[...]
            r.ptaps[...] = r.taps[...]
            for at in range(3):
                self.locals()[at].wait()

        @pl.when(self.other)
        def receive():
            for copy in self.bias_copies():
                copy.start()
            for at in range(AHEAD):
                self.weight_copy("over", at).start()
            self.relay(0)
            self.relay(1)
            self.relay_on(0)
            self.relay(2)
            self.relay_on(1)
            self.relay(3)
            self.relay_on(2)
            item = self.item_copies()
            item[0].wait_recv()
            item[1].wait_recv()
            for copy in self.bias_copies():
                copy.wait()
            self.landed(0)
            self.landed(1)
            self.relay(4)
            self.relay_on(3)
            self.landed(2)

    def arrive(self, local, ats, cotangent=False):
        @pl.when(self.own)
        def here():
            for at in local:
                self.locals()[at].wait()

        @pl.when(self.other)
        def there():
            for at in ats:
                self.landed(at)
            if cotangent:
                self.item_copies()[2].wait_recv()

    def drain(self):
        @pl.when(self.own)
        def here():
            for copy in self.item_copies():
                copy.wait_send()

        @pl.when(self.other)
        def there():
            for at in range(PIECES):
                for kind in ("first", "second", "third"):
                    self.weight_copy(kind, at).wait_send()


    def attend(self, q_ref, k_ref, v_ref):
        r = self.r
        width, length = self.width, self.length
        pairs = width // PAIR
        live = r.live[0:1, :]
        factor = live * HEAD_DIM ** (-0.25)
        plan = (
            (q_ref, r.sqk[0], r.pqk[0:1, :], factor),
            (k_ref, r.sqk[1], r.pqk[1:2, :], factor),
            (v_ref, r.sv[...], r.phalves[:, : self.width], live),
        )
        for at, (kept, weight, bias, scale) in enumerate(plan):
            rows = slice(at * width, (at + 1) * width)
            value = (dot(weight.T, r.x[...], NT) + column(bias)) * scale
            kept[...] = value
            r.qkv[rows, :] = value.astype(bf16)
        self.onward(5, PIECES + 4)
        seg = segments(length)
        counts = segment_counts(live, seg)
        diagonal = same_head()
        state = []
        for pair in range(pairs):
            rows = slice(pair * PAIR, (pair + 1) * PAIR)
            q = split(q_ref[rows, :])
            k = split(k_ref[rows, :])
            qm_turned = jnp.where(diagonal, (dot(q[0], seg) + dot(q[1], seg)) / counts, 0.0)
            km_turned = jnp.where(diagonal, (dot(k[0], seg) + dot(k[1], seg)) / counts, 0.0)
            qm = qm_turned.T
            km = km_turned.T
            qm_parts = split(qm)
            scores = dot3(split(km), q)
            weights = jnp.exp(scores - head_max(scores))
            r.first[rows, :] = (weights / head_sum(weights)).astype(bf16)
            third = softmax_lanes(dot3(qm_parts, k) - 10000.0 * (1.0 - live))
            r.third[rows, :] = third.astype(bf16)
            scores = dot3(qm_parts, split(km_turned))
            second = softmax_lanes(jnp.where(diagonal, scores, -1e30))
            carried = jnp.where(diagonal, dot3(split(third), split(v_ref[rows, :]), NT), 0.0)
            r.marks[0, pair] = qm
            r.marks[1, pair] = km
            r.marks[2, pair] = second
            r.marks[3, pair] = carried
            square_sum = head_sum(jnp.sum(second * second, axis=1, keepdims=True))
            state.append((split(second), second.T / square_sum))
            if pair == 2:
                self.onward(PIECES + 5, 6)
        for step in range(NS_ITERS):
            following = []
            for pair in range(pairs):
                matrix, approx = state[pair]
                r.chain[step, 0, pair] = approx
                approx_parts = split(approx)
                product = dot3(matrix, approx_parts)
                r.chain[step, 1, pair] = product
                parts = split(product)
                along = dot3(approx_parts, parts)
                r.chain[step, 2, pair] = along
                inner = 7.0 * product - dot3(parts, parts)
                r.chain[step, 3, pair] = inner
                approx = 3.25 * approx - 3.75 * along + 0.25 * dot3(split(along), split(inner))
                following.append((matrix, approx))
            state = following
        self.onward(7)
        for pair in range(pairs):
            rows = slice(pair * PAIR, (pair + 1) * PAIR)
            inverse = state[pair][1]
            mixed = dot3(split(inverse), split(r.marks[3, pair]))
            r.marks[4, pair] = inverse
            r.marks[5, pair] = mixed
            out = dot(mixed.T.astype(bf16), r.first[rows, :])
            v = split(v_ref[rows, :])
            smoothed = []
            for half in range(2):
                head_rows = slice(half * HEAD_DIM, (half + 1) * HEAD_DIM)
                band = split(band_matrix(r.ptaps, 2 * pair + half, False))
                high = windows(v[0][head_rows])
                smooth = dot(high, band[0]) + (
                    dot(high, band[1]) + dot(windows(v[1][head_rows]), band[0])
                )
                smoothed.append(blocks_back(smooth, HEAD_DIM))
            out = out + jnp.concatenate(smoothed, axis=0)
            r.attended[:, rows] = out.astype(bf16).T

    def attend_back(self, joined):
        r = self.r
        width, length = self.width, self.length
        pairs = width // PAIR
        live = r.live[0:1, :]
        factor = live * HEAD_DIM ** (-0.25)
        diagonal = same_head()
        flip = jnp.where(iota((128, 128), 0) + iota((128, 128), 1) == 127, 1.0, 0.0).astype(bf16)
        state = []
        for pair in range(pairs):
            rows = slice(pair * PAIR, (pair + 1) * PAIR)
            d_out = r.d_attended[rows, :]
            d_mixed = split(jnp.where(diagonal, dot(r.first[rows, :], d_out, NT), 0.0))
            d_inverse = dot3(d_mixed, split(r.marks[3, pair]), NT)
            d_carried = dot3(split(r.marks[4, pair]), d_mixed, TN)
            state.append((d_inverse, jnp.zeros((PAIR, PAIR), f32), d_carried))
            d_v = dot(d_carried.T.astype(bf16), r.third[rows, :])
            smoothed = []
            for half in range(2):
                head = 2 * pair + half
                head_rows = slice(half * HEAD_DIM, (half + 1) * HEAD_DIM)
                band = split(band_matrix(r.ptaps, head, True))
                around = windows(d_out[head_rows])
                smoothed.append(blocks_back(dot(around, band[0]) + dot(around, band[1]), HEAD_DIM))
                start = 2 * width + head * HEAD_DIM
                flipped = dot(blocks_down(d_out[head_rows]), flip).astype(bf16)
                products = dot(flipped, windows(r.qkv[start : start + HEAD_DIM, :]), TN)
                lined = pltpu.roll(products, 17, 1, stride=1, stride_axis=0)
                total = jnp.sum(lined, axis=0, keepdims=True)
                r.small[5:6, head * 128 : (head + 1) * 128] = total[:, 256:]
            d_v = (d_v + jnp.concatenate(smoothed, axis=0)) * live
            place = slice(2 * width + pair * PAIR, 2 * width + (pair + 1) * PAIR)
            joined[place, :] = d_v.astype(bf16)
            r.small[4:5, place] = row_sums(d_v)
        self.store(r.g_rest, slice(2 * width, 3 * width), dot(r.x[...].T, joined[2 * width :, :], NT))
        self.launch("g_rest", 2 * width, 3 * width)
        self.tick()
        for step in reversed(range(NS_ITERS)):
            following = []
            for pair in range(pairs):
                d_approx, d_matrix, d_carried = state[pair]
                approx = split(r.chain[step, 0, pair])
                product = split(r.chain[step, 1, pair])
                along = split(r.chain[step, 2, pair])
                inner = split(r.chain[step, 3, pair])
                d_parts = split(0.25 * d_approx)
                d_inner = dot3(along, d_parts, TN)
                d_along = split(dot3(d_parts, inner, NT) - 3.75 * d_approx)
                d_parts = split(d_inner)
                d_product = 7.0 * d_inner - dot3(d_parts, product, NT) - dot3(product, d_parts, TN)
                d_product = split(d_product + dot3(approx, d_along, TN))
                d_next = 3.25 * d_approx + dot3(d_along, product, NT)
                d_matrix = d_matrix + dot3(d_product, approx, NT)
                d_next = d_next + dot3(split(r.marks[2, pair]), d_product, TN)
                following.append((d_next, d_matrix, d_carried))
            state = following
            self.tick()
        seg_turned = segments_turned(length)
        counts = segment_counts(live, segments(length))
        for pair in range(pairs):
            rows = slice(pair * PAIR, (pair + 1) * PAIR)
            k_rows = slice(width + pair * PAIR, width + (pair + 1) * PAIR)
            v_rows = slice(2 * width + pair * PAIR, 2 * width + (pair + 1) * PAIR)
            d_approx, d_matrix, d_carried = state[pair]
            qm = r.marks[0, pair]
            km = r.marks[1, pair]
            second = r.marks[2, pair]
            square_sum = head_sum(jnp.sum(second * second, axis=1, keepdims=True))
            turned = d_approx.T
            along = head_sum(jnp.sum(turned * second, axis=1, keepdims=True))
            d_matrix = d_matrix + turned / square_sum
            d_matrix = d_matrix - second * (2.0 * along / (square_sum * square_sum))
            d_scores = second * (d_matrix - jnp.sum(d_matrix * second, axis=1, keepdims=True))
            d_scores = split(d_scores)
            d_out = r.d_attended[rows, :]
            first = r.first[rows, :].astype(f32)
            d_first = dot(r.marks[5, pair].astype(bf16), d_out)
            d_first = (first * (d_first - head_sum(d_first * first))).astype(bf16)
            third = r.third[rows, :]
            d_third = dot(d_carried.astype(bf16), r.qkv[v_rows, :])
            wide = third.astype(f32)
            d_third = wide * (d_third - jnp.sum(d_third * wide, axis=1, keepdims=True))
            d_third = d_third.astype(bf16)
            d_qm = dot3(d_scores, split(km))
            d_qm = d_qm + jnp.where(diagonal, dot(d_third, r.qkv[k_rows, :], NT), 0.0)
            d_km = dot3(d_scores, split(qm), TN)
            d_km = d_km + jnp.where(diagonal, dot(d_first, r.qkv[rows, :], NT), 0.0)
            d_qm = split(d_qm.T / counts)
            d_km = split(d_km.T / counts)
            d_q = dot(km.T.astype(bf16), d_first) + (dot(d_qm[0], seg_turned) + dot(d_qm[1], seg_turned))
            d_k = dot(qm.T.astype(bf16), d_third) + (dot(d_km[0], seg_turned) + dot(d_km[1], seg_turned))
            for at, (value, scale) in enumerate(((d_q, factor), (d_k, factor))):
                place = slice(at * width + pair * PAIR, at * width + (pair + 1) * PAIR)
                value = value * scale
                joined[place, :] = value.astype(bf16)
                r.small[4:5, place] = row_sums(value)
            self.tick()


    def exchange(self, stage, chunk):
        r = self.r
        at = stage % 2
        rows_at = self.length // CHUNKS
        rows = pl.ds(chunk * rows_at, rows_at)
        sems = (r.send_sem.at[stage], r.recv_sem.at[stage])
        return self.remote(r.mine.at[at, rows], r.theirs.at[at, rows], sems, chunk, self.sister)

    def chunk_rows(self, chunk):
        rows_at = self.length // CHUNKS
        start = chunk * rows_at
        if not isinstance(chunk, int):
            start = pl.multiple_of(start, rows_at)
        return pl.ds(start, rows_at)

    def together(self, stage, chunk):
        self.exchange(stage, chunk).wait()
        rows = self.chunk_rows(chunk)
        at = stage % 2
        return self.r.mine[at, rows, :].astype(f32) + self.r.theirs[at, rows, :].astype(f32)

    def offer(self, stage, chunk, value):
        self.r.mine[stage % 2, self.chunk_rows(chunk), :] = value.astype(bf16)
        self.exchange(stage, chunk).start()

    def feed(self, low_ref, active_ref, slope_ref, d_low_ref, scale_ref):
        r = self.r
        block = 256
        units, width = self.units, self.width
        wide = units // 2
        out_bias, first_gain, first_shift, down_bias, second_gain, second_shift = (
            ref[...].reshape(1, self.model)
            for ref in (
                r.out_bias,
                r.first_gain,
                r.first_shift,
                r.down_bias,
                r.second_gain,
                r.second_shift,
            )
        )
        r.small[...] = jnp.zeros_like(r.small)

        def add_row(at, value):
            columns = slice((at % 2) * self.model, (at % 2 + 1) * self.model)
            r.small[at // 2 : at // 2 + 1, columns] += jnp.sum(value, axis=0, keepdims=True)

        self.onward(PIECES + 6)
        self.arrive([3], [3])

        @pl.loop(0, CHUNKS)
        def project(chunk):
            self.offer(0, chunk, dot(r.attended[self.chunk_rows(chunk), :], r.so[...]))

        self.onward(PIECES + 7)
        self.arrive([4], [4, 5])

        def raise_rows(chunk):
            rows = self.chunk_rows(chunk)
            summed = self.together(0, chunk) + out_bias + r.x[rows, :].astype(f32)
            normal, scale = normalize(summed)
            r.normal[rows, :] = normal
            scale_ref[rows, :] = scale
            low = (normal * first_gain + first_shift).astype(bf16)
            low_ref[rows, :] = low
            for at in range(0, units, block):
                columns = slice(at, at + block)
                raised = dot(low, r.su[:, columns]) + r.phalves[:, width + at : width + at + block]
                bell = 0.5 + 0.5 * lax.erf(raised * 0.7071067811865476)
                active_ref[rows, columns] = (raised * bell).astype(bf16)
                density = jnp.exp(-0.5 * raised * raised) * 0.3989422804014327
                slope_ref[rows, columns] = (bell + raised * density).astype(bf16)

        pl.loop(0, CHUNKS)(raise_rows)
        self.arrive([5], [6, 7])

        @pl.loop(0, CHUNKS)
        def lower(chunk):
            self.offer(1, chunk, dot(active_ref[self.chunk_rows(chunk), :], r.sd[...]))

        self.arrive([6], [], True)

        @pl.loop(0, CHUNKS)
        def turn(chunk):
            rows = self.chunk_rows(chunk)
            hidden = r.normal[rows, :] * first_gain + first_shift
            result = self.together(1, chunk) + down_bias + hidden
            normal, scale = normalize(result)
            r.out[rows, :] = (normal * second_gain + second_shift).astype(bf16)
            cotangent = r.cot[rows, :].astype(f32)
            d_result = normalize_back(cotangent * second_gain, normal, scale)
            add_row(4, cotangent * normal)
            add_row(5, cotangent)
            add_row(3, d_result)
            d_low_ref[rows, :] = d_result.astype(bf16)

        for chunk in range(CHUNKS):
            self.deliver(r.out, r.output, 0, chunk)
        turned = d_low_ref[...].T
        for at in range(0, units, wide):
            columns = slice(at, at + wide)
            self.store(r.g_down, columns, dot(turned, active_ref[:, columns]))
            self.launch("g_down", at, at + wide)

        def descend(chunk):
            rows = self.chunk_rows(chunk)
            d_low = d_low_ref[rows, :]
            for at in range(0, units, block):
                columns = slice(at, at + block)
                d_raised = dot(d_low, r.sd[columns, :], NT) * slope_ref[rows, columns].astype(f32)
                r.small[3:4, columns] += jnp.sum(d_raised, axis=0, keepdims=True)
                slope_ref[rows, columns] = d_raised.astype(bf16)
            self.offer(2, chunk, dot(slope_ref[rows, :], r.su[...], NT))

        pl.loop(0, CHUNKS // 2)(descend)
        self.tick()
        pl.loop(CHUNKS // 2, CHUNKS)(descend)
        self.tick()
        turned = low_ref[...].T
        for at in range(0, units, wide):
            columns = slice(at, at + wide)
            self.store(r.g_up, columns, dot(turned, slope_ref[:, columns]))
            self.launch("g_up", at, at + wide)
        self.tick()

        @pl.loop(0, CHUNKS)
        def back(chunk):
            rows = self.chunk_rows(chunk)
            d_hidden = d_low_ref[rows, :].astype(f32) + self.together(2, chunk)
            normal = r.normal[rows, :]
            add_row(1, d_hidden * normal)
            add_row(2, d_hidden)
            d_summed = normalize_back(d_hidden * first_gain, normal, scale_ref[rows, :])
            add_row(0, d_summed)
            r.normal[rows, :] = d_summed
            d_low_ref[rows, :] = d_summed.astype(bf16)

        r.d_attended[...] = dot(r.so[...], d_low_ref[...], NT).astype(bf16)
        turned = d_low_ref[...].T
        self.store(r.g_rest, slice(3 * width, 4 * width), dot(turned, r.attended[...]))
        self.launch("g_rest", 3 * width, 4 * width)
        self.tick()

    def store(self, ref, columns, value):
        value = value.astype(bf16)
        if self.parts:
            value = value.reshape(ref.shape[:-1] + (value.shape[1],))
            ref[:, :, :, :, :, columns] = value
        else:
            ref[:, columns] = value

    def deliver(self, source, target, at, chunk):
        r = self.r
        rows = self.chunk_rows(chunk)
        local, away = self.deliveries(source, target, at, chunk)

        @pl.when(self.own)
        def here():
            local.start()
            if chunk < CHUNKS // 2:
                away.start()

        if chunk >= CHUNKS // 2:

            @pl.when(self.other)
            def there():
                away.start()

    def deliveries(self, source, target, at, chunk):
        r = self.r
        rows = self.chunk_rows(chunk)
        local = pltpu.make_async_copy(source.at[rows], target.at[rows], r.home_sem.at[at, chunk])
        device = self.beyond if chunk < CHUNKS // 2 else self.cross
        sems = (r.away_sem.at[2 * at], r.away_sem.at[2 * at + 1])
        return local, self.remote(source.at[rows], target.at[rows], sems, chunk, device)

    def delivered(self, source, target, at):
        for chunk in range(CHUNKS):
            local, away = self.deliveries(source, target, at, chunk)

            @pl.when(self.own)
            def here():
                local.wait()
                if chunk < CHUNKS // 2:
                    away.wait_send()

            @pl.when(self.other)
            def there():
                away.wait_recv()
                if chunk >= CHUNKS // 2:
                    away.wait_send()


    def part_copy(self, part, level):
        name, start, count, order = self.parts[part]
        ref = getattr(self.r, name)
        bit = order[level]
        index = []
        for b in reversed(range(self.bits + 1)):
            if b in order[:level]:
                index.append(self.place[b])
            else:
                index.append(1 - self.place[b] if b == bit else slice(None))
        source = ref.at[tuple(index) + (slice(None), slice(start, start + count))]
        landing = self.r.landings[part * (self.bits + 1) + level]
        sems = (self.r.part_sem.at[0, part], self.r.part_sem.at[1, part])
        return self.remote(source, landing, sems, level, self.partner(bit))

    def part_finish(self, part, level):
        name, start, count, order = self.parts[part]
        ref = getattr(self.r, name)
        self.part_copy(part, level).wait()
        index = []
        for b in reversed(range(self.bits + 1)):
            index.append(self.place[b] if b in order[: level + 1] else slice(None))
        index = tuple(index) + (slice(None), slice(start, start + count))
        landing = self.r.landings[part * (self.bits + 1) + level]
        total = ref[index].astype(f32) + landing[...].astype(f32)
        if level < self.bits:
            ref[index] = total.astype(bf16)
        else:
            self.part_last(part, total)

    def direct(self, part):
        return self.parts[part][3][-1] == 0

    def direct_rows(self, part, half):
        name, start, count, order = self.parts[part]
        index = tuple(self.place[b] for b in reversed(range(1, self.bits + 1)))
        return getattr(self.r, name), index + (half, slice(None), slice(start, start + count))

    def direct_copies(self, part):
        r = self.r
        level = self.bits
        beyond = (r.part_sem.at[0, part], r.part_sem.at[1, part])
        aside = (r.swap_sem.at[0], r.swap_sem.at[1])
        over = (r.cross_sem.at[0], r.cross_sem.at[1])
        landing = r.landings[part * (self.bits + 1) + level]
        core = self.core
        ref, same = self.direct_rows(part, core)
        ref, other = self.direct_rows(part, 1 - core)
        return (
            self.remote(ref.at[same], landing, beyond, level, self.beyond),
            self.remote(ref.at[other], landing, over, part, self.cross),
            self.remote(ref.at[other], r.swap_in.at[part], aside, part, self.sister),
        )

    def direct_start(self, part):
        beyond, over, aside = self.direct_copies(part)

        @pl.when(self.own)
        def here():
            aside.start()

        @pl.when(self.other)
        def there():
            beyond.start()
            over.start()

    def direct_finish(self, part):
        beyond, over, aside = self.direct_copies(part)
        landing = self.r.landings[part * (self.bits + 1) + self.bits]
        target, columns = self.part_target(part)

        @pl.when(self.own)
        def here():
            beyond.wait_recv()
            ref, index = self.direct_rows(part, self.core)
            target[:, columns] = ref[index].astype(f32) + landing[...].astype(f32)
            aside.wait_send()

        @pl.when(self.other)
        def there():
            over.wait_recv()
            aside.wait_recv()
            target[:, columns] = self.r.swap_in[part].astype(f32) + landing[...].astype(f32)
            beyond.wait_send()
            over.wait_send()

    def part_swap(self, part):
        name, start, count, order = self.parts[part]
        ref = self.r.swap_out.at[part]
        sems = (self.r.swap_sem.at[0], self.r.swap_sem.at[1])
        return self.remote(ref, self.r.swap_in.at[part], sems, part, self.cross)

    def part_target(self, part):
        name, start, count, order = self.parts[part]
        return getattr(self.r, "t" + name[1:]), slice(start, start + count)

    def part_last(self, part, total):
        target, columns = self.part_target(part)

        @pl.when(self.own)
        def here():
            target[:, columns] = total

        @pl.when(self.other)
        def there():
            self.r.swap_out[part] = total.astype(bf16)
            self.part_swap(part).start()

    def launch(self, wanted, first, last):
        for part, (name, start, count, order) in enumerate(self.parts):
            if name == wanted and first <= start < last:
                self.part_copy(part, 0).start()
                self.levels[part] = 0

    def advance(self, part):
        level = self.levels[part]
        if level is None or level > self.bits:
            return
        if level == self.bits and self.direct(part):
            self.direct_finish(part)
        else:
            self.part_finish(part, level)
        if level + 1 == self.bits and self.direct(part):
            self.direct_start(part)
        elif level < self.bits:
            self.part_copy(part, level + 1).start()
        self.levels[part] = level + 1

    def tick(self):
        if self.parts and self.agenda:
            for part in self.agenda.pop(0):
                self.advance(part)

    def small_copy(self, level):
        r = self.r
        source = r.small if level == 0 else r.small_sum.at[level - 1]
        sems = (r.small_sem.at[0], r.small_sem.at[1])
        return self.remote(source, r.small_land.at[level], sems, level, self.partner(level))

    def small_advance(self):
        r = self.r
        level = self.small_level
        self.small_level += 1
        self.small_copy(level).wait()
        own = r.small[...] if level == 0 else r.small_sum[level - 1]
        r.small_sum[level] = own + r.small_land[level]
        if level < self.bits:
            self.small_copy(level + 1).start()

    def small_swap(self):
        r = self.r
        sems = (r.small_sem.at[0], r.small_sem.at[1])
        return self.remote(r.small_sum.at[self.bits], r.small_sister, sems, self.bits + 1, self.sister)

    def small_done(self):
        r = self.r
        total = r.small_sum[self.bits]
        r.tsmall[0:3, :] = total[0:3]

        @pl.when(self.own)
        def here():
            self.small_swap().start()
            r.tsmall[3:8, :] = total[3:8]
            self.small_swap().wait_send()

        @pl.when(self.other)
        def there():
            self.small_swap().wait_recv()
            r.tsmall[3:8, :] = r.small_sister[3:8, :]

    def finish(self, joined):
        r = self.r
        width, model, length = self.width, self.model, self.length
        bits = self.bits
        if self.parts:
            self.small_copy(0).start()
        turned = r.x[...].T
        for at in range(2):
            rows = slice(at * width, (at + 1) * width)
            self.store(r.g_rest, rows, dot(turned, joined[rows, :], NT))
            self.launch("g_rest", at * width, (at + 1) * width)
        rows_at = length // CHUNKS
        for chunk in range(CHUNKS):
            columns = slice(chunk * rows_at, (chunk + 1) * rows_at)
            back = dot(r.sqk[0], joined[0:width, columns])
            back = back + dot(r.sqk[1], joined[width : 2 * width, columns])
            back = back + dot(r.sv[...], joined[2 * width :, columns])
            self.offer(3, chunk, back.astype(bf16).T)
        for chunk in range(CHUNKS):
            rows = self.chunk_rows(chunk)
            r.grad[rows, :] = (r.normal[rows, :] + self.together(3, chunk)).astype(bf16)
            self.deliver(r.grad, r.tokens_grad, 1, chunk)
        if self.parts:
            for at, part in enumerate(FINAL):
                self.advance(part)
                if at % 6 == 5 and self.small_level <= bits:
                    self.small_advance()
            while self.small_level <= bits:
                self.small_advance()
            for level in range(bits + 1):
                for part in range(len(self.parts)):
                    if self.levels[part] <= level:
                        self.advance(part)
            self.small_done()
        else:
            r.tsmall[...] = r.small[...]
        self.delivered(r.out, r.output, 0)
        self.delivered(r.grad, r.tokens_grad, 1)
        for part in range(len(self.parts)):
            target, columns = self.part_target(part)
            if self.direct(part):
                continue

            @pl.when(self.other)
            def there():
                self.part_swap(part).wait()
                target[:, columns] = r.swap_in[part].astype(f32)

        self.drain()


def layer_kernel(names, bits, parts, agenda, sizes, *refs):
    found = dict(zip(names, refs))
    found["landings"] = refs[len(names) :]
    layer = Layer(found, bits, parts, sizes)
    layer.agenda = list(agenda)
    length, model, width, units, heads = sizes
    layer.greet()
    layer.begin()
    pl.run_scoped(layer.attend, *[pltpu.VMEM((width, length), f32)] * 3)
    pl.run_scoped(
        layer.feed,
        pltpu.VMEM((length, model), bf16),
        pltpu.VMEM((length, units), bf16),
        pltpu.VMEM((length, units), bf16),
        pltpu.VMEM((length, model), bf16),
        pltpu.VMEM((length, 1), f32),
    )

    def back(joined):
        layer.attend_back(joined)
        layer.finish(joined)

    pl.run_scoped(back, pltpu.VMEM((3 * width, length), bf16))


ORDERS = {
    3: (
        (1, 0, 2, 3),
        (1, 2, 3, 0),
        (2, 0, 3, 1),
        (1, 2, 3, 0),
        (2, 0, 1, 3),
        (0, 2, 1, 3),
        (2, 3, 1, 0),
        (2, 1, 3, 0),
        (0, 1, 2, 3),
        (1, 2, 3, 0),
        (1, 2, 0, 3),
        (1, 0, 2, 3),
    ),
}
AGENDA = (
    [],
    [],
    [],
    [2],
    [],
    [],
    [],
    [],
    [],
    [0, 1, 3],
    [5, 2, 4],
    [6, 7],
    [0, 11],
    [10, 4],
)
FINAL = (7, 2, 1, 11, 3, 4, 0, 5, 6, 2, 8, 9, 10, 5, 11, 6, 4, 0, 8, 10, 6, 7, 9, 1, 3, 5, 11, 8, 10, 7, 1, 9, 3, 8, 9)


def body(
    tokens,
    cotangent,
    lengths,
    masked,
    qk_weight,
    qk_bias,
    value_weight,
    value_bias,
    conv_taps,
    out_weight,
    out_bias,
    first_gain,
    first_shift,
    up_weight,
    up_bias,
    down_weight,
    down_bias,
    second_gain,
    second_shift,
):
    chips = lax.axis_size("chip")
    length, model = tokens.shape
    width = value_weight.shape[1]
    units = up_weight.shape[1]
    heads = conv_taps.shape[0]
    pairs = width // PAIR
    bits = chips.bit_length() - 1
    share = model // (2 * chips)
    fused = bits in ORDERS and share % 16 == 0
    parts = []
    if fused:
        count = units // 4
        for at, order in enumerate(ORDERS[bits]):
            parts.append((("g_down", "g_up", "g_rest")[at // 4], at % 4 * count, count, order))
    shape = jax.ShapeDtypeStruct
    hbm = pl.BlockSpec(memory_space=pl.ANY)
    inputs = [
        ("tokens", tokens, hbm),
        ("cotangent", cotangent, hbm),
        ("wqk", jnp.transpose(qk_weight, (1, 0, 2)), hbm),
        ("wv", value_weight, hbm),
        ("wo", out_weight, hbm),
        ("wu", up_weight, hbm),
        ("wd", down_weight, hbm),
        ("lengths", lengths, SMEM),
        ("masked", masked, VMEM),
        ("qk_bias", qk_bias, VMEM),
        ("taps", conv_taps, VMEM),
        ("v_bias", value_bias, VMEM),
        ("u_bias", up_bias, VMEM),
        ("out_bias", out_bias, VMEM),
        ("first_gain", first_gain, VMEM),
        ("first_shift", first_shift, VMEM),
        ("down_bias", down_bias, VMEM),
        ("second_gain", second_gain, VMEM),
        ("second_shift", second_shift, VMEM),
    ]
    outputs = [("output", shape((length, model), bf16), hbm), ("tokens_grad", shape((length, model), bf16), hbm)]
    outputs.append(("tsmall", shape((8, units), f32), VMEM))
    scratch = []
    for name in ("down", "up", "rest"):
        if fused:
            outputs.append(("t_" + name, shape((share, units), f32), VMEM))
            scratch.append(("g_" + name, pltpu.VMEM((2,) * (bits + 1) + (share, units), bf16)))
        else:
            outputs.append(("g_" + name, shape((model, units), bf16), VMEM))
    dma = pltpu.SemaphoreType.DMA
    scratch += [
        ("sqk", pltpu.VMEM((2, model, width), bf16)),
        ("sv", pltpu.VMEM((model, width), bf16)),
        ("so", pltpu.VMEM((width, model), bf16)),
        ("su", pltpu.VMEM((model, units), bf16)),
        ("sd", pltpu.VMEM((units, model), bf16)),
        ("x", pltpu.VMEM((length, model), bf16)),
        ("cot", pltpu.VMEM((length, model), bf16)),
        ("live", pltpu.VMEM((8, length), f32)),
        ("pqk", pltpu.VMEM((2, width), f32)),
        ("halves", pltpu.VMEM((1, width + units), f32)),
        ("phalves", pltpu.VMEM((1, width + units), f32)),
        ("ptaps", pltpu.VMEM((heads, KERNEL), f32)),
        ("qkv", pltpu.VMEM((3 * width, length), bf16)),
        ("first", pltpu.VMEM((width, length), bf16)),
        ("third", pltpu.VMEM((width, length), bf16)),
        ("attended", pltpu.VMEM((length, width), bf16)),
        ("marks", pltpu.VMEM((6, pairs, PAIR, PAIR), f32)),
        ("chain", pltpu.VMEM((NS_ITERS, 4, pairs, PAIR, PAIR), f32)),
        ("mine", pltpu.VMEM((2, length, model), bf16)),
        ("theirs", pltpu.VMEM((2, length, model), bf16)),
        ("normal", pltpu.VMEM((length, model), f32)),
        ("d_attended", pltpu.VMEM((width, length), bf16)),
        ("out", pltpu.VMEM((length, model), bf16)),
        ("grad", pltpu.VMEM((length, model), bf16)),
        ("small", pltpu.VMEM((8, units), f32)),
        ("weight_sem", dma((8, PIECES))),
        ("local_sem", dma((7,))),
        ("item_sem", dma((2, 3))),
        ("bias_sem", dma((2, 3))),
        ("send_sem", dma((4, CHUNKS))),
        ("recv_sem", dma((4, CHUNKS))),
        ("home_sem", dma((2, CHUNKS))),
        ("away_sem", dma((4, CHUNKS))),
    ]
    landings = []
    if fused:
        levels = bits + 1
        scratch += [
            ("small_land", pltpu.VMEM((levels, 8, units), f32)),
            ("small_sum", pltpu.VMEM((levels, 8, units), f32)),
            ("small_sister", pltpu.VMEM((8, units), f32)),
            ("small_sem", dma((2, levels + 1))),
            ("part_sem", dma((2, len(parts), levels))),
            ("swap_sem", dma((2, len(parts)))),
            ("cross_sem", dma((2, len(parts)))),
            ("swap_out", pltpu.VMEM((len(parts), share, parts[0][2]), bf16)),
            ("swap_in", pltpu.VMEM((len(parts), share, parts[0][2]), bf16)),
        ]
        for name, start, count, order in parts:
            landings += [pltpu.VMEM((2,) * (bits - level) + (share, count), bf16) for level in range(levels)]
    names = [n for n, *_ in inputs + outputs + scratch]
    got = pl.pallas_call(
        functools.partial(
            layer_kernel, names, bits, parts, AGENDA, (length, model, width, units, heads)
        ),
        out_shape=[kind for _, kind, _ in outputs],
        in_specs=[spec for *_, spec in inputs],
        out_specs=[spec for *_, spec in outputs],
        scratch_shapes=[kind for _, kind in scratch] + landings,
        compiler_params=pltpu.CompilerParams(
            collective_id=0, has_side_effects=True, vmem_limit_bytes=VMEM_LIMIT
        ),
        name="layer",
    )(*[value for _, value, _ in inputs])
    output, tokens_grad, small, down, up, rest = got
    if not fused:
        swap = lambda v: lax.ppermute(v, ("core", "mp"), [(0, 0), (1, 2), (2, 1), (3, 3)])
        gather = lambda g: swap(
            lax.psum_scatter(g, ("chip", "mp"), scatter_dimension=0, tiled=True).astype(f32)
        )
        down, up, rest = gather(down), gather(up), gather(rest)
        small = lax.psum(small, ("chip", "mp"))
        small = jnp.concatenate([small[:3], swap(small[3:])], axis=0)
    return arrange(output, tokens_grad, small, up, down, rest, heads)


def arrange_kernel(
    output,
    tokens_grad,
    small,
    up,
    down,
    rest,
    output_to,
    tokens_grad_to,
    qk_to,
    qk_bias_to,
    v_to,
    v_bias_to,
    taps_to,
    out_to,
    out_bias_to,
    first_gain_to,
    first_shift_to,
    up_to,
    up_bias_to,
    down_to,
    down_bias_to,
    second_gain_to,
    second_shift_to,
    output_at,
    tokens_grad_at,
    up_at,
    down_at,
    rest_at,
    small_at,
    sems,
):
    pairs = (
        (small, small_at),
        (rest, rest_at),
        (output, output_at),
        (tokens_grad, tokens_grad_at),
        (up, up_at),
        (down, down_at),
    )
    coming = [pltpu.make_async_copy(a, b, sems.at[0, i]) for i, (a, b) in enumerate(pairs)]
    pairs = (
        (output_at, output_to),
        (tokens_grad_at, tokens_grad_to),
        (up_at, up_to),
        (down_at, down_to),
    )
    going = [pltpu.make_async_copy(a, b, sems.at[1, i]) for i, (a, b) in enumerate(pairs)]
    for copy in coming:
        copy.start()
    for copy in coming[:2]:
        copy.wait()
    small, rest = small_at, rest_at
    width = v_to.shape[1]
    model = out_bias_to.shape[0]
    units = up_bias_to.shape[0]
    for at in range(2):
        columns = slice(at * width, (at + 1) * width)
        qk_to[:, at, :] = rest[:, columns]
        qk_bias_to[at : at + 1, :] = small[4:5, columns]
    v_to[...] = rest[:, 2 * width : 3 * width]
    out_to[...] = rest[:, 3 * width :]
    v_bias_to[...] = small[4:5, 2 * width : 3 * width].reshape(width)
    up_bias_to[...] = small[3:4, :].reshape(units)
    for head in range(taps_to.shape[0]):
        taps_to[head : head + 1, :] = small[5:6, head * 128 : head * 128 + KERNEL]
    common = (out_bias_to, first_gain_to, first_shift_to, down_bias_to, second_gain_to, second_shift_to)
    for at, ref in enumerate(common):
        columns = slice(at % 2 * model, (at % 2 + 1) * model)
        ref[...] = small[at // 2 : at // 2 + 1, columns].reshape(model)
    for here, there in zip(coming[2:], going):
        here.wait()
        there.start()
    for copy in going:
        copy.wait()


def arrange(output, tokens_grad, small, up, down, rest, heads):
    share, units = up.shape
    width = rest.shape[1] // 4
    model = output.shape[1]
    hbm = pl.BlockSpec(memory_space=pl.ANY)
    kinds = [
        (output.shape, bf16),
        (output.shape, bf16),
        ((share, 2, width), f32),
        ((2, width), f32),
        ((share, width), f32),
        ((width,), f32),
        ((heads, KERNEL), f32),
        ((share, width), f32),
        ((model,), f32),
        ((model,), f32),
        ((model,), f32),
        ((share, units), f32),
        ((units,), f32),
        ((share, units), f32),
        ((model,), f32),
        ((model,), f32),
        ((model,), f32),
    ]
    got = pl.pallas_call(
        arrange_kernel,
        out_shape=[jax.ShapeDtypeStruct(a, b) for a, b in kinds],
        in_specs=[hbm] * 6,
        out_specs=[hbm if at in (0, 1, 11, 13) else VMEM for at in range(len(kinds))],
        scratch_shapes=[
            pltpu.VMEM(output.shape, bf16),
            pltpu.VMEM(output.shape, bf16),
            pltpu.VMEM(up.shape, f32),
            pltpu.VMEM(up.shape, f32),
            pltpu.VMEM(up.shape, f32),
            pltpu.VMEM(small.shape, f32),
            pltpu.SemaphoreType.DMA((2, 6)),
        ],
        compiler_params=pltpu.CompilerParams(vmem_limit_bytes=VMEM_LIMIT),
        name="arrange",
    )(output, tokens_grad, small, up, down, rest)
    got = list(got)
    got[7] = got[7].T
    got[13] = got[13].T
    return tuple(got)


def solution(mesh):
    dp = ("chip", "core")
    placed = (
        P(dp, None),
        P(dp, None),
        P(dp),
        P(dp, None),
        P(None, None, "mp"),
        P(None, "mp"),
        P(None, "mp"),
        P("mp"),
        P("mp", None),
        P("mp", None),
        P(),
        P(),
        P(),
        P(None, "mp"),
        P("mp"),
        P("mp", None),
        P(),
        P(),
        P(),
    )
    chips = mesh.shape["dp"] // 2
    fine = Mesh(mesh.devices.reshape(chips, 2, mesh.shape["mp"]), ("chip", "core", "mp"))
    return jax.shard_map(
        body,
        mesh=fine,
        in_specs=placed,
        out_specs=(
            P(dp, None),
            P(dp, None),
            P(dp, None, "mp"),
            P(None, "mp"),
            P(dp, "mp"),
            P("mp"),
            P("mp", None),
            P("mp", dp),
            P(),
            P(),
            P(),
            P(dp, "mp"),
            P("mp"),
            P("mp", dp),
            P(),
            P(),
            P(),
        ),
        check_vma=False,
    )
```

```python
import functools
import types

import jax
import jax.numpy as jnp
from jax import lax
from jax.experimental import pallas as pl
from jax.experimental.pallas import tpu as pltpu
from jax.sharding import Mesh
from jax.sharding import PartitionSpec as P

HEAD_DIM = 64
LANDMARKS = 64
NS_ITERS = 6
KERNEL = 33
EDGE = 112
BAND = 160
PAIR = 2 * HEAD_DIM
CHUNKS = 4
PIECES = 8
AHEAD = 2
VMEM_LIMIT = 64 << 20

f32 = jnp.float32
bf16 = jnp.bfloat16
NN = (((1,), (0,)), ((), ()))
NT = (((1,), (1,)), ((), ()))
TN = (((0,), (0,)), ((), ()))
MESH = pl.DeviceIdType.MESH
VMEM = pl.BlockSpec(memory_space=pltpu.VMEM)
SMEM = pl.BlockSpec(memory_space=pltpu.SMEM)


def dot(a, b, dims=NN):
    return lax.dot_general(a, b, dims, preferred_element_type=f32)


def split(value):
    high = value.astype(bf16)
    return high, (value - high.astype(f32)).astype(bf16)


def dot3(a, b, dims=NN):
    return dot(a[0], b[0], dims) + (dot(a[0], b[1], dims) + dot(a[1], b[0], dims))


def iota(shape, axis):
    return lax.broadcasted_iota(jnp.int32, shape, axis)


def same_head():
    return iota((PAIR, PAIR), 0) // HEAD_DIM == iota((PAIR, PAIR), 1) // HEAD_DIM


def identity():
    return jnp.where(iota((PAIR, PAIR), 0) == iota((PAIR, PAIR), 1), 1.0, 0.0).astype(f32)


def segments(length):
    spread = length // LANDMARKS
    hit = iota((length, PAIR), 0) // spread == iota((length, PAIR), 1) % LANDMARKS
    return jnp.where(hit, 1.0, 0.0).astype(bf16)


def segments_turned(length):
    spread = length // LANDMARKS
    hit = iota((PAIR, length), 1) // spread == iota((PAIR, length), 0) % LANDMARKS
    return jnp.where(hit, 1.0, 0.0).astype(bf16)


def segment_counts(live, seg):
    rows = jnp.broadcast_to(live, (8, live.shape[1])).astype(bf16)
    return jnp.maximum(dot(rows, seg)[0:1], 1.0)


def head_sum(value):
    heads = value.shape[0] // HEAD_DIM
    cut = value.reshape(heads, HEAD_DIM, value.shape[1])
    total = jnp.sum(cut, axis=1, keepdims=True)
    return jnp.broadcast_to(total, cut.shape).reshape(value.shape)


def head_max(value):
    heads = value.shape[0] // HEAD_DIM
    cut = value.reshape(heads, HEAD_DIM, value.shape[1])
    top = jnp.max(cut, axis=1, keepdims=True)
    return jnp.broadcast_to(top, cut.shape).reshape(value.shape)


def softmax_lanes(scores):
    weights = jnp.exp(scores - jnp.max(scores, axis=1, keepdims=True))
    return weights / jnp.sum(weights, axis=1, keepdims=True)


def band_matrix(taps_ref, head, turned):
    gap = iota((BAND, 128), 0) - iota((BAND, 128), 1)
    total = jnp.zeros((BAND, 128), f32)
    for tap in range(KERNEL):
        source = KERNEL - 1 - tap if turned else tap
        weight = taps_ref[head : head + 1, source : source + 1]
        total = jnp.where(gap == tap, weight, total)
    zeros = jnp.zeros((EDGE, 128), f32)
    return jnp.concatenate([zeros, total, zeros], axis=0)


def windows(rows):
    zeros = jnp.zeros((rows.shape[0], 128), rows.dtype)
    padded = jnp.concatenate([zeros, rows, zeros], axis=1)
    blocks = rows.shape[1] // 128
    return jnp.concatenate([padded[:, b * 128 : b * 128 + 384] for b in range(blocks)], axis=0)


def blocks_down(rows):
    blocks = rows.shape[1] // 128
    return jnp.concatenate([rows[:, b * 128 : (b + 1) * 128] for b in range(blocks)], axis=0)


def blocks_back(stacked, height):
    blocks = stacked.shape[0] // height
    return jnp.concatenate([stacked[b * height : (b + 1) * height] for b in range(blocks)], axis=1)


def normalize(value):
    middle = jnp.mean(value, axis=1, keepdims=True)
    centered = value - middle
    spread = jnp.mean(centered * centered, axis=1, keepdims=True)
    scale = lax.rsqrt(spread + 1e-05)
    return centered * scale, scale


def normalize_back(grad, normal, scale):
    middle = jnp.mean(grad, axis=1, keepdims=True)
    along = jnp.mean(grad * normal, axis=1, keepdims=True)
    return scale * (grad - middle - normal * along)


def column(row):
    return jnp.broadcast_to(row, (8, row.shape[1])).T[:, 0:1]


def row_sums(value):
    parts = split(value)
    ones = jnp.ones((8, value.shape[1]), bf16)
    return (dot(ones, parts[0], NT) + dot(ones, parts[1], NT))[0:1]


class Layer:
    def __init__(self, refs, bits, parts, sizes):
        self.r = types.SimpleNamespace(**refs)
        self.bits = bits
        self.parts = parts
        self.length, self.model, self.width, self.units, self.heads = sizes
        self.chip = lax.axis_index("chip")
        self.core = lax.axis_index("core")
        self.half = lax.axis_index("mp")
        self.own = self.core == self.half
        self.other = self.core != self.half
        self.sister = (self.chip, 1 - self.core, self.half)
        self.beyond = (self.chip, self.core, 1 - self.half)
        self.cross = (self.chip, 1 - self.core, 1 - self.half)
        self.place = [self.half] + [lax.rem(lax.div(self.chip, 2**i), 2) for i in range(bits)]
        self.levels = [None] * len(parts)
        self.small_level = 0

    def partner(self, bit):
        if bit == 0:
            return self.beyond
        step = 2 ** (bit - 1)
        return (self.chip + step * (1 - 2 * self.place[bit]), self.core, self.half)

    def greet(self):
        known = [self.sister, self.beyond, self.cross]
        known += [self.partner(bit) for bit in range(1, (self.bits if self.parts else 2) + 1)]
        barrier = pltpu.get_barrier_semaphore()
        for device in known:
            pl.semaphore_signal(barrier, inc=1, device_id=device, device_id_type=MESH)
        pl.semaphore_wait(barrier, len(known))

    def remote(self, source, target, sems, at, device):
        return pltpu.make_async_remote_copy(
            src_ref=source,
            dst_ref=target,
            send_sem=sems[0].at[at],
            recv_sem=sems[1].at[at],
            device_id=device,
            device_id_type=MESH,
        )


    def pieces(self):
        r = self.r
        found = []
        for a, b in ((r.wqk.at[0], r.sqk.at[0]), (r.wqk.at[1], r.sqk.at[1]), (r.wv, r.sv), (r.wo, r.so)):
            found.append((a, b, 0, 1))
        for a, b in ((r.wu, r.su), (r.wd, r.sd)):
            found += [(a, b, sub, 2) for sub in range(2)]
        return found

    def quarter(self, flips):
        low, high = self.place[1], self.place[2]
        if 0 in flips:
            low = 1 - low
        if 1 in flips:
            high = 1 - high
        return low + 2 * high

    def weight_copy(self, kind, at, arriving=False):
        source, target, sub, subs = self.pieces()[at]
        first, second = (0, 1) if at % 2 else (1, 0)
        if kind == "over":
            flips, device, lane = (), self.cross, 0
        elif kind == "first":
            flips, device, lane = (), self.partner(first + 1), 1
            if arriving:
                flips = (first,)
        elif kind == "second":
            flips, device, lane = (), self.partner(second + 1), 2
            if arriving:
                flips = (second,)
        else:
            flips, device, lane = (first,), self.partner(second + 1), 3
            if arriving:
                flips = (first, second)
        rows = source.shape[0] // 4
        step = rows // subs
        start = self.quarter(flips) * rows + sub * step
        place = pl.ds(pl.multiple_of(start, 16), step)
        sems = (self.r.weight_sem.at[2 * lane], self.r.weight_sem.at[2 * lane + 1])
        begin = source if kind == "over" else target
        return self.remote(begin.at[place], target.at[place], sems, at, device)

    def relay(self, at):
        self.weight_copy("over", at, True).wait_recv()
        self.weight_copy("first", at).start()
        self.weight_copy("second", at).start()
        self.weight_copy("over", at).wait_send()
        if at + AHEAD < PIECES:
            self.weight_copy("over", at + AHEAD).start()

    def relay_on(self, at):
        self.weight_copy("first", at, True).wait_recv()
        self.weight_copy("third", at).start()

    def landed(self, at):
        self.weight_copy("second", at, True).wait_recv()
        self.weight_copy("third", at, True).wait_recv()

    def onward(self, *steps):
        @pl.when(self.other)
        def forward():
            for step in steps:
                if step < PIECES:
                    self.relay(step)
                else:
                    self.relay_on(step - PIECES)

    def locals(self):
        r = self.r
        pairs = ((r.tokens, r.x), (r.wqk, r.sqk), (r.wv, r.sv), (r.wo, r.so), (r.wu, r.su), (r.wd, r.sd), (r.cotangent, r.cot))
        return [pltpu.make_async_copy(a, b, r.local_sem.at[i]) for i, (a, b) in enumerate(pairs)]

    def item_copies(self):
        r = self.r
        sems = (r.item_sem.at[0], r.item_sem.at[1])
        pairs = ((r.live, r.live), (r.tokens, r.x), (r.cotangent, r.cot))
        return [self.remote(a, b, sems, i, self.sister) for i, (a, b) in enumerate(pairs)]

    def bias_copies(self):
        r = self.r
        sems = (r.bias_sem.at[0], r.bias_sem.at[1])
        pairs = ((r.qk_bias, r.pqk), (r.halves, r.phalves), (r.taps, r.ptaps))
        return [self.remote(a, b, sems, i, self.cross) for i, (a, b) in enumerate(pairs)]

    def begin(self):
        r = self.r
        length = self.length
        r.halves[:, : self.width] = r.v_bias[...].reshape(1, self.width)
        r.halves[:, self.width :] = r.u_bias[...].reshape(1, self.units)

        @pl.when(self.own)
        def send():
            for copy in self.locals():
                copy.start()
            listed = r.masked[...].astype(f32)
            count = listed.shape[1]
            wide = jnp.broadcast_to(listed, (count, count))
            wide = jnp.where(iota((count, count), 0) == iota((count, count), 1), wide, 0.0)
            listed = jnp.sum(wide, axis=1, keepdims=True)
            places = iota((count, length), 1)
            hit = jnp.where(places.astype(f32) == listed, 1.0, 0.0)
            hit = jnp.max(hit, axis=0, keepdims=True)
            live = jnp.where(iota((1, length), 1) < r.lengths[0], 1.0 - hit, 0.0)
            r.live[...] = jnp.broadcast_to(live, (8, length))
            item = self.item_copies()
            item[0].start()
            item[1].start()
            item[2].start()
            r.pqk[...] = r.qk_bias[...]
            r.phalves[...] = r.halves[...]
            r.ptaps[...] = r.taps[...]
            for at in range(3):
                self.locals()[at].wait()

        @pl.when(self.other)
        def receive():
            for copy in self.bias_copies():
                copy.start()
            for at in range(AHEAD):
                self.weight_copy("over", at).start()
            self.relay(0)
            self.relay(1)
            self.relay_on(0)
            self.relay(2)
            self.relay_on(1)
            self.relay(3)
            self.relay_on(2)
            item = self.item_copies()
            item[0].wait_recv()
            item[1].wait_recv()
            for copy in self.bias_copies():
                copy.wait()
            self.landed(0)
            self.landed(1)
            self.relay(4)
            self.relay_on(3)
            self.landed(2)

    def arrive(self, local, ats, cotangent=False):
        @pl.when(self.own)
        def here():
            for at in local:
                self.locals()[at].wait()

        @pl.when(self.other)
        def there():
            for at in ats:
                self.landed(at)
            if cotangent:
                self.item_copies()[2].wait_recv()

    def drain(self):
        @pl.when(self.own)
        def here():
            for copy in self.item_copies():
                copy.wait_send()

        @pl.when(self.other)
        def there():
            for at in range(PIECES):
                for kind in ("first", "second", "third"):
                    self.weight_copy(kind, at).wait_send()


    def attend(self, q_ref, k_ref, v_ref):
        r = self.r
        width, length = self.width, self.length
        pairs = width // PAIR
        live = r.live[0:1, :]
        factor = live * HEAD_DIM ** (-0.25)
        plan = (
            (q_ref, r.sqk[0], r.pqk[0:1, :], factor),
            (k_ref, r.sqk[1], r.pqk[1:2, :], factor),
            (v_ref, r.sv[...], r.phalves[:, : self.width], live),
        )
        for at, (kept, weight, bias, scale) in enumerate(plan):
            rows = slice(at * width, (at + 1) * width)
            value = (dot(weight.T, r.x[...], NT) + column(bias)) * scale
            kept[...] = value
            r.qkv[rows, :] = value.astype(bf16)
        self.onward(5, PIECES + 4)
        seg = segments(length)
        counts = segment_counts(live, seg)
        diagonal = same_head()
        state = []
        for pair in range(pairs):
            rows = slice(pair * PAIR, (pair + 1) * PAIR)
            q = split(q_ref[rows, :])
            k = split(k_ref[rows, :])
            qm_turned = jnp.where(diagonal, (dot(q[0], seg) + dot(q[1], seg)) / counts, 0.0)
            km_turned = jnp.where(diagonal, (dot(k[0], seg) + dot(k[1], seg)) / counts, 0.0)
            qm = qm_turned.T
            km = km_turned.T
            qm_parts = split(qm)
            scores = dot3(split(km), q)
            weights = jnp.exp(scores - head_max(scores))
            r.first[rows, :] = (weights / head_sum(weights)).astype(bf16)
            third = softmax_lanes(dot3(qm_parts, k) - 10000.0 * (1.0 - live))
            r.third[rows, :] = third.astype(bf16)
            scores = dot3(qm_parts, split(km_turned))
            second = softmax_lanes(jnp.where(diagonal, scores, -1e30))
            carried = jnp.where(diagonal, dot3(split(third), split(v_ref[rows, :]), NT), 0.0)
            r.marks[0, pair] = qm
            r.marks[1, pair] = km
            r.marks[2, pair] = second
            r.marks[3, pair] = carried
            square_sum = head_sum(jnp.sum(second * second, axis=1, keepdims=True))
            state.append((split(second), second.T / square_sum))
            if pair == 2:
                self.onward(PIECES + 5, 6)
        for step in range(NS_ITERS):
            following = []
            for pair in range(pairs):
                matrix, approx = state[pair]
                r.chain[step, 0, pair] = approx
                approx_parts = split(approx)
                product = dot3(matrix, approx_parts)
                r.chain[step, 1, pair] = product
                parts = split(product)
                along = dot3(approx_parts, parts)
                r.chain[step, 2, pair] = along
                inner = 7.0 * product - dot3(parts, parts)
                r.chain[step, 3, pair] = inner
                approx = 3.25 * approx - 3.75 * along + 0.25 * dot3(split(along), split(inner))
                following.append((matrix, approx))
            state = following
        self.onward(7)
        for pair in range(pairs):
            rows = slice(pair * PAIR, (pair + 1) * PAIR)
            inverse = state[pair][1]
            mixed = dot3(split(inverse), split(r.marks[3, pair]))
            r.marks[4, pair] = inverse
            r.marks[5, pair] = mixed
            out = dot(mixed.T.astype(bf16), r.first[rows, :])
            v = split(v_ref[rows, :])
            smoothed = []
            for half in range(2):
                head_rows = slice(half * HEAD_DIM, (half + 1) * HEAD_DIM)
                band = split(band_matrix(r.ptaps, 2 * pair + half, False))
                high = windows(v[0][head_rows])
                smooth = dot(high, band[0]) + (
                    dot(high, band[1]) + dot(windows(v[1][head_rows]), band[0])
                )
                smoothed.append(blocks_back(smooth, HEAD_DIM))
            out = out + jnp.concatenate(smoothed, axis=0)
            r.attended[:, rows] = out.astype(bf16).T

    def attend_back(self, joined):
        r = self.r
        width, length = self.width, self.length
        pairs = width // PAIR
        live = r.live[0:1, :]
        factor = live * HEAD_DIM ** (-0.25)
        diagonal = same_head()
        flip = jnp.where(iota((128, 128), 0) + iota((128, 128), 1) == 127, 1.0, 0.0).astype(bf16)
        state = []
        for pair in range(pairs):
            rows = slice(pair * PAIR, (pair + 1) * PAIR)
            d_out = r.d_attended[rows, :]
            d_mixed = split(jnp.where(diagonal, dot(r.first[rows, :], d_out, NT), 0.0))
            d_inverse = dot3(d_mixed, split(r.marks[3, pair]), NT)
            d_carried = dot3(split(r.marks[4, pair]), d_mixed, TN)
            state.append((d_inverse, jnp.zeros((PAIR, PAIR), f32), d_carried))
            d_v = dot(d_carried.T.astype(bf16), r.third[rows, :])
            smoothed = []
            for half in range(2):
                head = 2 * pair + half
                head_rows = slice(half * HEAD_DIM, (half + 1) * HEAD_DIM)
                band = split(band_matrix(r.ptaps, head, True))
                around = windows(d_out[head_rows])
                smoothed.append(blocks_back(dot(around, band[0]) + dot(around, band[1]), HEAD_DIM))
                start = 2 * width + head * HEAD_DIM
                flipped = dot(blocks_down(d_out[head_rows]), flip).astype(bf16)
                products = dot(flipped, windows(r.qkv[start : start + HEAD_DIM, :]), TN)
                lined = pltpu.roll(products, 17, 1, stride=1, stride_axis=0)
                total = jnp.sum(lined, axis=0, keepdims=True)
                r.small[5:6, head * 128 : (head + 1) * 128] = total[:, 256:]
            d_v = (d_v + jnp.concatenate(smoothed, axis=0)) * live
            place = slice(2 * width + pair * PAIR, 2 * width + (pair + 1) * PAIR)
            joined[place, :] = d_v.astype(bf16)
            r.small[4:5, place] = row_sums(d_v)
        self.store(r.g_rest, slice(2 * width, 3 * width), dot(r.x[...].T, joined[2 * width :, :], NT))
        self.launch("g_rest", 2 * width, 3 * width)
        self.tick()
        for step in reversed(range(NS_ITERS)):
            following = []
            for pair in range(pairs):
                d_approx, d_matrix, d_carried = state[pair]
                approx = split(r.chain[step, 0, pair])
                product = split(r.chain[step, 1, pair])
                along = split(r.chain[step, 2, pair])
                inner = split(r.chain[step, 3, pair])
                d_parts = split(0.25 * d_approx)
                d_inner = dot3(along, d_parts, TN)
                d_along = split(dot3(d_parts, inner, NT) - 3.75 * d_approx)
                d_parts = split(d_inner)
                d_product = 7.0 * d_inner - dot3(d_parts, product, NT) - dot3(product, d_parts, TN)
                d_product = split(d_product + dot3(approx, d_along, TN))
                d_next = 3.25 * d_approx + dot3(d_along, product, NT)
                d_matrix = d_matrix + dot3(d_product, approx, NT)
                d_next = d_next + dot3(split(r.marks[2, pair]), d_product, TN)
                following.append((d_next, d_matrix, d_carried))
            state = following
            self.tick()
        seg_turned = segments_turned(length)
        counts = segment_counts(live, segments(length))
        for pair in range(pairs):
            rows = slice(pair * PAIR, (pair + 1) * PAIR)
            k_rows = slice(width + pair * PAIR, width + (pair + 1) * PAIR)
            v_rows = slice(2 * width + pair * PAIR, 2 * width + (pair + 1) * PAIR)
            d_approx, d_matrix, d_carried = state[pair]
            qm = r.marks[0, pair]
            km = r.marks[1, pair]
            second = r.marks[2, pair]
            square_sum = head_sum(jnp.sum(second * second, axis=1, keepdims=True))
            turned = d_approx.T
            along = head_sum(jnp.sum(turned * second, axis=1, keepdims=True))
            d_matrix = d_matrix + turned / square_sum
            d_matrix = d_matrix - second * (2.0 * along / (square_sum * square_sum))
            d_scores = second * (d_matrix - jnp.sum(d_matrix * second, axis=1, keepdims=True))
            d_scores = split(d_scores)
            d_out = r.d_attended[rows, :]
            first = r.first[rows, :].astype(f32)
            d_first = dot(r.marks[5, pair].astype(bf16), d_out)
            d_first = (first * (d_first - head_sum(d_first * first))).astype(bf16)
            third = r.third[rows, :]
            d_third = dot(d_carried.astype(bf16), r.qkv[v_rows, :])
            wide = third.astype(f32)
            d_third = wide * (d_third - jnp.sum(d_third * wide, axis=1, keepdims=True))
            d_third = d_third.astype(bf16)
            d_qm = dot3(d_scores, split(km))
            d_qm = d_qm + jnp.where(diagonal, dot(d_third, r.qkv[k_rows, :], NT), 0.0)
            d_km = dot3(d_scores, split(qm), TN)
            d_km = d_km + jnp.where(diagonal, dot(d_first, r.qkv[rows, :], NT), 0.0)
            d_qm = split(d_qm.T / counts)
            d_km = split(d_km.T / counts)
            d_q = dot(km.T.astype(bf16), d_first) + (dot(d_qm[0], seg_turned) + dot(d_qm[1], seg_turned))
            d_k = dot(qm.T.astype(bf16), d_third) + (dot(d_km[0], seg_turned) + dot(d_km[1], seg_turned))
            for at, (value, scale) in enumerate(((d_q, factor), (d_k, factor))):
                place = slice(at * width + pair * PAIR, at * width + (pair + 1) * PAIR)
                value = value * scale
                joined[place, :] = value.astype(bf16)
                r.small[4:5, place] = row_sums(value)
            self.tick()


    def exchange(self, stage, chunk):
        r = self.r
        at = stage % 2
        rows_at = self.length // CHUNKS
        rows = pl.ds(chunk * rows_at, rows_at)
        sems = (r.send_sem.at[stage], r.recv_sem.at[stage])
        return self.remote(r.mine.at[at, rows], r.theirs.at[at, rows], sems, chunk, self.sister)

    def chunk_rows(self, chunk):
        rows_at = self.length // CHUNKS
        start = chunk * rows_at
        if not isinstance(chunk, int):
            start = pl.multiple_of(start, rows_at)
        return pl.ds(start, rows_at)

    def together(self, stage, chunk):
        self.exchange(stage, chunk).wait()
        rows = self.chunk_rows(chunk)
        at = stage % 2
        return self.r.mine[at, rows, :].astype(f32) + self.r.theirs[at, rows, :].astype(f32)

    def offer(self, stage, chunk, value):
        self.r.mine[stage % 2, self.chunk_rows(chunk), :] = value.astype(bf16)
        self.exchange(stage, chunk).start()

    def feed(self, low_ref, active_ref, slope_ref, d_low_ref, scale_ref):
        r = self.r
        block = 256
        units, width = self.units, self.width
        wide = units // 2
        out_bias, first_gain, first_shift, down_bias, second_gain, second_shift = (
            ref[...].reshape(1, self.model)
            for ref in (
                r.out_bias,
                r.first_gain,
                r.first_shift,
                r.down_bias,
                r.second_gain,
                r.second_shift,
            )
        )
        r.small[...] = jnp.zeros_like(r.small)

        def add_row(at, value):
            columns = slice((at % 2) * self.model, (at % 2 + 1) * self.model)
            r.small[at // 2 : at // 2 + 1, columns] += jnp.sum(value, axis=0, keepdims=True)

        self.onward(PIECES + 6)
        self.arrive([3], [3])

        @pl.loop(0, CHUNKS)
        def project(chunk):
            self.offer(0, chunk, dot(r.attended[self.chunk_rows(chunk), :], r.so[...]))

        self.onward(PIECES + 7)
        self.arrive([4], [4, 5])

        def raise_rows(chunk):
            rows = self.chunk_rows(chunk)
            summed = self.together(0, chunk) + out_bias + r.x[rows, :].astype(f32)
            normal, scale = normalize(summed)
            r.normal[rows, :] = normal
            scale_ref[rows, :] = scale
            low = (normal * first_gain + first_shift).astype(bf16)
            low_ref[rows, :] = low
            for at in range(0, units, block):
                columns = slice(at, at + block)
                raised = dot(low, r.su[:, columns]) + r.phalves[:, width + at : width + at + block]
                bell = 0.5 + 0.5 * lax.erf(raised * 0.7071067811865476)
                active_ref[rows, columns] = (raised * bell).astype(bf16)
                density = jnp.exp(-0.5 * raised * raised) * 0.3989422804014327
                slope_ref[rows, columns] = (bell + raised * density).astype(bf16)

        pl.loop(0, CHUNKS)(raise_rows)
        self.arrive([5], [6, 7])

        @pl.loop(0, CHUNKS)
        def lower(chunk):
            self.offer(1, chunk, dot(active_ref[self.chunk_rows(chunk), :], r.sd[...]))

        self.arrive([6], [], True)

        @pl.loop(0, CHUNKS)
        def turn(chunk):
            rows = self.chunk_rows(chunk)
            hidden = r.normal[rows, :] * first_gain + first_shift
            result = self.together(1, chunk) + down_bias + hidden
            normal, scale = normalize(result)
            r.out[rows, :] = (normal * second_gain + second_shift).astype(bf16)
            cotangent = r.cot[rows, :].astype(f32)
            d_result = normalize_back(cotangent * second_gain, normal, scale)
            add_row(4, cotangent * normal)
            add_row(5, cotangent)
            add_row(3, d_result)
            d_low_ref[rows, :] = d_result.astype(bf16)

        for chunk in range(CHUNKS):
            self.deliver(r.out, r.output, 0, chunk)
        turned = d_low_ref[...].T
        for at in range(0, units, wide):
            columns = slice(at, at + wide)
            self.store(r.g_down, columns, dot(turned, active_ref[:, columns]))
            self.launch("g_down", at, at + wide)

        def descend(chunk):
            rows = self.chunk_rows(chunk)
            d_low = d_low_ref[rows, :]
            for at in range(0, units, block):
                columns = slice(at, at + block)
                d_raised = dot(d_low, r.sd[columns, :], NT) * slope_ref[rows, columns].astype(f32)
                r.small[3:4, columns] += jnp.sum(d_raised, axis=0, keepdims=True)
                slope_ref[rows, columns] = d_raised.astype(bf16)
            self.offer(2, chunk, dot(slope_ref[rows, :], r.su[...], NT))

        pl.loop(0, CHUNKS // 2)(descend)
        self.tick()
        pl.loop(CHUNKS // 2, CHUNKS)(descend)
        self.tick()
        turned = low_ref[...].T
        for at in range(0, units, wide):
            columns = slice(at, at + wide)
            self.store(r.g_up, columns, dot(turned, slope_ref[:, columns]))
            self.launch("g_up", at, at + wide)
        self.tick()

        @pl.loop(0, CHUNKS)
        def back(chunk):
            rows = self.chunk_rows(chunk)
            d_hidden = d_low_ref[rows, :].astype(f32) + self.together(2, chunk)
            normal = r.normal[rows, :]
            add_row(1, d_hidden * normal)
            add_row(2, d_hidden)
            d_summed = normalize_back(d_hidden * first_gain, normal, scale_ref[rows, :])
            add_row(0, d_summed)
            r.normal[rows, :] = d_summed
            d_low_ref[rows, :] = d_summed.astype(bf16)

        r.d_attended[...] = dot(r.so[...], d_low_ref[...], NT).astype(bf16)
        turned = d_low_ref[...].T
        self.store(r.g_rest, slice(3 * width, 4 * width), dot(turned, r.attended[...]))
        self.launch("g_rest", 3 * width, 4 * width)
        self.tick()

    def store(self, ref, columns, value):
        value = value.astype(bf16)
        if self.parts:
            value = value.reshape(ref.shape[:-1] + (value.shape[1],))
            ref[:, :, :, :, :, columns] = value
        else:
            ref[:, columns] = value

    def deliver(self, source, target, at, chunk):
        r = self.r
        rows = self.chunk_rows(chunk)
        local, away = self.deliveries(source, target, at, chunk)

        @pl.when(self.own)
        def here():
            local.start()
            if chunk < CHUNKS // 2:
                away.start()

        if chunk >= CHUNKS // 2:

            @pl.when(self.other)
            def there():
                away.start()

    def deliveries(self, source, target, at, chunk):
        r = self.r
        rows = self.chunk_rows(chunk)
        local = pltpu.make_async_copy(source.at[rows], target.at[rows], r.home_sem.at[at, chunk])
        device = self.beyond if chunk < CHUNKS // 2 else self.cross
        sems = (r.away_sem.at[2 * at], r.away_sem.at[2 * at + 1])
        return local, self.remote(source.at[rows], target.at[rows], sems, chunk, device)

    def delivered(self, source, target, at):
        for chunk in range(CHUNKS):
            local, away = self.deliveries(source, target, at, chunk)

            @pl.when(self.own)
            def here():
                local.wait()
                if chunk < CHUNKS // 2:
                    away.wait_send()

            @pl.when(self.other)
            def there():
                away.wait_recv()
                if chunk >= CHUNKS // 2:
                    away.wait_send()


    def part_copy(self, part, level):
        name, start, count, order = self.parts[part]
        ref = getattr(self.r, name)
        bit = order[level]
        index = []
        for b in reversed(range(self.bits + 1)):
            if b in order[:level]:
                index.append(self.place[b])
            else:
                index.append(1 - self.place[b] if b == bit else slice(None))
        source = ref.at[tuple(index) + (slice(None), slice(start, start + count))]
        landing = self.r.landings[part * (self.bits + 1) + level]
        sems = (self.r.part_sem.at[0, part], self.r.part_sem.at[1, part])
        return self.remote(source, landing, sems, level, self.partner(bit))

    def part_finish(self, part, level):
        name, start, count, order = self.parts[part]
        ref = getattr(self.r, name)
        self.part_copy(part, level).wait()
        index = []
        for b in reversed(range(self.bits + 1)):
            index.append(self.place[b] if b in order[: level + 1] else slice(None))
        index = tuple(index) + (slice(None), slice(start, start + count))
        landing = self.r.landings[part * (self.bits + 1) + level]
        total = ref[index].astype(f32) + landing[...].astype(f32)
        if level < self.bits:
            ref[index] = total.astype(bf16)
        else:
            self.part_last(part, total)

    def direct(self, part):
        return self.parts[part][3][-1] == 0

    def direct_rows(self, part, half):
        name, start, count, order = self.parts[part]
        index = tuple(self.place[b] for b in reversed(range(1, self.bits + 1)))
        return getattr(self.r, name), index + (half, slice(None), slice(start, start + count))

    def direct_copies(self, part):
        r = self.r
        level = self.bits
        beyond = (r.part_sem.at[0, part], r.part_sem.at[1, part])
        aside = (r.swap_sem.at[0], r.swap_sem.at[1])
        over = (r.cross_sem.at[0], r.cross_sem.at[1])
        landing = r.landings[part * (self.bits + 1) + level]
        core = self.core
        ref, same = self.direct_rows(part, core)
        ref, other = self.direct_rows(part, 1 - core)
        return (
            self.remote(ref.at[same], landing, beyond, level, self.beyond),
            self.remote(ref.at[other], landing, over, part, self.cross),
            self.remote(ref.at[other], r.swap_in.at[part], aside, part, self.sister),
        )

    def direct_start(self, part):
        beyond, over, aside = self.direct_copies(part)

        @pl.when(self.own)
        def here():
            aside.start()

        @pl.when(self.other)
        def there():
            beyond.start()
            over.start()

    def direct_finish(self, part):
        beyond, over, aside = self.direct_copies(part)
        landing = self.r.landings[part * (self.bits + 1) + self.bits]
        target, columns = self.part_target(part)

        @pl.when(self.own)
        def here():
            beyond.wait_recv()
            ref, index = self.direct_rows(part, self.core)
            target[:, columns] = ref[index].astype(f32) + landing[...].astype(f32)
            aside.wait_send()

        @pl.when(self.other)
        def there():
            over.wait_recv()
            aside.wait_recv()
            target[:, columns] = self.r.swap_in[part].astype(f32) + landing[...].astype(f32)
            beyond.wait_send()
            over.wait_send()

    def part_swap(self, part):
        name, start, count, order = self.parts[part]
        ref = self.r.swap_out.at[part]
        sems = (self.r.swap_sem.at[0], self.r.swap_sem.at[1])
        return self.remote(ref, self.r.swap_in.at[part], sems, part, self.cross)

    def part_target(self, part):
        name, start, count, order = self.parts[part]
        return getattr(self.r, "t" + name[1:]), slice(start, start + count)

    def part_last(self, part, total):
        target, columns = self.part_target(part)

        @pl.when(self.own)
        def here():
            target[:, columns] = total

        @pl.when(self.other)
        def there():
            self.r.swap_out[part] = total.astype(bf16)
            self.part_swap(part).start()

    def launch(self, wanted, first, last):
        for part, (name, start, count, order) in enumerate(self.parts):
            if name == wanted and first <= start < last:
                self.part_copy(part, 0).start()
                self.levels[part] = 0

    def advance(self, part):
        level = self.levels[part]
        if level is None or level > self.bits:
            return
        if level == self.bits and self.direct(part):
            self.direct_finish(part)
        else:
            self.part_finish(part, level)
        if level + 1 == self.bits and self.direct(part):
            self.direct_start(part)
        elif level < self.bits:
            self.part_copy(part, level + 1).start()
        self.levels[part] = level + 1

    def tick(self):
        if self.parts and self.agenda:
            for part in self.agenda.pop(0):
                self.advance(part)

    def small_copy(self, level):
        r = self.r
        source = r.small if level == 0 else r.small_sum.at[level - 1]
        sems = (r.small_sem.at[0], r.small_sem.at[1])
        return self.remote(source, r.small_land.at[level], sems, level, self.partner(level))

    def small_advance(self):
        r = self.r
        level = self.small_level
        self.small_level += 1
        self.small_copy(level).wait()
        own = r.small[...] if level == 0 else r.small_sum[level - 1]
        r.small_sum[level] = own + r.small_land[level]
        if level < self.bits:
            self.small_copy(level + 1).start()
        else:

            @pl.when(self.own)
            def pass_on():
                self.small_swap().start()

    def small_swap(self):
        r = self.r
        sems = (r.small_sem.at[0], r.small_sem.at[1])
        return self.remote(r.small_sum.at[self.bits], r.small_sister, sems, self.bits + 1, self.sister)

    def small_done(self):
        r = self.r
        total = r.small_sum[self.bits]
        r.tsmall[0:3, :] = total[0:3]

        @pl.when(self.own)
        def here():
            r.tsmall[3:8, :] = total[3:8]
            self.small_swap().wait_send()

        @pl.when(self.other)
        def there():
            self.small_swap().wait_recv()
            r.tsmall[3:8, :] = r.small_sister[3:8, :]

    def finish(self, joined):
        r = self.r
        width, model, length = self.width, self.model, self.length
        bits = self.bits
        if self.parts:
            self.small_copy(0).start()
        turned = r.x[...].T
        for at in range(2):
            rows = slice(at * width, (at + 1) * width)
            self.store(r.g_rest, rows, dot(turned, joined[rows, :], NT))
            self.launch("g_rest", at * width, (at + 1) * width)
        rows_at = length // CHUNKS
        for chunk in range(CHUNKS):
            columns = slice(chunk * rows_at, (chunk + 1) * rows_at)
            back = dot(r.sqk[0], joined[0:width, columns])
            back = back + dot(r.sqk[1], joined[width : 2 * width, columns])
            back = back + dot(r.sv[...], joined[2 * width :, columns])
            self.offer(3, chunk, back.astype(bf16).T)
        for chunk in range(CHUNKS):
            rows = self.chunk_rows(chunk)
            r.grad[rows, :] = (r.normal[rows, :] + self.together(3, chunk)).astype(bf16)
            self.deliver(r.grad, r.tokens_grad, 1, chunk)
        if self.parts:
            for at, part in enumerate(FINAL):
                self.advance(part)
                if at % 6 == 5 and self.small_level <= bits:
                    self.small_advance()
            while self.small_level <= bits:
                self.small_advance()
            for level in range(bits + 1):
                for part in range(len(self.parts)):
                    if self.levels[part] <= level:
                        self.advance(part)
            self.small_done()
        else:
            r.tsmall[...] = r.small[...]
        self.delivered(r.out, r.output, 0)
        self.delivered(r.grad, r.tokens_grad, 1)
        for part in range(len(self.parts)):
            target, columns = self.part_target(part)
            if self.direct(part):
                continue

            @pl.when(self.other)
            def there():
                self.part_swap(part).wait()
                target[:, columns] = r.swap_in[part].astype(f32)

        self.drain()


def layer_kernel(names, bits, parts, agenda, sizes, *refs):
    found = dict(zip(names, refs))
    found["landings"] = refs[len(names) :]
    layer = Layer(found, bits, parts, sizes)
    layer.agenda = list(agenda)
    length, model, width, units, heads = sizes
    layer.greet()
    layer.begin()
    pl.run_scoped(layer.attend, *[pltpu.VMEM((width, length), f32)] * 3)
    pl.run_scoped(
        layer.feed,
        pltpu.VMEM((length, model), bf16),
        pltpu.VMEM((length, units), bf16),
        pltpu.VMEM((length, units), bf16),
        pltpu.VMEM((length, model), bf16),
        pltpu.VMEM((length, 1), f32),
    )

    def back(joined):
        layer.attend_back(joined)
        layer.finish(joined)

    pl.run_scoped(back, pltpu.VMEM((3 * width, length), bf16))


ORDERS = {
    3: (
        (1, 0, 2, 3),
        (1, 2, 3, 0),
        (2, 0, 3, 1),
        (1, 2, 3, 0),
        (2, 0, 1, 3),
        (0, 2, 1, 3),
        (2, 3, 1, 0),
        (2, 1, 3, 0),
        (0, 1, 2, 3),
        (1, 2, 3, 0),
        (1, 2, 0, 3),
        (1, 0, 2, 3),
    ),
}
AGENDA = (
    [],
    [],
    [],
    [2],
    [],
    [],
    [],
    [],
    [],
    [0, 1, 3],
    [5, 2, 4],
    [6, 7],
    [0, 11],
    [10, 4],
)
FINAL = (7, 2, 1, 11, 3, 4, 0, 5, 6, 2, 8, 9, 10, 5, 11, 6, 4, 0, 8, 10, 6, 7, 9, 1, 3, 5, 11, 8, 10, 7, 1, 9, 3, 8, 9)


def body(
    tokens,
    cotangent,
    lengths,
    masked,
    qk_weight,
    qk_bias,
    value_weight,
    value_bias,
    conv_taps,
    out_weight,
    out_bias,
    first_gain,
    first_shift,
    up_weight,
    up_bias,
    down_weight,
    down_bias,
    second_gain,
    second_shift,
):
    chips = lax.axis_size("chip")
    length, model = tokens.shape
    width = value_weight.shape[1]
    units = up_weight.shape[1]
    heads = conv_taps.shape[0]
    pairs = width // PAIR
    bits = chips.bit_length() - 1
    share = model // (2 * chips)
    fused = bits in ORDERS and share % 16 == 0
    parts = []
    if fused:
        count = units // 4
        for at, order in enumerate(ORDERS[bits]):
            parts.append((("g_down", "g_up", "g_rest")[at // 4], at % 4 * count, count, order))
    shape = jax.ShapeDtypeStruct
    hbm = pl.BlockSpec(memory_space=pl.ANY)
    inputs = [
        ("tokens", tokens, hbm),
        ("cotangent", cotangent, hbm),
        ("wqk", jnp.transpose(qk_weight, (1, 0, 2)), hbm),
        ("wv", value_weight, hbm),
        ("wo", out_weight, hbm),
        ("wu", up_weight, hbm),
        ("wd", down_weight, hbm),
        ("lengths", lengths, SMEM),
        ("masked", masked, VMEM),
        ("qk_bias", qk_bias, VMEM),
        ("taps", conv_taps, VMEM),
        ("v_bias", value_bias, VMEM),
        ("u_bias", up_bias, VMEM),
        ("out_bias", out_bias, VMEM),
        ("first_gain", first_gain, VMEM),
        ("first_shift", first_shift, VMEM),
        ("down_bias", down_bias, VMEM),
        ("second_gain", second_gain, VMEM),
        ("second_shift", second_shift, VMEM),
    ]
    outputs = [("output", shape((length, model), bf16), hbm), ("tokens_grad", shape((length, model), bf16), hbm)]
    outputs.append(("tsmall", shape((8, units), f32), VMEM))
    scratch = []
    for name in ("down", "up", "rest"):
        if fused:
            outputs.append(("t_" + name, shape((share, units), f32), VMEM))
            scratch.append(("g_" + name, pltpu.VMEM((2,) * (bits + 1) + (share, units), bf16)))
        else:
            outputs.append(("g_" + name, shape((model, units), bf16), VMEM))
    dma = pltpu.SemaphoreType.DMA
    scratch += [
        ("sqk", pltpu.VMEM((2, model, width), bf16)),
        ("sv", pltpu.VMEM((model, width), bf16)),
        ("so", pltpu.VMEM((width, model), bf16)),
        ("su", pltpu.VMEM((model, units), bf16)),
        ("sd", pltpu.VMEM((units, model), bf16)),
        ("x", pltpu.VMEM((length, model), bf16)),
        ("cot", pltpu.VMEM((length, model), bf16)),
        ("live", pltpu.VMEM((8, length), f32)),
        ("pqk", pltpu.VMEM((2, width), f32)),
        ("halves", pltpu.VMEM((1, width + units), f32)),
        ("phalves", pltpu.VMEM((1, width + units), f32)),
        ("ptaps", pltpu.VMEM((heads, KERNEL), f32)),
        ("qkv", pltpu.VMEM((3 * width, length), bf16)),
        ("first", pltpu.VMEM((width, length), bf16)),
        ("third", pltpu.VMEM((width, length), bf16)),
        ("attended", pltpu.VMEM((length, width), bf16)),
        ("marks", pltpu.VMEM((6, pairs, PAIR, PAIR), f32)),
        ("chain", pltpu.VMEM((NS_ITERS, 4, pairs, PAIR, PAIR), f32)),
        ("mine", pltpu.VMEM((2, length, model), bf16)),
        ("theirs", pltpu.VMEM((2, length, model), bf16)),
        ("normal", pltpu.VMEM((length, model), f32)),
        ("d_attended", pltpu.VMEM((width, length), bf16)),
        ("out", pltpu.VMEM((length, model), bf16)),
        ("grad", pltpu.VMEM((length, model), bf16)),
        ("small", pltpu.VMEM((8, units), f32)),
        ("weight_sem", dma((8, PIECES))),
        ("local_sem", dma((7,))),
        ("item_sem", dma((2, 3))),
        ("bias_sem", dma((2, 3))),
        ("send_sem", dma((4, CHUNKS))),
        ("recv_sem", dma((4, CHUNKS))),
        ("home_sem", dma((2, CHUNKS))),
        ("away_sem", dma((4, CHUNKS))),
    ]
    landings = []
    if fused:
        levels = bits + 1
        scratch += [
            ("small_land", pltpu.VMEM((levels, 8, units), f32)),
            ("small_sum", pltpu.VMEM((levels, 8, units), f32)),
            ("small_sister", pltpu.VMEM((8, units), f32)),
            ("small_sem", dma((2, levels + 1))),
            ("part_sem", dma((2, len(parts), levels))),
            ("swap_sem", dma((2, len(parts)))),
            ("cross_sem", dma((2, len(parts)))),
            ("swap_out", pltpu.VMEM((len(parts), share, parts[0][2]), bf16)),
            ("swap_in", pltpu.VMEM((len(parts), share, parts[0][2]), bf16)),
        ]
        for name, start, count, order in parts:
            landings += [pltpu.VMEM((2,) * (bits - level) + (share, count), bf16) for level in range(levels)]
    names = [n for n, *_ in inputs + outputs + scratch]
    got = pl.pallas_call(
        functools.partial(
            layer_kernel, names, bits, parts, AGENDA, (length, model, width, units, heads)
        ),
        out_shape=[kind for _, kind, _ in outputs],
        in_specs=[spec for *_, spec in inputs],
        out_specs=[spec for *_, spec in outputs],
        scratch_shapes=[kind for _, kind in scratch] + landings,
        compiler_params=pltpu.CompilerParams(
            collective_id=0, has_side_effects=True, vmem_limit_bytes=VMEM_LIMIT
        ),
        name="layer",
    )(*[value for _, value, _ in inputs])
    output, tokens_grad, small, down, up, rest = got
    if not fused:
        swap = lambda v: lax.ppermute(v, ("core", "mp"), [(0, 0), (1, 2), (2, 1), (3, 3)])
        gather = lambda g: swap(
            lax.psum_scatter(g, ("chip", "mp"), scatter_dimension=0, tiled=True).astype(f32)
        )
        down, up, rest = gather(down), gather(up), gather(rest)
        small = lax.psum(small, ("chip", "mp"))
        small = jnp.concatenate([small[:3], swap(small[3:])], axis=0)
    return arrange(output, tokens_grad, small, up, down, rest, heads)


def arrange_kernel(
    output,
    tokens_grad,
    small,
    up,
    down,
    rest,
    output_to,
    tokens_grad_to,
    qk_to,
    qk_bias_to,
    v_to,
    v_bias_to,
    taps_to,
    out_to,
    out_bias_to,
    first_gain_to,
    first_shift_to,
    up_to,
    up_bias_to,
    down_to,
    down_bias_to,
    second_gain_to,
    second_shift_to,
    output_at,
    tokens_grad_at,
    up_at,
    down_at,
    rest_at,
    small_at,
    sems,
):
    rows = output.shape[0] // CHUNKS
    ahead = [(small, small_at), (rest, rest_at), (up, up_at), (down, down_at)]
    after = [(up_at, up_to), (down_at, down_to)]
    for chunk in range(CHUNKS):
        place = pl.ds(chunk * rows, rows)
        ahead += [(output.at[place], output_at.at[place]), (tokens_grad.at[place], tokens_grad_at.at[place])]
        after += [(output_at.at[place], output_to.at[place]), (tokens_grad_at.at[place], tokens_grad_to.at[place])]
    coming = [pltpu.make_async_copy(a, b, sems.at[0, i]) for i, (a, b) in enumerate(ahead)]
    going = [pltpu.make_async_copy(a, b, sems.at[1, i]) for i, (a, b) in enumerate(after)]
    for copy in coming:
        copy.start()
    for copy in coming[:2]:
        copy.wait()
    for here, there in zip(coming[2:], going):
        here.wait()
        there.start()
    small, rest = small_at, rest_at
    width = v_to.shape[1]
    model = out_bias_to.shape[0]
    units = up_bias_to.shape[0]
    for at in range(2):
        columns = slice(at * width, (at + 1) * width)
        qk_to[:, at, :] = rest[:, columns]
        qk_bias_to[at : at + 1, :] = small[4:5, columns]
    v_to[...] = rest[:, 2 * width : 3 * width]
    out_to[...] = rest[:, 3 * width :]
    v_bias_to[...] = small[4:5, 2 * width : 3 * width].reshape(width)
    up_bias_to[...] = small[3:4, :].reshape(units)
    for head in range(taps_to.shape[0]):
        taps_to[head : head + 1, :] = small[5:6, head * 128 : head * 128 + KERNEL]
    common = (out_bias_to, first_gain_to, first_shift_to, down_bias_to, second_gain_to, second_shift_to)
    for at, ref in enumerate(common):
        columns = slice(at % 2 * model, (at % 2 + 1) * model)
        ref[...] = small[at // 2 : at // 2 + 1, columns].reshape(model)
    for copy in going:
        copy.wait()


def arrange(output, tokens_grad, small, up, down, rest, heads):
    share, units = up.shape
    width = rest.shape[1] // 4
    model = output.shape[1]
    hbm = pl.BlockSpec(memory_space=pl.ANY)
    kinds = [
        (output.shape, bf16),
        (output.shape, bf16),
        ((share, 2, width), f32),
        ((2, width), f32),
        ((share, width), f32),
        ((width,), f32),
        ((heads, KERNEL), f32),
        ((share, width), f32),
        ((model,), f32),
        ((model,), f32),
        ((model,), f32),
        ((share, units), f32),
        ((units,), f32),
        ((share, units), f32),
        ((model,), f32),
        ((model,), f32),
        ((model,), f32),
    ]
    got = pl.pallas_call(
        arrange_kernel,
        out_shape=[jax.ShapeDtypeStruct(a, b) for a, b in kinds],
        in_specs=[hbm] * 6,
        out_specs=[hbm if at in (0, 1, 11, 13) else VMEM for at in range(len(kinds))],
        scratch_shapes=[
            pltpu.VMEM(output.shape, bf16),
            pltpu.VMEM(output.shape, bf16),
            pltpu.VMEM(up.shape, f32),
            pltpu.VMEM(up.shape, f32),
            pltpu.VMEM(up.shape, f32),
            pltpu.VMEM(small.shape, f32),
            pltpu.SemaphoreType.DMA((2, 4 + 2 * CHUNKS)),
        ],
        compiler_params=pltpu.CompilerParams(vmem_limit_bytes=VMEM_LIMIT),
        name="arrange",
    )(output, tokens_grad, small, up, down, rest)
    got = list(got)
    got[7] = got[7].T
    got[13] = got[13].T
    return tuple(got)


def solution(mesh):
    dp = ("chip", "core")
    placed = (
        P(dp, None),
        P(dp, None),
        P(dp),
        P(dp, None),
        P(None, None, "mp"),
        P(None, "mp"),
        P(None, "mp"),
        P("mp"),
        P("mp", None),
        P("mp", None),
        P(),
        P(),
        P(),
        P(None, "mp"),
        P("mp"),
        P("mp", None),
        P(),
        P(),
        P(),
    )
    chips = mesh.shape["dp"] // 2
    fine = Mesh(mesh.devices.reshape(chips, 2, mesh.shape["mp"]), ("chip", "core", "mp"))
    return jax.shard_map(
        body,
        mesh=fine,
        in_specs=placed,
        out_specs=(
            P(dp, None),
            P(dp, None),
            P(dp, None, "mp"),
            P(None, "mp"),
            P(dp, "mp"),
            P("mp"),
            P("mp", None),
            P("mp", dp),
            P(),
            P(),
            P(),
            P(dp, "mp"),
            P("mp"),
            P("mp", dp),
            P(),
            P(),
            P(),
        ),
        check_vma=False,
    )
```

```python
import functools
import types

import jax
import jax.numpy as jnp
from jax import lax
from jax.experimental import pallas as pl
from jax.experimental.pallas import tpu as pltpu
from jax.sharding import Mesh
from jax.sharding import PartitionSpec as P

HEAD_DIM = 64
LANDMARKS = 64
NS_ITERS = 6
KERNEL = 33
EDGE = 112
BAND = 160
PAIR = 2 * HEAD_DIM
CHUNKS = 4
PIECES = 8
AHEAD = 2
VMEM_LIMIT = 64 << 20

f32 = jnp.float32
bf16 = jnp.bfloat16
NN = (((1,), (0,)), ((), ()))
NT = (((1,), (1,)), ((), ()))
TN = (((0,), (0,)), ((), ()))
MESH = pl.DeviceIdType.MESH
VMEM = pl.BlockSpec(memory_space=pltpu.VMEM)
SMEM = pl.BlockSpec(memory_space=pltpu.SMEM)


def dot(a, b, dims=NN):
    return lax.dot_general(a, b, dims, preferred_element_type=f32)


def split(value):
    high = value.astype(bf16)
    return high, (value - high.astype(f32)).astype(bf16)


def dot3(a, b, dims=NN):
    return dot(a[0], b[0], dims) + (dot(a[0], b[1], dims) + dot(a[1], b[0], dims))


def iota(shape, axis):
    return lax.broadcasted_iota(jnp.int32, shape, axis)


def same_head():
    return iota((PAIR, PAIR), 0) // HEAD_DIM == iota((PAIR, PAIR), 1) // HEAD_DIM


def identity():
    return jnp.where(iota((PAIR, PAIR), 0) == iota((PAIR, PAIR), 1), 1.0, 0.0).astype(f32)


def segments(length):
    spread = length // LANDMARKS
    hit = iota((length, PAIR), 0) // spread == iota((length, PAIR), 1) % LANDMARKS
    return jnp.where(hit, 1.0, 0.0).astype(bf16)


def segments_turned(length):
    spread = length // LANDMARKS
    hit = iota((PAIR, length), 1) // spread == iota((PAIR, length), 0) % LANDMARKS
    return jnp.where(hit, 1.0, 0.0).astype(bf16)


def segment_counts(live, seg):
    rows = jnp.broadcast_to(live, (8, live.shape[1])).astype(bf16)
    return jnp.maximum(dot(rows, seg)[0:1], 1.0)


def head_sum(value):
    heads = value.shape[0] // HEAD_DIM
    cut = value.reshape(heads, HEAD_DIM, value.shape[1])
    total = jnp.sum(cut, axis=1, keepdims=True)
    return jnp.broadcast_to(total, cut.shape).reshape(value.shape)


def head_max(value):
    heads = value.shape[0] // HEAD_DIM
    cut = value.reshape(heads, HEAD_DIM, value.shape[1])
    top = jnp.max(cut, axis=1, keepdims=True)
    return jnp.broadcast_to(top, cut.shape).reshape(value.shape)


def softmax_lanes(scores):
    weights = jnp.exp(scores - jnp.max(scores, axis=1, keepdims=True))
    return weights / jnp.sum(weights, axis=1, keepdims=True)


def band_matrix(taps_ref, head, turned):
    gap = iota((BAND, 128), 0) - iota((BAND, 128), 1)
    total = jnp.zeros((BAND, 128), f32)
    for tap in range(KERNEL):
        source = KERNEL - 1 - tap if turned else tap
        weight = taps_ref[head : head + 1, source : source + 1]
        total = jnp.where(gap == tap, weight, total)
    zeros = jnp.zeros((EDGE, 128), f32)
    return jnp.concatenate([zeros, total, zeros], axis=0)


def windows(rows):
    zeros = jnp.zeros((rows.shape[0], 128), rows.dtype)
    padded = jnp.concatenate([zeros, rows, zeros], axis=1)
    blocks = rows.shape[1] // 128
    return jnp.concatenate([padded[:, b * 128 : b * 128 + 384] for b in range(blocks)], axis=0)


def blocks_down(rows):
    blocks = rows.shape[1] // 128
    return jnp.concatenate([rows[:, b * 128 : (b + 1) * 128] for b in range(blocks)], axis=0)


def blocks_back(stacked, height):
    blocks = stacked.shape[0] // height
    return jnp.concatenate([stacked[b * height : (b + 1) * height] for b in range(blocks)], axis=1)


def normalize(value):
    middle = jnp.mean(value, axis=1, keepdims=True)
    centered = value - middle
    spread = jnp.mean(centered * centered, axis=1, keepdims=True)
    scale = lax.rsqrt(spread + 1e-05)
    return centered * scale, scale


def normalize_back(grad, normal, scale):
    middle = jnp.mean(grad, axis=1, keepdims=True)
    along = jnp.mean(grad * normal, axis=1, keepdims=True)
    return scale * (grad - middle - normal * along)


def column(row):
    return jnp.broadcast_to(row, (8, row.shape[1])).T[:, 0:1]


def row_sums(value):
    parts = split(value)
    ones = jnp.ones((8, value.shape[1]), bf16)
    return (dot(ones, parts[0], NT) + dot(ones, parts[1], NT))[0:1]


class Layer:
    def __init__(self, refs, bits, parts, sizes):
        self.r = types.SimpleNamespace(**refs)
        self.bits = bits
        self.parts = parts
        self.length, self.model, self.width, self.units, self.heads = sizes
        self.chip = lax.axis_index("chip")
        self.core = lax.axis_index("core")
        self.half = lax.axis_index("mp")
        self.own = self.core == self.half
        self.other = self.core != self.half
        self.sister = (self.chip, 1 - self.core, self.half)
        self.beyond = (self.chip, self.core, 1 - self.half)
        self.cross = (self.chip, 1 - self.core, 1 - self.half)
        self.place = [self.half] + [lax.rem(lax.div(self.chip, 2**i), 2) for i in range(bits)]
        self.levels = [None] * len(parts)
        self.small_level = 0

    def partner(self, bit):
        if bit == 0:
            return self.beyond
        step = 2 ** (bit - 1)
        return (self.chip + step * (1 - 2 * self.place[bit]), self.core, self.half)

    def greet(self):
        known = [self.sister, self.beyond, self.cross]
        known += [self.partner(bit) for bit in range(1, (self.bits if self.parts else 2) + 1)]
        barrier = pltpu.get_barrier_semaphore()
        for device in known:
            pl.semaphore_signal(barrier, inc=1, device_id=device, device_id_type=MESH)
        pl.semaphore_wait(barrier, len(known))

    def remote(self, source, target, sems, at, device):
        return pltpu.make_async_remote_copy(
            src_ref=source,
            dst_ref=target,
            send_sem=sems[0].at[at],
            recv_sem=sems[1].at[at],
            device_id=device,
            device_id_type=MESH,
        )


    def pieces(self):
        r = self.r
        found = []
        for a, b in ((r.wqk.at[0], r.sqk.at[0]), (r.wqk.at[1], r.sqk.at[1]), (r.wv, r.sv), (r.wo, r.so)):
            found.append((a, b, 0, 1))
        for a, b in ((r.wu, r.su), (r.wd, r.sd)):
            found += [(a, b, sub, 2) for sub in range(2)]
        return found

    def quarter(self, flips):
        low, high = self.place[1], self.place[2]
        if 0 in flips:
            low = 1 - low
        if 1 in flips:
            high = 1 - high
        return low + 2 * high

    def weight_copy(self, kind, at, arriving=False):
        source, target, sub, subs = self.pieces()[at]
        first, second = (0, 1) if at % 2 else (1, 0)
        if kind == "over":
            flips, device, lane = (), self.cross, 0
        elif kind == "first":
            flips, device, lane = (), self.partner(first + 1), 1
            if arriving:
                flips = (first,)
        elif kind == "second":
            flips, device, lane = (), self.partner(second + 1), 2
            if arriving:
                flips = (second,)
        else:
            flips, device, lane = (first,), self.partner(second + 1), 3
            if arriving:
                flips = (first, second)
        rows = source.shape[0] // 4
        step = rows // subs
        start = self.quarter(flips) * rows + sub * step
        place = pl.ds(pl.multiple_of(start, 16), step)
        sems = (self.r.weight_sem.at[2 * lane], self.r.weight_sem.at[2 * lane + 1])
        begin = source if kind == "over" else target
        return self.remote(begin.at[place], target.at[place], sems, at, device)

    def relay(self, at):
        self.weight_copy("over", at, True).wait_recv()
        self.weight_copy("first", at).start()
        self.weight_copy("second", at).start()
        self.weight_copy("over", at).wait_send()
        if at + AHEAD < PIECES:
            self.weight_copy("over", at + AHEAD).start()

    def relay_on(self, at):
        self.weight_copy("first", at, True).wait_recv()
        self.weight_copy("third", at).start()

    def landed(self, at):
        self.weight_copy("second", at, True).wait_recv()
        self.weight_copy("third", at, True).wait_recv()

    def onward(self, *steps):
        @pl.when(self.other)
        def forward():
            for step in steps:
                if step < PIECES:
                    self.relay(step)
                else:
                    self.relay_on(step - PIECES)

    def locals(self):
        r = self.r
        pairs = ((r.tokens, r.x), (r.wqk, r.sqk), (r.wv, r.sv), (r.wo, r.so), (r.wu, r.su), (r.wd, r.sd), (r.cotangent, r.cot))
        return [pltpu.make_async_copy(a, b, r.local_sem.at[i]) for i, (a, b) in enumerate(pairs)]

    def item_copies(self):
        r = self.r
        sems = (r.item_sem.at[0], r.item_sem.at[1])
        pairs = ((r.live, r.live), (r.tokens, r.x), (r.cotangent, r.cot))
        return [self.remote(a, b, sems, i, self.sister) for i, (a, b) in enumerate(pairs)]

    def bias_copies(self):
        r = self.r
        sems = (r.bias_sem.at[0], r.bias_sem.at[1])
        pairs = ((r.qk_bias, r.pqk), (r.halves, r.phalves), (r.taps, r.ptaps))
        return [self.remote(a, b, sems, i, self.cross) for i, (a, b) in enumerate(pairs)]

    def bands(self, band_ref):
        for head in range(self.heads):
            band_ref[0, head], band_ref[1, head] = split(band_matrix(self.r.ptaps, head, False))

    def begin(self, band_ref):
        r = self.r
        length = self.length
        r.halves[:, : self.width] = r.v_bias[...].reshape(1, self.width)
        r.halves[:, self.width :] = r.u_bias[...].reshape(1, self.units)

        @pl.when(self.own)
        def send():
            for copy in self.locals():
                copy.start()
            listed = r.masked[...].astype(f32)
            count = listed.shape[1]
            wide = jnp.broadcast_to(listed, (count, count))
            wide = jnp.where(iota((count, count), 0) == iota((count, count), 1), wide, 0.0)
            listed = jnp.sum(wide, axis=1, keepdims=True)
            places = iota((count, length), 1)
            hit = jnp.where(places.astype(f32) == listed, 1.0, 0.0)
            hit = jnp.max(hit, axis=0, keepdims=True)
            live = jnp.where(iota((1, length), 1) < r.lengths[0], 1.0 - hit, 0.0)
            r.live[...] = jnp.broadcast_to(live, (8, length))
            item = self.item_copies()
            item[0].start()
            item[1].start()
            item[2].start()
            r.pqk[...] = r.qk_bias[...]
            r.phalves[...] = r.halves[...]
            r.ptaps[...] = r.taps[...]
            self.bands(band_ref)
            for at in range(3):
                self.locals()[at].wait()

        @pl.when(self.other)
        def receive():
            for copy in self.bias_copies():
                copy.start()
            for at in range(AHEAD):
                self.weight_copy("over", at).start()
            self.relay(0)
            self.relay(1)
            self.relay_on(0)
            self.relay(2)
            self.relay_on(1)
            self.relay(3)
            self.relay_on(2)
            item = self.item_copies()
            item[0].wait_recv()
            item[1].wait_recv()
            for copy in self.bias_copies():
                copy.wait()
            self.bands(band_ref)
            self.landed(0)
            self.landed(1)
            self.relay(4)
            self.relay_on(3)
            self.landed(2)

    def arrive(self, local, ats, cotangent=False):
        @pl.when(self.own)
        def here():
            for at in local:
                self.locals()[at].wait()

        @pl.when(self.other)
        def there():
            for at in ats:
                self.landed(at)
            if cotangent:
                self.item_copies()[2].wait_recv()

    def drain(self):
        @pl.when(self.own)
        def here():
            for copy in self.item_copies():
                copy.wait_send()

        @pl.when(self.other)
        def there():
            for at in range(PIECES):
                for kind in ("first", "second", "third"):
                    self.weight_copy(kind, at).wait_send()


    def attend(self, q_ref, k_ref, v_ref, band_ref):
        r = self.r
        width, length = self.width, self.length
        pairs = width // PAIR
        live = r.live[0:1, :]
        factor = live * HEAD_DIM ** (-0.25)
        plan = (
            (q_ref, r.sqk[0], r.pqk[0:1, :], factor),
            (k_ref, r.sqk[1], r.pqk[1:2, :], factor),
            (v_ref, r.sv[...], r.phalves[:, : self.width], live),
        )
        for at, (kept, weight, bias, scale) in enumerate(plan):
            rows = slice(at * width, (at + 1) * width)
            value = (dot(weight.T, r.x[...], NT) + column(bias)) * scale
            kept[...] = value
            r.qkv[rows, :] = value.astype(bf16)
        self.onward(5, PIECES + 4)
        seg = segments(length)
        counts = segment_counts(live, seg)
        diagonal = same_head()
        state = []
        for pair in range(pairs):
            rows = slice(pair * PAIR, (pair + 1) * PAIR)
            q = split(q_ref[rows, :])
            k = split(k_ref[rows, :])
            qm_turned = jnp.where(diagonal, (dot(q[0], seg) + dot(q[1], seg)) / counts, 0.0)
            km_turned = jnp.where(diagonal, (dot(k[0], seg) + dot(k[1], seg)) / counts, 0.0)
            qm = qm_turned.T
            km = km_turned.T
            qm_parts = split(qm)
            scores = dot3(split(km), q)
            weights = jnp.exp(scores - head_max(scores))
            r.first[rows, :] = (weights / head_sum(weights)).astype(bf16)
            third = softmax_lanes(dot3(qm_parts, k) - 10000.0 * (1.0 - live))
            r.third[rows, :] = third.astype(bf16)
            scores = dot3(qm_parts, split(km_turned))
            second = softmax_lanes(jnp.where(diagonal, scores, -1e30))
            carried = jnp.where(diagonal, dot3(split(third), split(v_ref[rows, :]), NT), 0.0)
            r.marks[0, pair] = qm
            r.marks[1, pair] = km
            r.marks[2, pair] = second
            r.marks[3, pair] = carried
            square_sum = head_sum(jnp.sum(second * second, axis=1, keepdims=True))
            state.append((split(second), second.T / square_sum))
            if pair == 2:
                self.onward(PIECES + 5, 6)
        for step in range(NS_ITERS):
            following = []
            for pair in range(pairs):
                matrix, approx = state[pair]
                r.chain[step, 0, pair] = approx
                approx_parts = split(approx)
                product = dot3(matrix, approx_parts)
                r.chain[step, 1, pair] = product
                parts = split(product)
                along = dot3(approx_parts, parts)
                r.chain[step, 2, pair] = along
                inner = 7.0 * product - dot3(parts, parts)
                r.chain[step, 3, pair] = inner
                approx = 3.25 * approx - 3.75 * along + 0.25 * dot3(split(along), split(inner))
                following.append((matrix, approx))
            state = following
        self.onward(7)
        for pair in range(pairs):
            rows = slice(pair * PAIR, (pair + 1) * PAIR)
            inverse = state[pair][1]
            mixed = dot3(split(inverse), split(r.marks[3, pair]))
            r.marks[4, pair] = inverse
            r.marks[5, pair] = mixed
            out = dot(mixed.T.astype(bf16), r.first[rows, :])
            v = split(v_ref[rows, :])
            smoothed = []
            for half in range(2):
                head_rows = slice(half * HEAD_DIM, (half + 1) * HEAD_DIM)
                band = (band_ref[0, 2 * pair + half], band_ref[1, 2 * pair + half])
                high = windows(v[0][head_rows])
                smooth = dot(high, band[0]) + (
                    dot(high, band[1]) + dot(windows(v[1][head_rows]), band[0])
                )
                smoothed.append(blocks_back(smooth, HEAD_DIM))
            out = out + jnp.concatenate(smoothed, axis=0)
            r.attended[:, rows] = out.astype(bf16).T

    def attend_back(self, joined):
        r = self.r
        width, length = self.width, self.length
        pairs = width // PAIR
        live = r.live[0:1, :]
        factor = live * HEAD_DIM ** (-0.25)
        diagonal = same_head()
        flip = jnp.where(iota((128, 128), 0) + iota((128, 128), 1) == 127, 1.0, 0.0).astype(bf16)
        state = []
        for pair in range(pairs):
            rows = slice(pair * PAIR, (pair + 1) * PAIR)
            d_out = r.d_attended[rows, :]
            d_mixed = split(jnp.where(diagonal, dot(r.first[rows, :], d_out, NT), 0.0))
            d_inverse = dot3(d_mixed, split(r.marks[3, pair]), NT)
            d_carried = dot3(split(r.marks[4, pair]), d_mixed, TN)
            state.append((d_inverse, jnp.zeros((PAIR, PAIR), f32), d_carried))
            d_v = dot(d_carried.T.astype(bf16), r.third[rows, :])
            smoothed = []
            for half in range(2):
                head = 2 * pair + half
                head_rows = slice(half * HEAD_DIM, (half + 1) * HEAD_DIM)
                band = split(band_matrix(r.ptaps, head, True))
                around = windows(d_out[head_rows])
                smoothed.append(blocks_back(dot(around, band[0]) + dot(around, band[1]), HEAD_DIM))
                start = 2 * width + head * HEAD_DIM
                flipped = dot(blocks_down(d_out[head_rows]), flip).astype(bf16)
                products = dot(flipped, windows(r.qkv[start : start + HEAD_DIM, :]), TN)
                lined = pltpu.roll(products, 17, 1, stride=1, stride_axis=0)
                total = jnp.sum(lined, axis=0, keepdims=True)
                r.small[5:6, head * 128 : (head + 1) * 128] = total[:, 256:]
            d_v = (d_v + jnp.concatenate(smoothed, axis=0)) * live
            place = slice(2 * width + pair * PAIR, 2 * width + (pair + 1) * PAIR)
            joined[place, :] = d_v.astype(bf16)
            r.small[4:5, place] = row_sums(d_v)
        self.store(r.g_rest, slice(2 * width, 3 * width), dot(r.x[...].T, joined[2 * width :, :], NT))
        self.launch("g_rest", 2 * width, 3 * width)
        self.tick()
        for step in reversed(range(NS_ITERS)):
            following = []
            for pair in range(pairs):
                d_approx, d_matrix, d_carried = state[pair]
                approx = split(r.chain[step, 0, pair])
                product = split(r.chain[step, 1, pair])
                along = split(r.chain[step, 2, pair])
                inner = split(r.chain[step, 3, pair])
                d_parts = split(0.25 * d_approx)
                d_inner = dot3(along, d_parts, TN)
                d_along = split(dot3(d_parts, inner, NT) - 3.75 * d_approx)
                d_parts = split(d_inner)
                d_product = 7.0 * d_inner - dot3(d_parts, product, NT) - dot3(product, d_parts, TN)
                d_product = split(d_product + dot3(approx, d_along, TN))
                d_next = 3.25 * d_approx + dot3(d_along, product, NT)
                d_matrix = d_matrix + dot3(d_product, approx, NT)
                d_next = d_next + dot3(split(r.marks[2, pair]), d_product, TN)
                following.append((d_next, d_matrix, d_carried))
            state = following
            self.tick()
        seg_turned = segments_turned(length)
        counts = segment_counts(live, segments(length))
        for pair in range(pairs):
            rows = slice(pair * PAIR, (pair + 1) * PAIR)
            k_rows = slice(width + pair * PAIR, width + (pair + 1) * PAIR)
            v_rows = slice(2 * width + pair * PAIR, 2 * width + (pair + 1) * PAIR)
            d_approx, d_matrix, d_carried = state[pair]
            qm = r.marks[0, pair]
            km = r.marks[1, pair]
            second = r.marks[2, pair]
            square_sum = head_sum(jnp.sum(second * second, axis=1, keepdims=True))
            turned = d_approx.T
            along = head_sum(jnp.sum(turned * second, axis=1, keepdims=True))
            d_matrix = d_matrix + turned / square_sum
            d_matrix = d_matrix - second * (2.0 * along / (square_sum * square_sum))
            d_scores = second * (d_matrix - jnp.sum(d_matrix * second, axis=1, keepdims=True))
            d_scores = split(d_scores)
            d_out = r.d_attended[rows, :]
            first = r.first[rows, :].astype(f32)
            d_first = dot(r.marks[5, pair].astype(bf16), d_out)
            d_first = (first * (d_first - head_sum(d_first * first))).astype(bf16)
            third = r.third[rows, :]
            d_third = dot(d_carried.astype(bf16), r.qkv[v_rows, :])
            wide = third.astype(f32)
            d_third = wide * (d_third - jnp.sum(d_third * wide, axis=1, keepdims=True))
            d_third = d_third.astype(bf16)
            d_qm = dot3(d_scores, split(km))
            d_qm = d_qm + jnp.where(diagonal, dot(d_third, r.qkv[k_rows, :], NT), 0.0)
            d_km = dot3(d_scores, split(qm), TN)
            d_km = d_km + jnp.where(diagonal, dot(d_first, r.qkv[rows, :], NT), 0.0)
            d_qm = split(d_qm.T / counts)
            d_km = split(d_km.T / counts)
            d_q = dot(km.T.astype(bf16), d_first) + (dot(d_qm[0], seg_turned) + dot(d_qm[1], seg_turned))
            d_k = dot(qm.T.astype(bf16), d_third) + (dot(d_km[0], seg_turned) + dot(d_km[1], seg_turned))
            for at, (value, scale) in enumerate(((d_q, factor), (d_k, factor))):
                place = slice(at * width + pair * PAIR, at * width + (pair + 1) * PAIR)
                value = value * scale
                joined[place, :] = value.astype(bf16)
                r.small[4:5, place] = row_sums(value)
            self.tick()


    def exchange(self, stage, chunk):
        r = self.r
        at = stage % 2
        rows_at = self.length // CHUNKS
        rows = pl.ds(chunk * rows_at, rows_at)
        sems = (r.send_sem.at[stage], r.recv_sem.at[stage])
        return self.remote(r.mine.at[at, rows], r.theirs.at[at, rows], sems, chunk, self.sister)

    def chunk_rows(self, chunk):
        rows_at = self.length // CHUNKS
        start = chunk * rows_at
        if not isinstance(chunk, int):
            start = pl.multiple_of(start, rows_at)
        return pl.ds(start, rows_at)

    def together(self, stage, chunk):
        self.exchange(stage, chunk).wait()
        rows = self.chunk_rows(chunk)
        at = stage % 2
        return self.r.mine[at, rows, :].astype(f32) + self.r.theirs[at, rows, :].astype(f32)

    def offer(self, stage, chunk, value):
        self.r.mine[stage % 2, self.chunk_rows(chunk), :] = value.astype(bf16)
        self.exchange(stage, chunk).start()

    def feed(self, low_ref, active_ref, slope_ref, d_low_ref, scale_ref):
        r = self.r
        block = 256
        units, width = self.units, self.width
        wide = units // 2
        out_bias, first_gain, first_shift, down_bias, second_gain, second_shift = (
            ref[...].reshape(1, self.model)
            for ref in (
                r.out_bias,
                r.first_gain,
                r.first_shift,
                r.down_bias,
                r.second_gain,
                r.second_shift,
            )
        )
        r.small[...] = jnp.zeros_like(r.small)

        def add_row(at, value):
            columns = slice((at % 2) * self.model, (at % 2 + 1) * self.model)
            r.small[at // 2 : at // 2 + 1, columns] += jnp.sum(value, axis=0, keepdims=True)

        self.onward(PIECES + 6)
        self.arrive([3], [3])

        @pl.loop(0, CHUNKS)
        def project(chunk):
            self.offer(0, chunk, dot(r.attended[self.chunk_rows(chunk), :], r.so[...]))

        self.onward(PIECES + 7)
        self.arrive([4], [4, 5])

        def raise_rows(chunk):
            rows = self.chunk_rows(chunk)
            summed = self.together(0, chunk) + out_bias + r.x[rows, :].astype(f32)
            normal, scale = normalize(summed)
            r.normal[rows, :] = normal
            scale_ref[rows, :] = scale
            low = (normal * first_gain + first_shift).astype(bf16)
            low_ref[rows, :] = low
            for at in range(0, units, block):
                columns = slice(at, at + block)
                raised = dot(low, r.su[:, columns]) + r.phalves[:, width + at : width + at + block]
                bell = 0.5 + 0.5 * lax.erf(raised * 0.7071067811865476)
                active_ref[rows, columns] = (raised * bell).astype(bf16)
                density = jnp.exp(-0.5 * raised * raised) * 0.3989422804014327
                slope_ref[rows, columns] = (bell + raised * density).astype(bf16)

        pl.loop(0, CHUNKS)(raise_rows)
        self.arrive([5], [6, 7])

        @pl.loop(0, CHUNKS)
        def lower(chunk):
            self.offer(1, chunk, dot(active_ref[self.chunk_rows(chunk), :], r.sd[...]))

        self.arrive([6], [], True)

        @pl.loop(0, CHUNKS)
        def turn(chunk):
            rows = self.chunk_rows(chunk)
            hidden = r.normal[rows, :] * first_gain + first_shift
            result = self.together(1, chunk) + down_bias + hidden
            normal, scale = normalize(result)
            r.out[rows, :] = (normal * second_gain + second_shift).astype(bf16)
            cotangent = r.cot[rows, :].astype(f32)
            d_result = normalize_back(cotangent * second_gain, normal, scale)
            add_row(4, cotangent * normal)
            add_row(5, cotangent)
            add_row(3, d_result)
            d_low_ref[rows, :] = d_result.astype(bf16)

        for chunk in range(CHUNKS):
            self.deliver(r.out, r.output, 0, chunk)
        turned = d_low_ref[...].T
        for at in range(0, units, wide):
            columns = slice(at, at + wide)
            self.store(r.g_down, columns, dot(turned, active_ref[:, columns]))
            self.launch("g_down", at, at + wide)

        def descend(chunk):
            rows = self.chunk_rows(chunk)
            d_low = d_low_ref[rows, :]
            for at in range(0, units, block):
                columns = slice(at, at + block)
                d_raised = dot(d_low, r.sd[columns, :], NT) * slope_ref[rows, columns].astype(f32)
                r.small[3:4, columns] += jnp.sum(d_raised, axis=0, keepdims=True)
                slope_ref[rows, columns] = d_raised.astype(bf16)
            self.offer(2, chunk, dot(slope_ref[rows, :], r.su[...], NT))

        pl.loop(0, CHUNKS // 2)(descend)
        self.tick()
        pl.loop(CHUNKS // 2, CHUNKS)(descend)
        self.tick()
        turned = low_ref[...].T
        for at in range(0, units, wide):
            columns = slice(at, at + wide)
            self.store(r.g_up, columns, dot(turned, slope_ref[:, columns]))
            self.launch("g_up", at, at + wide)
        self.tick()

        @pl.loop(0, CHUNKS)
        def back(chunk):
            rows = self.chunk_rows(chunk)
            d_hidden = d_low_ref[rows, :].astype(f32) + self.together(2, chunk)
            normal = r.normal[rows, :]
            add_row(1, d_hidden * normal)
            add_row(2, d_hidden)
            d_summed = normalize_back(d_hidden * first_gain, normal, scale_ref[rows, :])
            add_row(0, d_summed)
            r.normal[rows, :] = d_summed
            d_low_ref[rows, :] = d_summed.astype(bf16)

        r.d_attended[...] = dot(r.so[...], d_low_ref[...], NT).astype(bf16)
        turned = d_low_ref[...].T
        self.store(r.g_rest, slice(3 * width, 4 * width), dot(turned, r.attended[...]))
        self.launch("g_rest", 3 * width, 4 * width)
        self.tick()

    def store(self, ref, columns, value):
        value = value.astype(bf16)
        if self.parts:
            value = value.reshape(ref.shape[:-1] + (value.shape[1],))
            ref[:, :, :, :, :, columns] = value
        else:
            ref[:, columns] = value

    def deliver(self, source, target, at, chunk):
        r = self.r
        rows = self.chunk_rows(chunk)
        local, away = self.deliveries(source, target, at, chunk)

        @pl.when(self.own)
        def here():
            local.start()
            if chunk < CHUNKS // 2:
                away.start()

        if chunk >= CHUNKS // 2:

            @pl.when(self.other)
            def there():
                away.start()

    def deliveries(self, source, target, at, chunk):
        r = self.r
        rows = self.chunk_rows(chunk)
        local = pltpu.make_async_copy(source.at[rows], target.at[rows], r.home_sem.at[at, chunk])
        device = self.beyond if chunk < CHUNKS // 2 else self.cross
        sems = (r.away_sem.at[2 * at], r.away_sem.at[2 * at + 1])
        return local, self.remote(source.at[rows], target.at[rows], sems, chunk, device)

    def delivered(self, source, target, at):
        for chunk in range(CHUNKS):
            local, away = self.deliveries(source, target, at, chunk)

            @pl.when(self.own)
            def here():
                local.wait()
                if chunk < CHUNKS // 2:
                    away.wait_send()

            @pl.when(self.other)
            def there():
                away.wait_recv()
                if chunk >= CHUNKS // 2:
                    away.wait_send()


    def part_copy(self, part, level):
        name, start, count, order = self.parts[part]
        ref = getattr(self.r, name)
        bit = order[level]
        index = []
        for b in reversed(range(self.bits + 1)):
            if b in order[:level]:
                index.append(self.place[b])
            else:
                index.append(1 - self.place[b] if b == bit else slice(None))
        source = ref.at[tuple(index) + (slice(None), slice(start, start + count))]
        landing = self.r.landings[part * (self.bits + 1) + level]
        sems = (self.r.part_sem.at[0, part], self.r.part_sem.at[1, part])
        return self.remote(source, landing, sems, level, self.partner(bit))

    def part_finish(self, part, level):
        name, start, count, order = self.parts[part]
        ref = getattr(self.r, name)
        self.part_copy(part, level).wait()
        index = []
        for b in reversed(range(self.bits + 1)):
            index.append(self.place[b] if b in order[: level + 1] else slice(None))
        index = tuple(index) + (slice(None), slice(start, start + count))
        landing = self.r.landings[part * (self.bits + 1) + level]
        total = ref[index].astype(f32) + landing[...].astype(f32)
        if level < self.bits:
            ref[index] = total.astype(bf16)
        else:
            self.part_last(part, total)

    def direct(self, part):
        return self.parts[part][3][-1] == 0

    def direct_rows(self, part, half):
        name, start, count, order = self.parts[part]
        index = tuple(self.place[b] for b in reversed(range(1, self.bits + 1)))
        return getattr(self.r, name), index + (half, slice(None), slice(start, start + count))

    def direct_copies(self, part):
        r = self.r
        level = self.bits
        beyond = (r.part_sem.at[0, part], r.part_sem.at[1, part])
        aside = (r.swap_sem.at[0], r.swap_sem.at[1])
        over = (r.cross_sem.at[0], r.cross_sem.at[1])
        landing = r.landings[part * (self.bits + 1) + level]
        core = self.core
        ref, same = self.direct_rows(part, core)
        ref, other = self.direct_rows(part, 1 - core)
        return (
            self.remote(ref.at[same], landing, beyond, level, self.beyond),
            self.remote(ref.at[other], landing, over, part, self.cross),
            self.remote(ref.at[other], r.swap_in.at[part], aside, part, self.sister),
        )

    def direct_start(self, part):
        beyond, over, aside = self.direct_copies(part)

        @pl.when(self.own)
        def here():
            aside.start()

        @pl.when(self.other)
        def there():
            beyond.start()
            over.start()

    def direct_finish(self, part):
        beyond, over, aside = self.direct_copies(part)
        landing = self.r.landings[part * (self.bits + 1) + self.bits]
        target, columns = self.part_target(part)

        @pl.when(self.own)
        def here():
            beyond.wait_recv()
            ref, index = self.direct_rows(part, self.core)
            target[:, columns] = ref[index].astype(f32) + landing[...].astype(f32)
            aside.wait_send()

        @pl.when(self.other)
        def there():
            over.wait_recv()
            aside.wait_recv()
            target[:, columns] = self.r.swap_in[part].astype(f32) + landing[...].astype(f32)
            beyond.wait_send()
            over.wait_send()

    def part_swap(self, part):
        name, start, count, order = self.parts[part]
        ref = self.r.swap_out.at[part]
        sems = (self.r.swap_sem.at[0], self.r.swap_sem.at[1])
        return self.remote(ref, self.r.swap_in.at[part], sems, part, self.cross)

    def part_target(self, part):
        name, start, count, order = self.parts[part]
        return getattr(self.r, "t" + name[1:]), slice(start, start + count)

    def part_last(self, part, total):
        target, columns = self.part_target(part)

        @pl.when(self.own)
        def here():
            target[:, columns] = total

        @pl.when(self.other)
        def there():
            self.r.swap_out[part] = total.astype(bf16)
            self.part_swap(part).start()

    def launch(self, wanted, first, last):
        for part, (name, start, count, order) in enumerate(self.parts):
            if name == wanted and first <= start < last:
                self.part_copy(part, 0).start()
                self.levels[part] = 0

    def advance(self, part):
        level = self.levels[part]
        if level is None or level > self.bits:
            return
        if level == self.bits and self.direct(part):
            self.direct_finish(part)
        else:
            self.part_finish(part, level)
        if level + 1 == self.bits and self.direct(part):
            self.direct_start(part)
        elif level < self.bits:
            self.part_copy(part, level + 1).start()
        self.levels[part] = level + 1

    def tick(self):
        if self.parts and self.agenda:
            for part in self.agenda.pop(0):
                self.advance(part)

    def small_copy(self, level):
        r = self.r
        source = r.small if level == 0 else r.small_sum.at[level - 1]
        sems = (r.small_sem.at[0], r.small_sem.at[1])
        return self.remote(source, r.small_land.at[level], sems, level, self.partner(level))

    def small_advance(self):
        r = self.r
        level = self.small_level
        self.small_level += 1
        self.small_copy(level).wait()
        own = r.small[...] if level == 0 else r.small_sum[level - 1]
        r.small_sum[level] = own + r.small_land[level]
        if level < self.bits:
            self.small_copy(level + 1).start()
        else:

            @pl.when(self.own)
            def pass_on():
                self.small_swap().start()

    def small_swap(self):
        r = self.r
        sems = (r.small_sem.at[0], r.small_sem.at[1])
        return self.remote(r.small_sum.at[self.bits], r.small_sister, sems, self.bits + 1, self.sister)

    def small_done(self):
        r = self.r
        total = r.small_sum[self.bits]
        r.tsmall[0:3, :] = total[0:3]

        @pl.when(self.own)
        def here():
            r.tsmall[3:8, :] = total[3:8]
            self.small_swap().wait_send()

        @pl.when(self.other)
        def there():
            self.small_swap().wait_recv()
            r.tsmall[3:8, :] = r.small_sister[3:8, :]

    def finish(self, joined):
        r = self.r
        width, model, length = self.width, self.model, self.length
        bits = self.bits
        if self.parts:
            self.small_copy(0).start()
        turned = r.x[...].T
        for at in range(2):
            rows = slice(at * width, (at + 1) * width)
            self.store(r.g_rest, rows, dot(turned, joined[rows, :], NT))
            self.launch("g_rest", at * width, (at + 1) * width)
        rows_at = length // CHUNKS
        for chunk in range(CHUNKS):
            columns = slice(chunk * rows_at, (chunk + 1) * rows_at)
            back = dot(r.sqk[0], joined[0:width, columns])
            back = back + dot(r.sqk[1], joined[width : 2 * width, columns])
            back = back + dot(r.sv[...], joined[2 * width :, columns])
            self.offer(3, chunk, back.astype(bf16).T)
        for chunk in range(CHUNKS):
            rows = self.chunk_rows(chunk)
            r.grad[rows, :] = (r.normal[rows, :] + self.together(3, chunk)).astype(bf16)
            self.deliver(r.grad, r.tokens_grad, 1, chunk)
        if self.parts:
            for at, part in enumerate(FINAL):
                self.advance(part)
                if at % 6 == 5 and self.small_level <= bits:
                    self.small_advance()
            while self.small_level <= bits:
                self.small_advance()
            for level in range(bits + 1):
                for part in range(len(self.parts)):
                    if self.levels[part] <= level:
                        self.advance(part)
            self.small_done()
        else:
            r.tsmall[...] = r.small[...]
        self.delivered(r.out, r.output, 0)
        self.delivered(r.grad, r.tokens_grad, 1)
        for part in range(len(self.parts)):
            target, columns = self.part_target(part)
            if self.direct(part):
                continue

            @pl.when(self.other)
            def there():
                self.part_swap(part).wait()
                target[:, columns] = r.swap_in[part].astype(f32)

        self.drain()


def layer_kernel(names, bits, parts, agenda, sizes, *refs):
    found = dict(zip(names, refs))
    found["landings"] = refs[len(names) :]
    layer = Layer(found, bits, parts, sizes)
    layer.agenda = list(agenda)
    length, model, width, units, heads = sizes
    layer.greet()

    def ahead(q_ref, k_ref, v_ref, band_ref):
        layer.begin(band_ref)
        layer.attend(q_ref, k_ref, v_ref, band_ref)

    bands = pltpu.VMEM((2, heads, 2 * EDGE + BAND, 128), bf16)
    pl.run_scoped(ahead, *[pltpu.VMEM((width, length), f32)] * 3, bands)
    pl.run_scoped(
        layer.feed,
        pltpu.VMEM((length, model), bf16),
        pltpu.VMEM((length, units), bf16),
        pltpu.VMEM((length, units), bf16),
        pltpu.VMEM((length, model), bf16),
        pltpu.VMEM((length, 1), f32),
    )

    def back(joined):
        layer.attend_back(joined)
        layer.finish(joined)

    pl.run_scoped(back, pltpu.VMEM((3 * width, length), bf16))


ORDERS = {
    3: (
        (1, 0, 2, 3),
        (1, 2, 3, 0),
        (2, 0, 3, 1),
        (1, 2, 3, 0),
        (2, 0, 1, 3),
        (0, 2, 1, 3),
        (2, 3, 1, 0),
        (2, 1, 3, 0),
        (0, 1, 2, 3),
        (1, 2, 3, 0),
        (1, 2, 0, 3),
        (1, 0, 2, 3),
    ),
}
AGENDA = (
    [],
    [],
    [],
    [2],
    [],
    [],
    [],
    [],
    [],
    [0, 1, 3],
    [5, 2, 4],
    [6, 7],
    [0, 11],
    [10, 4],
)
FINAL = (7, 2, 1, 11, 3, 4, 0, 5, 6, 2, 8, 9, 10, 5, 11, 6, 4, 0, 8, 10, 6, 7, 9, 1, 3, 5, 11, 8, 10, 7, 1, 9, 3, 8, 9)


def body(
    tokens,
    cotangent,
    lengths,
    masked,
    qk_weight,
    qk_bias,
    value_weight,
    value_bias,
    conv_taps,
    out_weight,
    out_bias,
    first_gain,
    first_shift,
    up_weight,
    up_bias,
    down_weight,
    down_bias,
    second_gain,
    second_shift,
):
    chips = lax.axis_size("chip")
    length, model = tokens.shape
    width = value_weight.shape[1]
    units = up_weight.shape[1]
    heads = conv_taps.shape[0]
    pairs = width // PAIR
    bits = chips.bit_length() - 1
    share = model // (2 * chips)
    fused = bits in ORDERS and share % 16 == 0
    parts = []
    if fused:
        count = units // 4
        for at, order in enumerate(ORDERS[bits]):
            parts.append((("g_down", "g_up", "g_rest")[at // 4], at % 4 * count, count, order))
    shape = jax.ShapeDtypeStruct
    hbm = pl.BlockSpec(memory_space=pl.ANY)
    inputs = [
        ("tokens", tokens, hbm),
        ("cotangent", cotangent, hbm),
        ("wqk", jnp.transpose(qk_weight, (1, 0, 2)), hbm),
        ("wv", value_weight, hbm),
        ("wo", out_weight, hbm),
        ("wu", up_weight, hbm),
        ("wd", down_weight, hbm),
        ("lengths", lengths, SMEM),
        ("masked", masked, VMEM),
        ("qk_bias", qk_bias, VMEM),
        ("taps", conv_taps, VMEM),
        ("v_bias", value_bias, VMEM),
        ("u_bias", up_bias, VMEM),
        ("out_bias", out_bias, VMEM),
        ("first_gain", first_gain, VMEM),
        ("first_shift", first_shift, VMEM),
        ("down_bias", down_bias, VMEM),
        ("second_gain", second_gain, VMEM),
        ("second_shift", second_shift, VMEM),
    ]
    outputs = [("output", shape((length, model), bf16), hbm), ("tokens_grad", shape((length, model), bf16), hbm)]
    outputs.append(("tsmall", shape((8, units), f32), VMEM))
    scratch = []
    for name in ("down", "up", "rest"):
        if fused:
            outputs.append(("t_" + name, shape((share, units), f32), VMEM))
            scratch.append(("g_" + name, pltpu.VMEM((2,) * (bits + 1) + (share, units), bf16)))
        else:
            outputs.append(("g_" + name, shape((model, units), bf16), VMEM))
    dma = pltpu.SemaphoreType.DMA
    scratch += [
        ("sqk", pltpu.VMEM((2, model, width), bf16)),
        ("sv", pltpu.VMEM((model, width), bf16)),
        ("so", pltpu.VMEM((width, model), bf16)),
        ("su", pltpu.VMEM((model, units), bf16)),
        ("sd", pltpu.VMEM((units, model), bf16)),
        ("x", pltpu.VMEM((length, model), bf16)),
        ("cot", pltpu.VMEM((length, model), bf16)),
        ("live", pltpu.VMEM((8, length), f32)),
        ("pqk", pltpu.VMEM((2, width), f32)),
        ("halves", pltpu.VMEM((1, width + units), f32)),
        ("phalves", pltpu.VMEM((1, width + units), f32)),
        ("ptaps", pltpu.VMEM((heads, KERNEL), f32)),
        ("qkv", pltpu.VMEM((3 * width, length), bf16)),
        ("first", pltpu.VMEM((width, length), bf16)),
        ("third", pltpu.VMEM((width, length), bf16)),
        ("attended", pltpu.VMEM((length, width), bf16)),
        ("marks", pltpu.VMEM((6, pairs, PAIR, PAIR), f32)),
        ("chain", pltpu.VMEM((NS_ITERS, 4, pairs, PAIR, PAIR), f32)),
        ("mine", pltpu.VMEM((2, length, model), bf16)),
        ("theirs", pltpu.VMEM((2, length, model), bf16)),
        ("normal", pltpu.VMEM((length, model), f32)),
        ("d_attended", pltpu.VMEM((width, length), bf16)),
        ("out", pltpu.VMEM((length, model), bf16)),
        ("grad", pltpu.VMEM((length, model), bf16)),
        ("small", pltpu.VMEM((8, units), f32)),
        ("weight_sem", dma((8, PIECES))),
        ("local_sem", dma((7,))),
        ("item_sem", dma((2, 3))),
        ("bias_sem", dma((2, 3))),
        ("send_sem", dma((4, CHUNKS))),
        ("recv_sem", dma((4, CHUNKS))),
        ("home_sem", dma((2, CHUNKS))),
        ("away_sem", dma((4, CHUNKS))),
    ]
    landings = []
    if fused:
        levels = bits + 1
        scratch += [
            ("small_land", pltpu.VMEM((levels, 8, units), f32)),
            ("small_sum", pltpu.VMEM((levels, 8, units), f32)),
            ("small_sister", pltpu.VMEM((8, units), f32)),
            ("small_sem", dma((2, levels + 1))),
            ("part_sem", dma((2, len(parts), levels))),
            ("swap_sem", dma((2, len(parts)))),
            ("cross_sem", dma((2, len(parts)))),
            ("swap_out", pltpu.VMEM((len(parts), share, parts[0][2]), bf16)),
            ("swap_in", pltpu.VMEM((len(parts), share, parts[0][2]), bf16)),
        ]
        for name, start, count, order in parts:
            landings += [pltpu.VMEM((2,) * (bits - level) + (share, count), bf16) for level in range(levels)]
    names = [n for n, *_ in inputs + outputs + scratch]
    got = pl.pallas_call(
        functools.partial(
            layer_kernel, names, bits, parts, AGENDA, (length, model, width, units, heads)
        ),
        out_shape=[kind for _, kind, _ in outputs],
        in_specs=[spec for *_, spec in inputs],
        out_specs=[spec for *_, spec in outputs],
        scratch_shapes=[kind for _, kind in scratch] + landings,
        compiler_params=pltpu.CompilerParams(
            collective_id=0, has_side_effects=True, vmem_limit_bytes=VMEM_LIMIT
        ),
        name="layer",
    )(*[value for _, value, _ in inputs])
    output, tokens_grad, small, down, up, rest = got
    if not fused:
        swap = lambda v: lax.ppermute(v, ("core", "mp"), [(0, 0), (1, 2), (2, 1), (3, 3)])
        gather = lambda g: swap(
            lax.psum_scatter(g, ("chip", "mp"), scatter_dimension=0, tiled=True).astype(f32)
        )
        down, up, rest = gather(down), gather(up), gather(rest)
        small = lax.psum(small, ("chip", "mp"))
        small = jnp.concatenate([small[:3], swap(small[3:])], axis=0)
    return arrange(output, tokens_grad, small, up, down, rest, heads)


def arrange_kernel(
    output,
    tokens_grad,
    small,
    up,
    down,
    rest,
    output_to,
    tokens_grad_to,
    qk_to,
    qk_bias_to,
    v_to,
    v_bias_to,
    taps_to,
    out_to,
    out_bias_to,
    first_gain_to,
    first_shift_to,
    up_to,
    up_bias_to,
    down_to,
    down_bias_to,
    second_gain_to,
    second_shift_to,
    output_at,
    tokens_grad_at,
    up_at,
    down_at,
    rest_at,
    small_at,
    sems,
):
    rows = output.shape[0] // CHUNKS
    ahead = [(small, small_at), (rest, rest_at), (up, up_at), (down, down_at)]
    after = [(up_at, up_to), (down_at, down_to)]
    for chunk in range(CHUNKS):
        place = pl.ds(chunk * rows, rows)
        ahead += [(output.at[place], output_at.at[place]), (tokens_grad.at[place], tokens_grad_at.at[place])]
        after += [(output_at.at[place], output_to.at[place]), (tokens_grad_at.at[place], tokens_grad_to.at[place])]
    coming = [pltpu.make_async_copy(a, b, sems.at[0, i]) for i, (a, b) in enumerate(ahead)]
    going = [pltpu.make_async_copy(a, b, sems.at[1, i]) for i, (a, b) in enumerate(after)]
    for copy in coming:
        copy.start()
    for copy in coming[:2]:
        copy.wait()
    for here, there in zip(coming[2:], going):
        here.wait()
        there.start()
    small, rest = small_at, rest_at
    width = v_to.shape[1]
    model = out_bias_to.shape[0]
    units = up_bias_to.shape[0]
    for at in range(2):
        columns = slice(at * width, (at + 1) * width)
        qk_to[:, at, :] = rest[:, columns]
        qk_bias_to[at : at + 1, :] = small[4:5, columns]
    v_to[...] = rest[:, 2 * width : 3 * width]
    out_to[...] = rest[:, 3 * width :]
    v_bias_to[...] = small[4:5, 2 * width : 3 * width].reshape(width)
    up_bias_to[...] = small[3:4, :].reshape(units)
    for head in range(taps_to.shape[0]):
        taps_to[head : head + 1, :] = small[5:6, head * 128 : head * 128 + KERNEL]
    common = (out_bias_to, first_gain_to, first_shift_to, down_bias_to, second_gain_to, second_shift_to)
    for at, ref in enumerate(common):
        columns = slice(at % 2 * model, (at % 2 + 1) * model)
        ref[...] = small[at // 2 : at // 2 + 1, columns].reshape(model)
    for copy in going:
        copy.wait()


def arrange(output, tokens_grad, small, up, down, rest, heads):
    share, units = up.shape
    width = rest.shape[1] // 4
    model = output.shape[1]
    hbm = pl.BlockSpec(memory_space=pl.ANY)
    kinds = [
        (output.shape, bf16),
        (output.shape, bf16),
        ((share, 2, width), f32),
        ((2, width), f32),
        ((share, width), f32),
        ((width,), f32),
        ((heads, KERNEL), f32),
        ((share, width), f32),
        ((model,), f32),
        ((model,), f32),
        ((model,), f32),
        ((share, units), f32),
        ((units,), f32),
        ((share, units), f32),
        ((model,), f32),
        ((model,), f32),
        ((model,), f32),
    ]
    got = pl.pallas_call(
        arrange_kernel,
        out_shape=[jax.ShapeDtypeStruct(a, b) for a, b in kinds],
        in_specs=[hbm] * 6,
        out_specs=[hbm if at in (0, 1, 11, 13) else VMEM for at in range(len(kinds))],
        scratch_shapes=[
            pltpu.VMEM(output.shape, bf16),
            pltpu.VMEM(output.shape, bf16),
            pltpu.VMEM(up.shape, f32),
            pltpu.VMEM(up.shape, f32),
            pltpu.VMEM(up.shape, f32),
            pltpu.VMEM(small.shape, f32),
            pltpu.SemaphoreType.DMA((2, 4 + 2 * CHUNKS)),
        ],
        compiler_params=pltpu.CompilerParams(vmem_limit_bytes=VMEM_LIMIT),
        name="arrange",
    )(output, tokens_grad, small, up, down, rest)
    got = list(got)
    got[7] = got[7].T
    got[13] = got[13].T
    return tuple(got)


def solution(mesh):
    dp = ("chip", "core")
    placed = (
        P(dp, None),
        P(dp, None),
        P(dp),
        P(dp, None),
        P(None, None, "mp"),
        P(None, "mp"),
        P(None, "mp"),
        P("mp"),
        P("mp", None),
        P("mp", None),
        P(),
        P(),
        P(),
        P(None, "mp"),
        P("mp"),
        P("mp", None),
        P(),
        P(),
        P(),
    )
    chips = mesh.shape["dp"] // 2
    fine = Mesh(mesh.devices.reshape(chips, 2, mesh.shape["mp"]), ("chip", "core", "mp"))
    return jax.shard_map(
        body,
        mesh=fine,
        in_specs=placed,
        out_specs=(
            P(dp, None),
            P(dp, None),
            P(dp, None, "mp"),
            P(None, "mp"),
            P(dp, "mp"),
            P("mp"),
            P("mp", None),
            P("mp", dp),
            P(),
            P(),
            P(),
            P(dp, "mp"),
            P("mp"),
            P("mp", dp),
            P(),
            P(),
            P(),
        ),
        check_vma=False,
    )
```
